32 devices in a mesh: dp: 8 (over y, x, core), tensor: 4 (over z).
Axes of the slice: x: 2, y: 2, z: 4, core: 2. Of those that a mesh axis runs over, the one named last changes fastest.
Arguments:
- encoder_layer_input: bfloat16 [8, 1024, 512], P('dp'), may hold values from -6 to 6
- decoder_layer_input: bfloat16 [8, 1024, 512], P('dp'), may hold values from -6 to 6
- source_pair_index: int32 [8, 1024], P('dp'), may hold values from 0 to 15, never falling along the last dimension, each value on 1 to 128 neighbouring positions
- target_pair_index: int32 [8, 1024], P('dp'), may hold values from 0 to 15, never falling along the last dimension, each value on 1 to 128 neighbouring positions
- masked: int32 [8, 1024], P('dp'), may hold values 0 or 1
- mask_embed: float32 [512], replicated, may hold values from -6 to 6
- enc_qkv: bfloat16 [3, 512, 512], P(None, None, 'tensor'), may hold values from -0.25 to 0.25
- enc_attn_out: bfloat16 [512, 512], P('tensor'), may hold values from -0.75 to 0.75
- enc_ffn_in: bfloat16 [512, 2048], P(None, 'tensor'), may hold values from -0.25 to 0.25
- enc_ffn_out: bfloat16 [2048, 512], P('tensor'), may hold values from -0.1875 to 0.1875
- dec_self_qkv: bfloat16 [3, 512, 512], P(None, None, 'tensor'), may hold values from -0.25 to 0.25
- dec_self_out: bfloat16 [512, 512], P('tensor'), may hold values from -0.75 to 0.75
- dec_cross_qkv: bfloat16 [3, 512, 512], P(None, None, 'tensor'), may hold values from -0.25 to 0.25
- dec_cross_out: bfloat16 [512, 512], P('tensor'), may hold values from -0.75 to 0.75
- dec_ffn_in: bfloat16 [512, 2048], P(None, 'tensor'), may hold values from -0.25 to 0.25
- dec_ffn_out: bfloat16 [2048, 512], P('tensor'), may hold values from -0.1875 to 0.1875
- norm_gain: float32 [5, 512], replicated, may hold values from 0.1 to 1.9
- norm_shift: float32 [5, 512], replicated, may hold values from -1.5 to 1.5
- encoder_output_cotangent: bfloat16 [8, 1024, 512], P('dp'), may hold values from -6 to 6
- decoder_output_cotangent: bfloat16 [8, 1024, 512], P('dp'), may hold values from -6 to 6
Outputs:
- enc_out: bfloat16 [8, 1024, 512], P('dp')
- dec_out: bfloat16 [8, 1024, 512], P('dp')
- enc_in_grad: float32 [8, 1024, 512], P('dp')
- dec_in_grad: float32 [8, 1024, 512], P('dp')
- mask_embed_grad: float32 [512], replicated
- enc_qkv_grad: float32 [3, 512, 512], P(None, None, 'tensor')
- enc_attn_out_grad: float32 [512, 512], P('tensor')
- enc_ffn_in_grad: float32 [512, 2048], P(None, 'tensor')
- enc_ffn_out_grad: float32 [2048, 512], P('tensor')
- dec_self_qkv_grad: float32 [3, 512, 512], P(None, None, 'tensor')
- dec_self_out_grad: float32 [512, 512], P('tensor')
- dec_cross_qkv_grad: float32 [3, 512, 512], P(None, None, 'tensor')
- dec_cross_out_grad: float32 [512, 512], P('tensor')
- dec_ffn_in_grad: float32 [512, 2048], P(None, 'tensor')
- dec_ffn_out_grad: float32 [2048, 512], P('tensor')
- norm_gain_grad: float32 [5, 512], replicated
- norm_shift_grad: float32 [5, 512], replicated
The draws below stay inside these ranges and needn't reach their ends.
Inputs may be any that keep to these rules, and one draw needn't show every extreme that they name: `source_pair_index`: within each packed row pair ids never fall and each of the 16 ids labels 1 to 128 consecutive tokens, so every pair has source and target tokens in its rows. `target_pair_index`: within each packed row pair ids never fall and each of the 16 ids labels 1 to 128 consecutive tokens.
All inputs are finite; a program needn't handle non-finite values. No bound on the sum of `masked` on one device may be relied on, other than what follows from the above.
Results may differ from the reference program's by a relative error of at most 0.025.
The reference program's roundings to bfloat16 on the way count: a program that leaves them out, or rounds other values in their place, can miss the bound.
Values sent between devices are 32-bit elements; how exact they have to be, the bound alone decides.
A program may use at most 192 MiB of HBM per device.

```python
import math
import jax
import jax.numpy as jnp
import numpy as np
from jax import lax

MODEL_WIDTH = 512
HEADS = 8
FF = 2048
HEAD_DIM = 64
ROW_LENGTH = 1024
SEGMENT_TOKENS = 128
PAIRS_PER_ROW = 16
NORMS = 5
PACKED_ROWS = 8


def with_ends(array, rng, low, top_value):
    shape = array.shape
    index_at = [jax.random.randint(jax.random.fold_in(rng, axis), (), 0, shape[axis]) for axis in range(len(shape))]
    array = array.at[tuple(index_at)].set(low)
    longest = shape.index(max(shape))
    index_at[longest] = (index_at[longest] + 1) % shape[longest]
    return array.at[tuple(index_at)].set(top_value)


def shard_levels(key, extent, pieces, low, top_value):
    def one(position, blocks):
        heights = jax.random.uniform(jax.random.fold_in(jax.random.fold_in(key, 6), position), (blocks,), jnp.float32, low / len(pieces), top_value / len(pieces))
        return jnp.repeat(jnp.exp(heights), extent[position] // blocks).reshape((-1,) + (1,) * (len(extent) - position - 1))

    loudness = one(*pieces[0])
    for cut in pieces[1:]:
        loudness = loudness * one(*cut)
    return loudness


def split_up(number_of, total, most, skew):
    loads = [(1 << 20) // math.isqrt(standing ** skew) + 1 for standing in range(2, number_of + 1)]
    rest, holding = total - most - (number_of - 1), [1] * (number_of - 1)
    while rest > 0:
        movable = [i for i in range(number_of - 1) if holding[i] < most]
        pool, remaining = sum([loads[i] for i in movable]), rest
        for i in movable:
            addition = min(most - holding[i], max(1, remaining * loads[i] // pool), rest)
            holding[i] = holding[i] + addition
            rest = rest - addition
    return np.array([most] + holding)


def ragged_sizes(own_key, number_of, total, limit, skew):
    if number_of == 2:
        one = jax.random.randint(own_key, (), max(1, total - limit), min(limit, total - 1) + 1)
        return jnp.stack([one, total - one])
    tallies = jnp.asarray(split_up(number_of, total, limit, skew), jnp.int32)
    twos = (number_of - 1) // 2
    giver, receiver = tallies[1:1 + 2 * twos:2], tallies[2:2 + 2 * twos:2]
    margin = jnp.minimum(giver - 1, limit - receiver)
    shifted = jax.random.randint(jax.random.fold_in(own_key, 1), (twos,), 0, 1 << 20) % (margin + 1)
    tallies = tallies.at[1:1 + 2 * twos:2].set(giver - shifted).at[2:2 + 2 * twos:2].set(receiver + shifted)
    return tallies[jax.random.permutation(jax.random.fold_in(own_key, 2), number_of)]


def noise(own_key, dims, deviation, bound, pieces=(), dtype=jnp.bfloat16):
    level = shard_levels(own_key, dims, pieces, -0.22, 0.18) if pieces else 1.0
    entries = jax.random.normal(own_key, dims, jnp.float32) * deviation * level
    return jnp.minimum(jnp.maximum(entries, -bound), bound).astype(dtype)


def setup_inputs(seed: int = 0) -> dict:
    streams_of = jax.random.split(jax.random.key(seed), 21)
    return {
        "encoder_layer_input": noise(streams_of[0], (PACKED_ROWS, ROW_LENGTH, MODEL_WIDTH), 1.0, 6.0, ((0, 8),)),
        "decoder_layer_input": noise(streams_of[1], (PACKED_ROWS, ROW_LENGTH, MODEL_WIDTH), 1.0, 6.0, ((0, 8),)),
        "source_pair_index": jax.vmap(lambda own: jnp.searchsorted(jnp.cumsum(ragged_sizes(own, PAIRS_PER_ROW, ROW_LENGTH, SEGMENT_TOKENS, 1)), jnp.arange(ROW_LENGTH), side="right"))(jax.random.split(streams_of[2], PACKED_ROWS)).reshape((PACKED_ROWS, ROW_LENGTH)).astype(jnp.int32),
        "target_pair_index": jax.vmap(lambda own: jnp.searchsorted(jnp.cumsum(ragged_sizes(own, PAIRS_PER_ROW, ROW_LENGTH, SEGMENT_TOKENS, 1)), jnp.arange(ROW_LENGTH), side="right"))(jax.random.split(streams_of[3], PACKED_ROWS)).reshape((PACKED_ROWS, ROW_LENGTH)).astype(jnp.int32),
        "masked": with_ends((jax.random.randint(streams_of[4], (PACKED_ROWS, ROW_LENGTH), 0, 2) < 1).astype(jnp.int32), jax.random.fold_in(streams_of[4], 1), 0, 1),
        "mask_embed": noise(streams_of[5], (MODEL_WIDTH,), 1.0, 6.0, (), jnp.float32),
        "enc_qkv": noise(streams_of[6], (3, MODEL_WIDTH, MODEL_WIDTH), MODEL_WIDTH ** -0.5, 0.25, ((2, 4),)),
        "enc_attn_out": noise(streams_of[7], (MODEL_WIDTH, MODEL_WIDTH), (MODEL_WIDTH // 8) ** -0.5, 0.75, ((0, 4),)),
        "enc_ffn_in": noise(streams_of[8], (MODEL_WIDTH, FF), MODEL_WIDTH ** -0.5, 0.25, ((1, 4),)),
        "enc_ffn_out": noise(streams_of[9], (FF, MODEL_WIDTH), (FF // 2) ** -0.5, 0.1875, ((0, 4),)),
        "dec_self_qkv": noise(streams_of[10], (3, MODEL_WIDTH, MODEL_WIDTH), MODEL_WIDTH ** -0.5, 0.25, ((2, 4),)),
        "dec_self_out": noise(streams_of[11], (MODEL_WIDTH, MODEL_WIDTH), (MODEL_WIDTH // 8) ** -0.5, 0.75, ((0, 4),)),
        "dec_cross_qkv": noise(streams_of[12], (3, MODEL_WIDTH, MODEL_WIDTH), MODEL_WIDTH ** -0.5, 0.25, ((2, 4),)),
        "dec_cross_out": noise(streams_of[13], (MODEL_WIDTH, MODEL_WIDTH), (MODEL_WIDTH // 8) ** -0.5, 0.75, ((0, 4),)),
        "dec_ffn_in": noise(streams_of[14], (MODEL_WIDTH, FF), MODEL_WIDTH ** -0.5, 0.25, ((1, 4),)),
        "dec_ffn_out": noise(streams_of[15], (FF, MODEL_WIDTH), (FF // 2) ** -0.5, 0.1875, ((0, 4),)),
        "norm_gain": jnp.clip(1.0 + 0.18 * jax.random.normal(streams_of[16], (NORMS, MODEL_WIDTH), jnp.float32), 0.1, 1.9),
        "norm_shift": noise(streams_of[17], (NORMS, MODEL_WIDTH), 0.3, 1.5, (), jnp.float32),
        "encoder_output_cotangent": noise(streams_of[18], (PACKED_ROWS, ROW_LENGTH, MODEL_WIDTH), 1.0, 6.0, ((0, 8),)),
        "decoder_output_cotangent": noise(streams_of[19], (PACKED_ROWS, ROW_LENGTH, MODEL_WIDTH), 1.0, 6.0, ((0, 8),)),
    }


@jax.custom_vjp
def low(v):
    return lax.optimization_barrier(v.astype(jnp.bfloat16)).astype(jnp.float32)

@jax.custom_vjp
def low_back(v):
    return v

def low_keep(v):
    return (low(v), None)

def low_pass(kept, grad):
    return (grad,)

def back_keep(v):
    return (v, None)

def back_low(kept, grad):
    return (low(grad),)
low.defvjp(low_keep, low_pass)
low_back.defvjp(back_keep, back_low)
highest = lax.Precision.HIGHEST
epsilon = 1e-05
floor_score = -1000000000.0

def layer_norm(totals, norm_gain, norm_shift):
    centered = totals - lax.optimization_barrier(jnp.mean(totals, axis=-1, keepdims=True))
    variance = lax.optimization_barrier(jnp.mean(centered * centered, axis=-1, keepdims=True))
    return centered * lax.rsqrt(variance + epsilon) * norm_gain + norm_shift

def project_in(inputs, weight):
    return jnp.dot(inputs, weight, precision=highest)

def project_out(inputs, weight):
    return low_back(jnp.dot(inputs, weight, precision=highest))

def split_heads(matrix):
    return matrix.reshape(matrix.shape[0], HEADS, HEAD_DIM)

def attend(query_low, key_low, query_seg, key_seg, qkv_weight, out_weight):
    queries = low(low_back(project_in(query_low, qkv_weight[0])))
    keys = low(low_back(project_in(key_low, qkv_weight[1])))
    values = low(low_back(project_in(key_low, qkv_weight[2])))
    raw_scores = low_back(jnp.einsum('qhc,khc->hqk', split_heads(queries), split_heads(keys), precision=highest))
    same_pair = query_seg[:, None] == key_seg[None, :]
    scores = jnp.where(same_pair[None], raw_scores * HEAD_DIM ** (-0.5), floor_score)
    shares = low(jax.nn.softmax(scores, axis=-1))
    mixed = jnp.einsum('hqk,khc->qhc', shares, split_heads(values), precision=highest)
    mixed = low(low_back(mixed.reshape(queries.shape[0], queries.shape[1])))
    return project_out(mixed, out_weight)

def feed_forward(inputs, weight_in, weight_out):
    before = low_back(project_in(low(inputs), weight_in))
    hidden = low(jax.nn.gelu(before, approximate=False))
    return project_out(hidden, weight_out)

def row_forward(params, row):
    mask_embed, enc_qkv, enc_attn_out, enc_ffn_in, enc_ffn_out, dec_self_qkv, dec_self_out, dec_cross_qkv, dec_cross_out, dec_ffn_in, dec_ffn_out, norm_gain, norm_shift = params
    source, target_in, enc_row_seg, dec_row_seg, mask_row = row
    source_low = low(source)
    first = layer_norm(source + attend(source_low, source_low, enc_row_seg, enc_row_seg, enc_qkv, enc_attn_out), norm_gain[0], norm_shift[0])
    encoded = layer_norm(first + feed_forward(first, enc_ffn_in, enc_ffn_out), norm_gain[1], norm_shift[1])
    target = jnp.where(mask_row[:, None] == 1, mask_embed[None, :], target_in)
    target_low = low(target)
    second = layer_norm(target + attend(target_low, target_low, dec_row_seg, dec_row_seg, dec_self_qkv, dec_self_out), norm_gain[2], norm_shift[2])
    third = layer_norm(second + attend(low(second), low(encoded), dec_row_seg, enc_row_seg, dec_cross_qkv, dec_cross_out), norm_gain[3], norm_shift[3])
    decoded = layer_norm(third + feed_forward(third, dec_ffn_in, dec_ffn_out), norm_gain[4], norm_shift[4])
    return (encoded, decoded)

def reference(encoder_layer_input, decoder_layer_input, source_pair_index, target_pair_index, masked, mask_embed, enc_qkv, enc_attn_out, enc_ffn_in, enc_ffn_out, dec_self_qkv, dec_self_out, dec_cross_qkv, dec_cross_out, dec_ffn_in, dec_ffn_out, norm_gain, norm_shift, encoder_output_cotangent, decoder_output_cotangent):
    params = tuple((argument.astype(jnp.float32) for argument in (mask_embed, enc_qkv, enc_attn_out, enc_ffn_in, enc_ffn_out, dec_self_qkv, dec_self_out, dec_cross_qkv, dec_cross_out, dec_ffn_in, dec_ffn_out, norm_gain, norm_shift)))
    inputs = (encoder_layer_input.astype(jnp.float32), decoder_layer_input.astype(jnp.float32))

    def forward(params, inputs):

        def scan_step(carry, row):
            return (carry, jax.checkpoint(row_forward)(params, row))
        carried, outputs = lax.scan(scan_step, jnp.zeros((), jnp.float32), (inputs[0], inputs[1], source_pair_index, target_pair_index, masked))
        return outputs
    outputs, pullback = jax.vjp(forward, params, inputs)
    param_grads, input_grads = pullback((encoder_output_cotangent.astype(jnp.float32), decoder_output_cotangent.astype(jnp.float32)))
    return (outputs[0].astype(jnp.bfloat16), outputs[1].astype(jnp.bfloat16), input_grads[0], input_grads[1], param_grads[0], param_grads[1], param_grads[2], param_grads[3], param_grads[4], param_grads[5], param_grads[6], param_grads[7], param_grads[8], param_grads[9], param_grads[10], param_grads[11], param_grads[12])
```

```python
import functools

import jax
import jax.numpy as jnp
from jax import lax
from jax.experimental import pallas as pl
from jax.experimental.pallas import tpu as pltpu
from jax.sharding import PartitionSpec as P

f32, bf16 = jnp.float32, jnp.bfloat16
HEAD_DIM = 64
EPS = 1e-05
FLOOR = -1000000000.0
BLK = 256
MB = 1 << 20
MESH = pl.DeviceIdType.MESH
VM = pltpu.VMEM


def nt(a, b):
    return lax.dot_general(a, b, (((1,), (1,)), ((), ())), preferred_element_type=f32)


def nn(a, b):
    return lax.dot_general(a, b, (((1,), (0,)), ((), ())), preferred_element_type=f32)


def tn(a, b):
    return lax.dot_general(a, b, (((0,), (0,)), ((), ())), preferred_element_type=f32)


def layer_norm(v):
    c = v - jnp.mean(v, axis=-1, keepdims=True)
    r = lax.rsqrt(jnp.mean(c * c, axis=-1, keepdims=True) + EPS)
    return c * r, r


def layer_norm_back(dy, n, r, gain):
    dn = dy * gain
    m1 = jnp.mean(dn, axis=-1, keepdims=True)
    m2 = jnp.mean(dn * n, axis=-1, keepdims=True)
    return r * (dn - m1 - n * m2)


def build(dst, own, land, kinds, rows):
    for k in range(kinds):
        size = own.shape[1]
        dst[k, :size] = own[k]
        rest = land[:, k * rows : (k + 1) * rows, :].reshape(24 * rows, land.shape[2])
        dst[k, size:] = rest.astype(bf16)


def block_diag(a, b):
    z = jnp.zeros_like(a)
    return jnp.concatenate(
        [jnp.concatenate([a, z], axis=1), jnp.concatenate([z, b], axis=1)], axis=0
    )


def two_heads(x):
    lane = lax.broadcasted_iota(jnp.int32, x.shape, 1)
    z = jnp.zeros_like(x)
    return jnp.concatenate([jnp.where(lane < HEAD_DIM, x, z), jnp.where(lane < HEAD_DIM, z, x)], 0)


def window(i, win, width, cross):
    if width == 1024:
        return 0
    if cross:
        return pl.multiple_of(win[i], 128)
    return pl.multiple_of(jnp.clip(i * BLK - 128, 0, 512), 128)


def attend_fwd(cross, from_norm, *refs):
    (win, x, xg, xs, blow, pq, pk, own, land, gain, shift) = refs[:11]
    (n_o, r_o, y_o, pt_o, q_o, v_o, kt_o, ot_o) = refs[11:19]
    (wt, k_s, vt_s) = refs[19:]
    i = pl.program_id(0)

    @pl.when(i == 0)
    def _():
        build(wt, own, land, 4, 16)
        for b in range(4):
            rows = slice(b * BLK, (b + 1) * BLK)
            kb = blow[rows]
            k_s[rows] = nt(kb, wt[1]).astype(bf16)
            v_o[rows] = nt(kb, wt[2]).astype(bf16)
            kt_o[:, rows] = nt(wt[1], kb).astype(bf16)
            vt_s[:, rows] = nt(wt[2], kb).astype(bf16)

    xv = x[...].astype(f32)
    if from_norm:
        xv = xv * xg[...] + xs[...]
    xl = xv.astype(bf16)
    qt = (nt(wt[0], xl) * 0.125).astype(bf16)
    q_o[...] = (nt(xl, wt[0]) * 0.125).astype(bf16)

    def heads(width):
        start = window(i, win, width, cross)
        keys = pl.ds(start, width)
        bias = jnp.where(pk[keys] == pq[...], 0.0, FLOOR).astype(f32)
        bias = jnp.concatenate([bias, bias], axis=1)
        for p in range(4):
            lanes = slice(p * 128, p * 128 + 128)
            rhs = block_diag(qt[p * 128 : p * 128 + 64], qt[p * 128 + 64 : p * 128 + 128])
            s = nn(k_s[keys, lanes], rhs) + bias
            e = jnp.exp(s - jnp.max(s, axis=0, keepdims=True))
            pt = (e * (1.0 / jnp.sum(e, axis=0, keepdims=True))).astype(bf16)
            pt_o[0, p, :width] = pt
            for h in range(2):
                ch = slice(p * 128 + h * 64, p * 128 + h * 64 + 64)
                ot_o[ch] = nn(vt_s[ch, keys], pt[:, h * BLK : (h + 1) * BLK]).astype(bf16)

    if cross:
        pl.when(win[4 + i] == 0)(lambda: heads(512))
        pl.when(win[4 + i] != 0)(lambda: heads(1024))
    else:
        heads(512)
    n, r = layer_norm(xv + tn(ot_o[...], wt[3]))
    n_o[...] = n
    r_o[...] = r
    y_o[...] = (n * gain[...] + shift[...]).astype(bf16)


def attend_bwd(cross, *refs):
    (win, dy, n, r, gain, own, land, pt, v, kt, q, ot, alow, blow) = refs[:14]
    if cross:
        dx_o, dkey_o, dqkv_o, dwo_o, gs_o = refs[14:19]
        wt, dk_s, dv_s = refs[19:]
    else:
        dx_o, dqkv_o, dwo_o, gs_o = refs[14:18]
        wt, dk_s, dv_s = refs[18:]
    i = pl.program_id(0)

    @pl.when(i == 0)
    def _():
        build(wt, own, land, 4, 16)
        dk_s[...] = jnp.zeros_like(dk_s)
        dv_s[...] = jnp.zeros_like(dv_s)
        dqkv_o[...] = jnp.zeros_like(dqkv_o)
        dwo_o[...] = jnp.zeros_like(dwo_o)
        gs_o[...] = jnp.zeros_like(gs_o)

    dyv, nv = dy[...], n[...]
    gs_o[0:1] += jnp.sum(dyv * nv, axis=0, keepdims=True)
    gs_o[1:2] += jnp.sum(dyv, axis=0, keepdims=True)
    d = layer_norm_back(dyv, nv, r[...], gain[...])
    g = d.astype(bf16)
    do = nt(g, wt[3]).astype(bf16)
    dot = nt(wt[3], g).astype(bf16)
    otv = ot[...]
    prod = dot.astype(f32) * otv.astype(f32)
    dqt = []

    def heads(width):
        start = window(i, win, width, cross)
        keys = pl.ds(start, width)
        rows = []
        for p in range(4):
            lanes = slice(p * 128, p * 128 + 128)
            a = slice(p * 128, p * 128 + 64)
            b = slice(p * 128 + 64, p * 128 + 128)
            delta = jnp.concatenate(
                [jnp.sum(prod[a], axis=0, keepdims=True), jnp.sum(prod[b], axis=0, keepdims=True)],
                axis=1,
            )
            dpt = nn(v[keys, lanes], block_diag(dot[a], dot[b]))
            ptv = pt[0, p, :width]
            dst = (ptv.astype(f32) * (dpt - delta)).astype(bf16)
            dv_s[keys, lanes] += nn(ptv, two_heads(do[:, lanes]))
            dk_s[keys, lanes] += nn(dst, two_heads(q[:, lanes]))
            rows.append((nn(kt[a, keys], dst[:, :BLK]) * 0.125).astype(bf16))
            rows.append((nn(kt[b, keys], dst[:, BLK:]) * 0.125).astype(bf16))
        dqt = jnp.concatenate(rows, axis=0)
        dqkv_o[0] += nn(dqt[:128], alow[...])
        dx = d + tn(dqt, wt[0])
        if cross:
            dx_o[...] = dx
        else:
            dx_o[pl.ds(pl.multiple_of(i * BLK, BLK), BLK)] = dx

    if cross:
        pl.when(win[4 + i] == 0)(lambda: heads(512))
        pl.when(win[4 + i] != 0)(lambda: heads(1024))
    else:
        heads(512)
    dwo_o[...] += nn(otv[:128], g)

    @pl.when(i == 3)
    def _():
        for b in range(4):
            rows = slice(b * BLK, (b + 1) * BLK)
            dkb, dvb = dk_s[rows].astype(bf16), dv_s[rows].astype(bf16)
            kx = nn(dkb, wt[1]) + nn(dvb, wt[2])
            if cross:
                dkey_o[rows] = kx
            else:
                dx_o[rows] += kx
            bl = blow[rows]
            dqkv_o[1] += tn(dkb[:, :128], bl)
            dqkv_o[2] += tn(dvb[:, :128], bl)


def ffn_fwd(*refs):
    (np_, gp_, sp_, alow, own, land, gain, shift) = refs[:8]
    (n_o, r_o, y_o, h_o, slope_o) = refs[8:13]
    (w,) = refs[13:]
    i = pl.program_id(0)

    @pl.when(i == 0)
    def _():
        build(w, own, land, 2, 64)

    acc = np_[...] * gp_[...] + sp_[...]
    al = alow[...]
    for c in range(4):
        hid = slice(c * 512, (c + 1) * 512)
        before = nt(al, w[0, hid])
        cdf = 0.5 + 0.5 * lax.erf(before * (0.5**0.5))
        pdf = jnp.exp(before * before * -0.5) * 0.3989422804014327
        slope_o[:, hid] = (cdf + before * pdf).astype(bf16)
        hidden = (before * cdf).astype(bf16)
        if c == 0:
            h_o[...] = hidden
        acc += nn(hidden, w[1, hid])
    n, r = layer_norm(acc)
    n_o[...] = n
    r_o[...] = r
    y_o[...] = (n * gain[...] + shift[...]).astype(bf16)


def ffn_bwd(two_dy, *refs):
    if two_dy:
        (dy, dy2, n, r, gain, alow, own, land, h, slope) = refs[:10]
        refs = refs[10:]
    else:
        (dy, n, r, gain, alow, own, land, h, slope) = refs[:9]
        refs = refs[9:]
    (dx_o, dw1_o, dw2_o, gs_o, w) = refs
    i = pl.program_id(0)

    @pl.when(i == 0)
    def _():
        build(w, own, land, 2, 64)
        dw1_o[...] = jnp.zeros_like(dw1_o)
        dw2_o[...] = jnp.zeros_like(dw2_o)
        gs_o[...] = jnp.zeros_like(gs_o)

    dyv, nv = dy[...].astype(f32), n[...]
    if two_dy:
        dyv = dyv + dy2[...]
    gs_o[0:1] += jnp.sum(dyv * nv, axis=0, keepdims=True)
    gs_o[1:2] += jnp.sum(dyv, axis=0, keepdims=True)
    d = layer_norm_back(dyv, nv, r[...], gain[...])
    g = d.astype(bf16)
    acc = d
    for c in range(4):
        hid = slice(c * 512, (c + 1) * 512)
        db = (nt(g, w[1, hid]) * slope[:, hid].astype(f32)).astype(bf16)
        acc += nn(db, w[0, hid])
        if c == 0:
            dw1_o[...] += tn(alow[...], db)
            dw2_o[...] += tn(h[...], g)
    dx_o[...] = acc


def whole(shape):
    return pl.BlockSpec(shape, lambda i: (0,) * len(shape))


def rows_of(width):
    return pl.BlockSpec((BLK, width), lambda i: (i, 0))


SDS = jax.ShapeDtypeStruct
SMEM_SPEC = pl.BlockSpec(memory_space=pltpu.SMEM)
PARAMS = pltpu.CompilerParams(vmem_limit_bytes=60 * MB)


def call_attend_fwd(cross, from_norm, win, x, xg, xs, blow, pq, pk, own, land, gain, shift):
    width = 1024 if cross else 512
    return pl.pallas_call(
        functools.partial(attend_fwd, cross, from_norm),
        grid=(4,),
        in_specs=[
            SMEM_SPEC,
            rows_of(512),
            whole((1, 512)),
            whole((1, 512)),
            whole((1024, 512)),
            pl.BlockSpec((1, BLK), lambda i: (0, i)),
            whole((1024, 1)),
            whole((4, 128, 512)),
            whole((24, 64, 512)),
            whole((1, 512)),
            whole((1, 512)),
        ],
        out_specs=[
            rows_of(512),
            rows_of(1),
            rows_of(512),
            pl.BlockSpec((1, 4, width, 512), lambda i: (i, 0, 0, 0)),
            rows_of(512),
            whole((1024, 512)),
            whole((512, 1024)),
            pl.BlockSpec((512, BLK), lambda i: (0, i)),
        ],
        out_shape=[
            SDS((1024, 512), f32),
            SDS((1024, 1), f32),
            SDS((1024, 512), bf16),
            SDS((4, 4, width, 512), bf16),
            SDS((1024, 512), bf16),
            SDS((1024, 512), bf16),
            SDS((512, 1024), bf16),
            SDS((512, 1024), bf16),
        ],
        scratch_shapes=[VM((4, 512, 512), bf16), VM((1024, 512), bf16), VM((512, 1024), bf16)],
        compiler_params=PARAMS,
    )(win, x, xg, xs, blow, pq, pk, own, land, gain, shift)


def call_attend_bwd(cross, win, dy, n, r, gain, own, land, saved, alow, blow):
    pt, q, v, kt, ot = saved
    width = 1024 if cross else 512
    dx_specs = [rows_of(512), whole((1024, 512))] if cross else [whole((1024, 512))]
    return pl.pallas_call(
        functools.partial(attend_bwd, cross),
        grid=(4,),
        in_specs=[
            SMEM_SPEC,
            rows_of(512),
            rows_of(512),
            rows_of(1),
            whole((1, 512)),
            whole((4, 128, 512)),
            whole((24, 64, 512)),
            pl.BlockSpec((1, 4, width, 512), lambda i: (i, 0, 0, 0)),
            whole((1024, 512)),
            whole((512, 1024)),
            rows_of(512),
            pl.BlockSpec((512, BLK), lambda i: (0, i)),
            rows_of(512),
            whole((1024, 512)),
        ],
        out_specs=dx_specs + [whole((3, 128, 512)), whole((128, 512)), whole((8, 512))],
        out_shape=[SDS((1024, 512), f32)] * len(dx_specs)
        + [SDS((3, 128, 512), f32), SDS((128, 512), f32), SDS((8, 512), f32)],
        scratch_shapes=[VM((4, 512, 512), bf16), VM((1024, 512), f32), VM((1024, 512), f32)],
        compiler_params=PARAMS,
    )(win, dy, n, r, gain, own, land, pt, v, kt, q, ot, alow, blow)


def call_ffn_fwd(n, g, s, alow, own, land, gain, shift):
    return pl.pallas_call(
        ffn_fwd,
        grid=(4,),
        in_specs=[
            rows_of(512),
            whole((1, 512)),
            whole((1, 512)),
            rows_of(512),
            whole((2, 512, 512)),
            whole((24, 128, 512)),
            whole((1, 512)),
            whole((1, 512)),
        ],
        out_specs=[rows_of(512), rows_of(1), rows_of(512), rows_of(512), rows_of(2048)],
        out_shape=[
            SDS((1024, 512), f32),
            SDS((1024, 1), f32),
            SDS((1024, 512), bf16),
            SDS((1024, 512), bf16),
            SDS((1024, 2048), bf16),
        ],
        scratch_shapes=[VM((2, 2048, 512), bf16)],
        compiler_params=PARAMS,
    )(n, g, s, alow, own, land, gain, shift)


def call_ffn_bwd(dys, n, r, gain, alow, own, land, h, slope):
    return pl.pallas_call(
        functools.partial(ffn_bwd, len(dys) == 2),
        grid=(4,),
        in_specs=[rows_of(512)] * len(dys)
        + [
            rows_of(512),
            rows_of(1),
            whole((1, 512)),
            rows_of(512),
            whole((2, 512, 512)),
            whole((24, 128, 512)),
            rows_of(512),
            rows_of(2048),
        ],
        out_specs=[rows_of(512), whole((512, 512)), whole((512, 512)), whole((8, 512))],
        out_shape=[
            SDS((1024, 512), f32),
            SDS((512, 512), f32),
            SDS((512, 512), f32),
            SDS((8, 512), f32),
        ],
        scratch_shapes=[VM((2, 2048, 512), bf16)],
        compiler_params=PARAMS,
    )(*dys, n, r, gain, alow, own, land, h, slope)


def plane_index():
    dp = lax.axis_index("dp")
    return dp, lax.rem(dp, 8)


def barrier_with(peers):
    sem = pltpu.get_barrier_semaphore()
    for peer in peers:
        pl.semaphore_signal(sem, inc=1, device_id=peer, device_id_type=MESH)
    pl.semaphore_wait(sem, len(peers))


def gather_kernel(tn_, groups, *refs):
    own, land = refs[:groups], refs[groups : 2 * groups]
    zs, zr, ps, pr = refs[2 * groups :]
    dp = lax.axis_index("dp")
    z = lax.axis_index("tensor")
    core = dp + 1 - 2 * lax.rem(dp, 2)
    xn = dp + 2 - 4 * lax.rem(lax.div(dp, 2), 2)
    yn = dp + 4 - 8 * lax.rem(lax.div(dp, 4), 2)
    zn = [lax.rem(z + k, tn_) for k in range(1, tn_)]
    barrier_with([(core, z), (xn, z), (yn, z)] + [(dp, k) for k in zn])

    def copy(src, dst, ss, rs, dev):
        return pltpu.make_async_remote_copy(
            src_ref=src, dst_ref=dst, send_sem=ss, recv_sem=rs, device_id=dev, device_id_type=MESH
        )

    first = []
    for g in range(groups):
        cs = [
            copy(own[g], land[g].at[k - 1, 0, 0], zs.at[g, k - 1], zr.at[g, k - 1],
                 (dp, lax.rem(z + tn_ - k, tn_)))
            for k in range(1, tn_)
        ]
        for c in cs:
            c.start()
        first.append(cs)

    second, third, pairs = [], [], []
    def stage2(g):
        for c in first[g]:
            c.wait_recv()
        l = land[g]
        cs = [
            copy(l.at[:, 0, 0], l.at[:, 0, 1], ps.at[g, 0], pr.at[g, 0], (xn, z)),
            copy(l.at[:, 0, 0], l.at[:, 0, 2], ps.at[g, 1], pr.at[g, 1], (yn, z)),
            copy(l.at[:, 0, 0], l.at[:, 1, 0], ps.at[g, 2], pr.at[g, 2], (core, z)),
        ]
        for c in cs:
            c.start()
        second.append(cs)

    def stage3(g):
        half = own[g].shape[0] // 2
        l = land[g]
        a, b = pl.ds(0, half), pl.ds(half, half)
        cs = [
            copy(l.at[:, 0, 1, a], l.at[:, 0, 3, a], ps.at[g, 3], pr.at[g, 3], (yn, z)),
            copy(l.at[:, 0, 2, b], l.at[:, 0, 3, b], ps.at[g, 4], pr.at[g, 4], (xn, z)),
            copy(l.at[:, 0, 1], l.at[:, 1, 1], ps.at[g, 5], pr.at[g, 5], (core, z)),
            copy(l.at[:, 0, 2], l.at[:, 1, 2], ps.at[g, 6], pr.at[g, 6], (core, z)),
        ]
        second[g][0].wait_recv()
        cs[0].start()
        cs[2].start()
        second[g][1].wait_recv()
        cs[1].start()
        cs[3].start()
        third.append(cs)

    def stage4(g):
        l = land[g]
        third[g][0].wait_recv()
        third[g][1].wait_recv()
        c = copy(l.at[:, 0, 3], l.at[:, 1, 3], ps.at[g, 7], pr.at[g, 7], (core, z))
        c.start()
        pairs.append(c)

    for t in range(groups + 2):
        if t < groups:
            stage2(t)
        if 0 <= t - 1 < groups:
            stage3(t - 1)
        if 0 <= t - 2 < groups:
            stage4(t - 2)
    for g in range(groups):
        second[g][2].wait_recv()
        third[g][2].wait_recv()
        third[g][3].wait_recv()
        pairs[g].wait_recv()
        for c in first[g] + second[g] + third[g] + [pairs[g]]:
            c.wait_send()


def gather_weights(tn_, blobs):
    groups = len(blobs)
    return pl.pallas_call(
        functools.partial(gather_kernel, tn_, groups),
        in_specs=[pl.BlockSpec(memory_space=pl.ANY)] * groups,
        out_specs=[pl.BlockSpec(memory_space=pl.ANY)] * groups,
        out_shape=[SDS((3, 2, 4) + b.shape, f32) for b in blobs],
        scratch_shapes=[
            pltpu.SemaphoreType.DMA((groups, 3)),
            pltpu.SemaphoreType.DMA((groups, 3)),
            pltpu.SemaphoreType.DMA((groups, 8)),
            pltpu.SemaphoreType.DMA((groups, 8)),
        ],
        compiler_params=pltpu.CompilerParams(collective_id=0, has_side_effects=True),
    )(*blobs)


def sum_kernel(count, *refs):
    part, out = refs[:count], refs[count : 2 * count]
    got_c, got_a, got_b, got_a2, got_b2, held = (
        refs[2 * count + k * count : 2 * count + (k + 1) * count] for k in range(6)
    )
    ss, rs = refs[8 * count :]
    dp, j = plane_index()
    z = lax.axis_index("tensor")
    c, x, y = lax.rem(j, 2), lax.rem(lax.div(j, 2), 2), lax.div(j, 4)
    cn, xn, yn = (dp + 1 - 2 * c, z), (dp + 2 - 4 * x, z), (dp + 4 - 8 * y, z)
    barrier_with([cn, xn, yn])

    def copy(k, s, src, dst, dev):
        return pltpu.make_async_remote_copy(
            src_ref=src, dst_ref=dst, send_sem=ss.at[k, s], recv_sem=rs.at[k, s],
            device_id=dev, device_id_type=MESH,
        )

    every = []

    def go(cp):
        cp.start()
        every.append(cp)
        return cp

    halves = []
    for k in range(count):
        h = part[k].shape[3] // 2
        halves.append((pl.ds(0, h), pl.ds(h, h)))
    s0 = [go(copy(k, 0, part[k].at[:, :, 1 - c], got_c[k], cn)) for k in range(count)]
    s1 = []
    for k in range(count):
        a, b = halves[k]
        s0[k].wait_recv()
        held[k][...] = part[k][:, :, c] + got_c[k][...]
        s1.append((
            go(copy(k, 1, held[k].at[:, 1 - x, a], got_a[k], xn)),
            go(copy(k, 2, held[k].at[1 - y, :, b], got_b[k], yn)),
        ))
    s2 = []
    for k in range(count):
        a, b = halves[k]
        s1[k][0].wait_recv()
        held[k][:, x, a] += got_a[k][...]
        s1[k][1].wait_recv()
        held[k][y, :, b] += got_b[k][...]
        s2.append((
            go(copy(k, 3, held[k].at[1 - y, x, a], got_a2[k], yn)),
            go(copy(k, 4, held[k].at[y, 1 - x, b], got_b2[k], xn)),
        ))
    s3 = []
    for k in range(count):
        a, b = halves[k]
        o = out[k]
        s2[k][0].wait_recv()
        o[y, x, c, a] = held[k][y, x, a] + got_a2[k][...]
        s2[k][1].wait_recv()
        o[y, x, c, b] = held[k][y, x, b] + got_b2[k][...]
        s3.append((
            go(copy(k, 5, o.at[y, x, c, a], o.at[y, x, c, a], yn)),
            go(copy(k, 6, o.at[y, x, c, b], o.at[y, x, c, b], xn)),
        ))
    s4 = []
    for k in range(count):
        a, b = halves[k]
        o = out[k]
        s3[k][0].wait_recv()
        s3[k][1].wait_recv()
        s4.append((
            go(copy(k, 7, o.at[:, x, c, a], o.at[:, x, c, a], xn)),
            go(copy(k, 8, o.at[y, :, c, b], o.at[y, :, c, b], yn)),
        ))
    s5 = []
    for k in range(count):
        o = out[k]
        s4[k][0].wait_recv()
        s4[k][1].wait_recv()
        s5.append(go(copy(k, 9, o.at[:, :, c], o.at[:, :, c], cn)))
    for k in range(count):
        s5[k].wait_recv()
    for cp in every:
        cp.wait_send()


def sum_over_plane(parts):
    count = len(parts)
    shapes = [p.shape[3:] for p in parts]

    def bufs(lead, cut):
        return [VM(lead + (r // cut, w), f32) for r, w in shapes]

    return pl.pallas_call(
        functools.partial(sum_kernel, count),
        in_specs=[pl.BlockSpec(memory_space=pltpu.VMEM)] * count,
        out_specs=[pl.BlockSpec(memory_space=pltpu.VMEM)] * count,
        out_shape=[SDS(p.shape, f32) for p in parts],
        scratch_shapes=bufs((2, 2), 1) + bufs((2,), 2) + bufs((2,), 2) + bufs((), 2) + bufs((), 2)
        + bufs((2, 2), 1)
        + [pltpu.SemaphoreType.DMA((count, 10)), pltpu.SemaphoreType.DMA((count, 10))],
        compiler_params=pltpu.CompilerParams(
            collective_id=1, has_side_effects=True, vmem_limit_bytes=60 * MB
        ),
    )(*parts)


def attn_slices(qkv, out_w, j):
    own = jnp.concatenate([jnp.transpose(qkv, (0, 2, 1)), out_w[None]], axis=0)
    parts = own.reshape(4, 2, 4, 16, own.shape[2])
    piece = lax.dynamic_slice(
        parts, (0, lax.rem(j, 2), lax.div(j, 2), 0, 0), (4, 1, 1, 16, own.shape[2])
    )
    return own, piece.reshape(64, own.shape[2]).astype(f32)


def ffn_slices(w_in, w_out, j):
    own = jnp.stack([w_in.T, w_out])
    parts = own.reshape(2, 8, 64, own.shape[2])
    piece = lax.dynamic_slice(parts, (0, j, 0, 0), (2, 1, 64, own.shape[2]))
    return own, piece.reshape(128, own.shape[2]).astype(f32)


def cross_windows(source, target):
    low, high = target[0, ::BLK], target[0, BLK - 1 :: BLK]
    begin = jnp.sum((source[0][None, :] < low[:, None]).astype(jnp.int32), axis=1)
    end = jnp.sum((source[0][None, :] <= high[:, None]).astype(jnp.int32), axis=1)
    start = jnp.minimum(begin // 128 * 128, 512)
    return jnp.concatenate([start, (end - start > 512).astype(jnp.int32)])


def per_device(planes, tn_, enc_in, dec_in, src_idx, tgt_idx, masked, mask_embed, enc_qkv, enc_out_w,
               enc_w1, enc_w2, self_qkv, self_out_w, cross_qkv, cross_out_w, dec_w1, dec_w2,
               gains, shifts, enc_cot, dec_cot):
    _, j = plane_index()
    own_e, blob_e = attn_slices(enc_qkv, enc_out_w, j)
    own_s, blob_s = attn_slices(self_qkv, self_out_w, j)
    own_c, blob_c = attn_slices(cross_qkv, cross_out_w, j)
    own_f, blob_f = ffn_slices(enc_w1, enc_w2, j)
    own_d, blob_d = ffn_slices(dec_w1, dec_w2, j)
    lands = gather_weights(tn_, [blob_e, blob_f, blob_s, blob_c, blob_d])
    land_e, land_f, land_s, land_c, land_d = [a.reshape((24,) + a.shape[3:]) for a in lands]

    x_e, x_d = enc_in[0], dec_in[0]
    is_masked = (masked[0] == 1)[:, None]
    target = jnp.where(is_masked, mask_embed[None, :], x_d.astype(f32))
    target_low = target.astype(bf16)
    src_col, tgt_col = src_idx.reshape(1024, 1), tgt_idx.reshape(1024, 1)
    win = cross_windows(src_idx, tgt_idx)
    g = [gains[k : k + 1] for k in range(5)]
    s = [shifts[k : k + 1] for k in range(5)]

    n0, r0, first_low, *save_e = call_attend_fwd(
        False, False, win, x_e, g[0], s[0], x_e, src_idx, src_col, own_e, land_e, g[0], s[0])
    n1, r1, enc_low, h_e, slope_e = call_ffn_fwd(
        n0, g[0], s[0], first_low, own_f, land_f, g[1], s[1])
    n2, r2, second_low, *save_s = call_attend_fwd(
        False, False, win, target, g[2], s[2], target_low, tgt_idx, tgt_col, own_s, land_s, g[2], s[2])
    n3, r3, third_low, *save_c = call_attend_fwd(
        True, True, win, n2, g[2], s[2], enc_low, tgt_idx, src_col, own_c, land_c, g[3], s[3])
    n4, r4, dec_low, h_d, slope_d = call_ffn_fwd(
        n3, g[3], s[3], third_low, own_d, land_d, g[4], s[4])

    d_third, dw1_d, dw2_d, gs4 = call_ffn_bwd(
        [dec_cot[0]], n4, r4, g[4], third_low, own_d, land_d, h_d, slope_d)
    d_second, d_key, dqkv_c, dwo_c, gs3 = call_attend_bwd(
        True, win, d_third, n3, r3, g[3], own_c, land_c, save_c, second_low, enc_low)
    d_target, dqkv_s, dwo_s, gs2 = call_attend_bwd(
        False, win, d_second, n2, r2, g[2], own_s, land_s, save_s, target_low, target_low)
    d_first, dw1_e, dw2_e, gs1 = call_ffn_bwd(
        [enc_cot[0], d_key], n1, r1, g[1], first_low, own_f, land_f, h_e, slope_e)
    d_enc, dqkv_e, dwo_e, gs0 = call_attend_bwd(
        False, win, d_first, n0, r0, g[0], own_e, land_e, save_e, x_e, x_e)

    dec_grad = jnp.where(is_masked, 0.0, d_target)
    mask_grad = jnp.sum(jnp.where(is_masked, d_target, 0.0), axis=0)
    small = jnp.concatenate([mask_grad[None]] + [a[:2] for a in (gs0, gs1, gs2, gs3, gs4)])
    small = jnp.pad(small, ((0, 21), (0, 0))).reshape(2, 2, 2, 16, 128)

    def chunks(a):
        return a.reshape(2, 2, 2, a.size // 4096, 512)

    mats = [dqkv_e, dwo_e, dw1_e, dw2_e, dqkv_s, dwo_s, dqkv_c, dwo_c, dw1_d, dw2_d]
    sums = sum_over_plane([chunks(a) for a in mats] + [small])
    if planes > 1:
        same = [[p * 8 + k for p in range(planes)] for k in range(8)]
        sums = lax.psum(sums, "dp", axis_index_groups=same)
    dqkv_e, dwo_e, dw1_e, dw2_e, dqkv_s, dwo_s, dqkv_c, dwo_c, dw1_d, dw2_d = [
        a.reshape(m.shape) for a, m in zip(sums, mats)]
    dqkv_e, dqkv_s, dqkv_c = [jnp.transpose(a, (0, 2, 1)) for a in (dqkv_e, dqkv_s, dqkv_c)]
    small = sums[-1].reshape(32, 512)
    return (
        enc_low[None],
        dec_low[None],
        d_enc[None],
        dec_grad[None],
        small[0],
        dqkv_e,
        dwo_e,
        dw1_e,
        dw2_e,
        dqkv_s,
        dwo_s,
        dqkv_c,
        dwo_c,
        dw1_d,
        dw2_d,
        small[1:11:2],
        small[2:12:2],
    )


def solution(mesh):
    tokens, index = P("dp", None, None), P("dp", None)
    qkv, cols, rows = P(None, None, "tensor"), P(None, "tensor"), P("tensor", None)
    weights = (qkv, rows, cols, rows, qkv, rows, qkv, rows, cols, rows)
    return jax.shard_map(
        functools.partial(per_device, mesh.shape["dp"] // 8, mesh.shape["tensor"]),
        mesh=mesh,
        in_specs=(tokens, tokens, index, index, index, P()) + weights + (P(), P(), tokens, tokens),
        out_specs=(tokens,) * 4 + (P(),) + weights + (P(), P()),
        check_vma=False,
    )
```

```python
import functools

import jax
import jax.numpy as jnp
from jax import lax
from jax.experimental import pallas as pl
from jax.experimental.pallas import tpu as pltpu
from jax.sharding import PartitionSpec as P

f32, bf16 = jnp.float32, jnp.bfloat16
HEAD_DIM = 64
EPS = 1e-05
FLOOR = -1000000000.0
BLK = 256
MB = 1 << 20
VMEM_MB = 60
MESH = pl.DeviceIdType.MESH
VM = pltpu.VMEM


def nt(a, b):
    return lax.dot_general(a, b, (((1,), (1,)), ((), ())), preferred_element_type=f32)


def nn(a, b):
    return lax.dot_general(a, b, (((1,), (0,)), ((), ())), preferred_element_type=f32)


def tn(a, b):
    return lax.dot_general(a, b, (((0,), (0,)), ((), ())), preferred_element_type=f32)


def layer_norm(v):
    c = v - jnp.mean(v, axis=-1, keepdims=True)
    r = lax.rsqrt(jnp.mean(c * c, axis=-1, keepdims=True) + EPS)
    return c * r, r


def layer_norm_back(dy, n, r, gain):
    dn = dy * gain
    m1 = jnp.mean(dn, axis=-1, keepdims=True)
    m2 = jnp.mean(dn * n, axis=-1, keepdims=True)
    return r * (dn - m1 - n * m2)


def block_diag(a, b):
    z = jnp.zeros_like(a)
    return jnp.concatenate(
        [jnp.concatenate([a, z], axis=1), jnp.concatenate([z, b], axis=1)], axis=0
    )


def two_heads(x):
    lane = lax.broadcasted_iota(jnp.int32, x.shape, 1)
    z = jnp.zeros_like(x)
    return jnp.concatenate([jnp.where(lane < HEAD_DIM, x, z), jnp.where(lane < HEAD_DIM, z, x)], 0)


def rows_at(b):
    return slice(b * BLK, (b + 1) * BLK)


def self_start(b):
    return min(max(b * BLK - 128, 0), 512)


def project_slot(w, kinds, get, rows_out):
    for b in range(4):
        xb = get(b)
        nat = nt(xb, w[kinds[0] * 128 : kinds[-1] * 128 + 128])
        tr = nt(w[kinds[0] * 128 : kinds[-1] * 128 + 128], xb)
        for k, kind in enumerate(kinds):
            cut = slice(k * 128, k * 128 + 128)
            for dst, val in rows_out(kind, b, nat[:, cut], tr[cut]):
                dst[...] = val.astype(bf16)


def softmax_block(k_s, qt, keys, pk, pq):
    bias = jnp.where(pk == pq, 0.0, FLOOR).astype(f32)
    s = nn(k_s[keys], block_diag(qt[:64], qt[64:])) + jnp.concatenate([bias, bias], axis=1)
    e = jnp.exp(s - jnp.max(s, axis=0, keepdims=True))
    return (e * (1.0 / jnp.sum(e, axis=0, keepdims=True))).astype(bf16)


def mix_block(vt_s, keys, pt):
    return jnp.concatenate([nn(vt_s[:64, keys], pt[:, :BLK]), nn(vt_s[64:, keys], pt[:, BLK:])], 0)


def wide(pkb):
    return jnp.concatenate([pkb, pkb], axis=1)


def ffn_slot(w, al, acc, slope_o, h_o, first, tick):
    for b in range(4):
        rows = rows_at(b)
        before = nt(al[rows], w[0])
        cdf = 0.5 + 0.5 * lax.erf(before * (0.5**0.5))
        pdf = jnp.exp(before * before * -0.5) * 0.3989422804014327
        slope_o[rows] = (cdf + before * pdf).astype(bf16)
        hidden = (before * cdf).astype(bf16)

        @pl.when(first)
        def _():
            h_o[rows] = hidden

        acc[rows] += nn(hidden, w[1])
        tick(b)


def finish_norm(acc, gain, shift, n_ref, r_o, y_ref):
    for b in range(4):
        rows = rows_at(b)
        n, r = layer_norm(acc[rows])
        n_ref[rows] = n
        r_o[rows] = r
        y_ref[rows] = (n * gain + shift).astype(bf16)


def plane_index():
    dp = lax.axis_index("dp")
    return dp, lax.rem(dp, 8)


def neighbours(tensor):
    dp, j = plane_index()
    z = lax.axis_index("tensor")
    c, x, y = lax.rem(j, 2), lax.rem(lax.div(j, 2), 2), lax.div(j, 4)
    core, xn, yn = (dp + 1 - 2 * c, z), (dp + 2 - 4 * x, z), (dp + 4 - 8 * y, z)
    down = {k: (dp, lax.rem(z + tensor - k, tensor)) for k in range(1, tensor)}
    return (c, x, y), core, xn, yn, down


def barrier_with(peers):
    sem = pltpu.get_barrier_semaphore()
    for peer in peers:
        pl.semaphore_signal(sem, inc=1, device_id=peer, device_id_type=MESH)
    pl.semaphore_wait(sem, len(peers))


class Gather:
    def __init__(self, items, ss, rs, tensor):
        self.items, self.ss, self.rs = items, ss, rs
        _, self.core, self.xn, self.yn, self.down = neighbours(tensor)

    def barrier(self):
        barrier_with([self.core, self.xn, self.yn] + list(self.down.values()))

    def copy(self, t, s, src, dst, dev):
        return lambda: pltpu.make_async_remote_copy(
            src_ref=src, dst_ref=dst, send_sem=self.ss.at[t, s], recv_sem=self.rs.at[t, s],
            device_id=dev, device_id_type=MESH,
        )

    def make(self, t):
        slot, src, land, spread = self.items[t]
        if not spread:
            return [self.copy(t, 0, src, land, self.down[slot])]
        half = land.shape[1] // 2
        a, b = pl.ds(0, half), pl.ds(half, half)
        return [
            self.copy(t, 0, src, land.at[0], self.down[slot]) if src is not None else None,
            self.copy(t, 1, land.at[0], land.at[1], self.xn),
            self.copy(t, 2, land.at[0], land.at[2], self.yn),
            self.copy(t, 3, land.at[0], land.at[4], self.core),
            self.copy(t, 4, land.at[1, a], land.at[3, a], self.yn),
            self.copy(t, 5, land.at[1], land.at[5], self.core),
            self.copy(t, 6, land.at[2, b], land.at[3, b], self.xn),
            self.copy(t, 7, land.at[2], land.at[6], self.core),
            self.copy(t, 8, land.at[3], land.at[7], self.core),
        ]

    def send(self, t):
        self.make(t)[0]().start()

    def spread(self, t):
        c = self.make(t)
        if c[0] is not None:
            c[0]().wait_recv()
        for k in (1, 2, 3):
            c[k]().start()

    def relay(self, t):
        c = self.make(t)
        c[1]().wait_recv()
        c[4]().start()
        c[5]().start()
        c[2]().wait_recv()
        c[6]().start()
        c[7]().start()

    def pair(self, t):
        c = self.make(t)
        c[4]().wait_recv()
        c[6]().wait_recv()
        c[8]().start()

    def advance(self, t, last):
        if t <= last:
            self.spread(t)
        if 0 <= t - 1 <= last:
            self.relay(t - 1)
        if 0 <= t - 2 <= last:
            self.pair(t - 2)

    def done(self, t):
        c = self.make(t)
        for k in (3, 5, 7, 8):
            c[k]().wait_recv()

    def finish(self):
        for t in range(len(self.items)):
            for c in self.make(t):
                if c is not None:
                    c().wait_send()
            if not self.items[t][3]:
                self.make(t)[0]().wait_recv()


def run_events(t, steps, events, point):
    for step in steps:
        acts = events.get((step, point))
        if acts:

            @pl.when(t == step)
            def _(acts=acts):
                for act in acts:
                    act()


def es_of(t):
    kind = jnp.where((t == 1) | (t >= 5), 1, 0)
    p = jnp.where(t < 2, 0, jnp.where(t < 5, t - 1, t - 4))
    return kind, jnp.minimum(p, 3)


def es_block(t):
    kind, p = es_of(t)
    return kind * 4 + p


def first_kernel(tensor, *refs):
    (lows, target, idx, pkb, own_es, own_f, gains, shifts) = refs[:8]
    blob_e, blob_s, blob_f, blob_c, blob_d = refs[8:13]
    (wes_o, pt_o, q_o, v_o, kt_o, ot_o, wf_o, slope_o, h_o, r0_o, r2_o, r1_o, n0_o, n2_o,
     n1_o, y0_o, y2_o, encl_o, zc_o, zd_o) = refs[13:33]
    (land_a, land_f, accs, na, ylow, encl, k_s, qt_s, vt_s, ss, rs, cs) = refs[33:]
    t = pl.program_id(0)
    items = [(k, blob_e, land_a.at[k - 1], True) for k in (1, 2, 3)]
    items += [(k, blob_s, land_a.at[2 + k], True) for k in (1, 2, 3)]
    items += [(k, blob_f, land_f.at[k - 1], True) for k in (1, 2, 3)]
    items += [(k, blob_c, zc_o.at[k - 1], False) for k in (1, 2, 3)]
    items += [(1, blob_d, zd_o, False)]
    net = Gather(items, ss, rs, tensor)
    outs = [
        (na.at[0], n0_o), (ylow.at[0], y0_o), (na.at[1], n2_o), (ylow.at[1], y2_o),
        (accs.at[0], n1_o), (encl, encl_o),
    ]

    def out(k):
        return pltpu.make_async_copy(*outs[k], cs.at[k])

    last = 8
    ev = {}

    def at(step, point, *acts):
        ev.setdefault((step, point), []).extend(acts)

    def adv(k):
        return lambda: net.advance(k, last)

    def send(*ks):
        return lambda: [net.send(k) for k in ks]

    def done(k):
        return lambda: net.done(k)

    at(0, -1, net.barrier, send(0, 1, 2))
    at(1, 3, adv(0), send(3, 4, 5), adv(1))
    at(2, -1, adv(2), done(0))
    at(2, 2, adv(3), send(6, 7, 8))
    at(3, -1, done(1))
    at(3, 2, adv(4))
    at(4, -1, done(2))
    at(4, 2, adv(5))
    at(5, -1, done(3))
    at(5, 2, adv(6), send(9, 10, 11))
    at(6, -1, done(4))
    at(6, 2, adv(7))
    at(7, -1, done(5))
    at(7, 2, adv(8))
    at(8, 0, adv(9), send(12))
    at(8, 3, adv(10))
    at(9, -1, done(6))
    at(10, -1, done(7))
    at(11, -1, done(8))
    kind, p = es_of(t)
    es_steps, f_steps = range(8), range(8, 12)

    @pl.when(t < 8)
    def _():
        run_events(t, es_steps, ev, -1)

        @pl.when(p == 0)
        def _():
            wes_o[0] = own_es[kind]

        @pl.when((p == 0) & (kind == 0))
        def _():
            accs[0] = lows[0].astype(f32)

        @pl.when((p == 0) & (kind == 1))
        def _():
            accs[1] = target[...]

        @pl.when(p > 0)
        def _():
            for m in range(4):
                piece = land_a[kind * 3 + p - 1, :, m * 16 : (m + 1) * 16, :]
                wes_o[0, m * 128 : (m + 1) * 128] = piece.reshape(128, 512).astype(bf16)

        w = wes_o.at[0]

        def outs_of(m, b, nat, tr):
            rows = rows_at(b)
            if m == 0:
                return [(q_o.at[0, rows], nat * 0.125), (qt_s.at[:, rows], tr * 0.125)]
            if m == 1:
                return [(k_s.at[rows], nat), (kt_o.at[0, :, rows], tr)]
            return [(v_o.at[0, rows], nat), (vt_s.at[:, rows], tr)]

        project_slot(w, (0, 1, 2), lambda b: lows[kind, rows_at(b)], outs_of)
        for b in range(4):
            rows = rows_at(b)
            keys = slice(self_start(b), self_start(b) + 512)
            pt = softmax_block(k_s, qt_s[:, rows], keys, wide(pkb[kind, keys]), idx[kind, :, rows])
            pt_o[0, b] = pt
            ot = mix_block(vt_s, keys, pt).astype(bf16)
            ot_o[0, :, rows] = ot
            accs[kind, rows] += tn(ot, w[384:])
            run_events(t, es_steps, ev, b)

        @pl.when(t == 4)
        def _():
            finish_norm(accs.at[0], gains[0:1], shifts[0:1], na.at[0], r0_o, ylow.at[0])
            out(0).start()
            out(1).start()

        @pl.when(t == 7)
        def _():
            finish_norm(accs.at[1], gains[2:3], shifts[2:3], na.at[1], r2_o, ylow.at[1])
            out(2).start()
            out(3).start()

    @pl.when(t >= 8)
    def _():
        run_events(t, f_steps, ev, -1)

        @pl.when(t == 8)
        def _():
            wf_o[0] = own_f[...]
            accs[0] = na[0] * gains[0:1] + shifts[0:1]

        @pl.when(t > 8)
        def _():
            for m in range(2):
                piece = land_f[t - 9, :, m * 64 : (m + 1) * 64, :]
                wf_o[0, m] = piece.reshape(512, 512).astype(bf16)

        ffn_slot(wf_o.at[0], ylow.at[0], accs.at[0], slope_o, h_o, t == 8,
                 lambda b: run_events(t, f_steps, ev, b))

        @pl.when(t == 11)
        def _():
            finish_norm(accs.at[0], gains[1:2], shifts[1:2], accs.at[0], r1_o, encl)
            out(4).start()
            out(5).start()
            for k in range(6):
                out(k).wait()
            net.finish()


def held(shape):
    return pl.BlockSpec(shape, lambda t: (0,) * len(shape), pipeline_mode=pl.Buffered(1))


def kept(shape):
    return pl.BlockSpec(shape, lambda t: (0,) * len(shape))


ANY = pl.BlockSpec(memory_space=pl.ANY)
SMEM_SPEC = pl.BlockSpec(memory_space=pltpu.SMEM)
SDS = jax.ShapeDtypeStruct


def by_es(*tail):
    return pl.BlockSpec((1,) + tail, lambda t: (es_block(t),) + (0,) * len(tail))


def call_first(tensor, lows, target, idx, pkb, own_es, own_f, gains, shifts, blobs):
    def chunk(t):
        return jnp.maximum(t - 8, 0)

    n_items = 13
    return pl.pallas_call(
        functools.partial(first_kernel, tensor),
        grid=(12,),
        in_specs=[
            held((2, 1024, 512)), held((1024, 512)), held((2, 1, 1024)), held((2, 1024, 128)),
            held((2, 512, 512)), held((2, 512, 512)), held((5, 512)), held((5, 512)),
        ] + [ANY] * 5,
        out_specs=[
            by_es(512, 512), by_es(4, 512, 512), by_es(1024, 128), by_es(1024, 128),
            by_es(128, 1024), by_es(128, 1024),
            pl.BlockSpec((1, 2, 512, 512), lambda t: (chunk(t), 0, 0, 0)),
            pl.BlockSpec((1024, 512), lambda t: (0, chunk(t))),
            kept((1024, 512)), kept((1024, 1)), kept((1024, 1)), kept((1024, 1)),
        ] + [ANY] * 8,
        out_shape=[
            SDS((8, 512, 512), bf16), SDS((8, 4, 512, 512), bf16), SDS((8, 1024, 128), bf16),
            SDS((8, 1024, 128), bf16), SDS((8, 128, 1024), bf16), SDS((8, 128, 1024), bf16),
            SDS((4, 2, 512, 512), bf16), SDS((1024, 2048), bf16), SDS((1024, 512), bf16),
            SDS((1024, 1), f32), SDS((1024, 1), f32), SDS((1024, 1), f32),
            SDS((1024, 512), f32), SDS((1024, 512), f32), SDS((1024, 512), f32),
            SDS((1024, 512), bf16), SDS((1024, 512), bf16), SDS((1024, 512), bf16), SDS((3, 64, 512), f32), SDS((128, 512), f32),
        ],
        scratch_shapes=[
            VM((6, 8, 64, 512), f32), VM((3, 8, 128, 512), f32), VM((2, 1024, 512), f32),
            VM((2, 1024, 512), f32), VM((2, 1024, 512), bf16), VM((1024, 512), bf16),
            VM((1024, 128), bf16), VM((128, 1024), bf16), VM((128, 1024), bf16),
            pltpu.SemaphoreType.DMA((n_items, 9)), pltpu.SemaphoreType.DMA((n_items, 9)),
            pltpu.SemaphoreType.DMA((6,)),
        ],
        compiler_params=pltpu.CompilerParams(
            collective_id=0, has_side_effects=True, vmem_limit_bytes=VMEM_MB * MB
        ),
    )(lows, target, idx, pkb, own_es, own_f, gains, shifts, *blobs)


def second_kernel(tensor, *refs):
    (n2, qlow, klow, tgt, pkb, own_c, own_d, gains, shifts) = refs[:9]
    zc, zd1, blob_d = refs[9:12]
    (wc_o, pt_o, q_o, v_o, kt_o, ot_o, wd_o, slope_o, h_o, r3_o, r4_o, n3_o, n4_o, y3_o,
     dec_o) = refs[12:27]
    (land_c, land_d, acc, n3, ylow, decl, k_s, qt_s, vt_s, ss, rs, cs) = refs[27:]
    t = pl.program_id(0)
    items = [(k, None, land_c.at[k - 1], True) for k in (1, 2, 3)]
    items += [(1, None, land_d.at[0], True)]
    items += [(k, blob_d, land_d.at[k - 1], True) for k in (2, 3)]
    net = Gather(items, ss, rs, tensor)
    moves = [(zc.at[k], land_c.at[k, 0]) for k in range(3)] + [(zd1, land_d.at[0, 0])]
    moves += [(n3, n3_o), (ylow, y3_o), (acc, n4_o), (decl, dec_o)]

    def move(k):
        return pltpu.make_async_copy(*moves[k], cs.at[k])

    last = 5
    ev = {}

    def at(step, point, *acts):
        ev.setdefault((step, point), []).extend(acts)

    def adv(k):
        return lambda: net.advance(k, last)

    def done(k):
        return lambda: net.done(k)

    def begin():
        for k in range(4):
            move(k).start()
        net.barrier()
        net.send(4)
        for k in range(4):
            move(k).wait()

    at(0, -1, begin, adv(0))
    at(0, 1, adv(1))
    at(0, 3, adv(2))
    at(1, -1, done(0))
    at(1, 0, adv(3), lambda: net.send(5))
    at(2, -1, done(1))
    at(2, 0, adv(4))
    at(3, -1, done(2))
    at(3, 0, adv(5))
    at(3, 3, adv(6))
    at(4, 3, adv(7))
    at(5, -1, done(3))
    at(6, -1, done(4))
    at(7, -1, done(5))
    c_steps, d_steps = range(4), range(4, 8)

    @pl.when(t < 4)
    def _():
        run_events(t, c_steps, ev, -1)

        @pl.when(t == 0)
        def _():
            wc_o[0] = own_c[...]
            acc[...] = n2[...] * gains[2:3] + shifts[2:3]

        @pl.when(t > 0)
        def _():
            for m in range(4):
                piece = land_c[t - 1, :, m * 16 : (m + 1) * 16, :]
                wc_o[0, m * 128 : (m + 1) * 128] = piece.reshape(128, 512).astype(bf16)

        w = wc_o.at[0]

        def outs_of(m, b, nat, tr):
            rows = rows_at(b)
            if m == 0:
                return [(q_o.at[0, rows], nat * 0.125), (qt_s.at[:, rows], tr * 0.125)]
            if m == 1:
                return [(k_s.at[rows], nat), (kt_o.at[0, :, rows], tr)]
            return [(v_o.at[0, rows], nat), (vt_s.at[:, rows], tr)]

        project_slot(w, (0,), lambda b: qlow[rows_at(b)], outs_of)
        project_slot(w, (1, 2), lambda b: klow[rows_at(b)], outs_of)
        for b in range(4):
            rows = rows_at(b)
            keys = slice(0, 1024)
            pt = softmax_block(k_s, qt_s[:, rows], keys, wide(pkb[...]), tgt[:, rows])
            pt_o[0, b] = pt
            ot = mix_block(vt_s, keys, pt).astype(bf16)
            ot_o[0, :, rows] = ot
            acc[rows] += tn(ot, w[384:])
            run_events(t, c_steps, ev, b)

        @pl.when(t == 3)
        def _():
            finish_norm(acc, gains[3:4], shifts[3:4], n3, r3_o, ylow)
            move(4).start()
            move(5).start()

    @pl.when(t >= 4)
    def _():
        run_events(t, d_steps, ev, -1)

        @pl.when(t == 4)
        def _():
            wd_o[0] = own_d[...]
            acc[...] = n3[...] * gains[3:4] + shifts[3:4]

        @pl.when(t > 4)
        def _():
            for m in range(2):
                piece = land_d[t - 5, :, m * 64 : (m + 1) * 64, :]
                wd_o[0, m] = piece.reshape(512, 512).astype(bf16)

        ffn_slot(wd_o.at[0], ylow, acc, slope_o, h_o, t == 4,
                 lambda b: run_events(t, d_steps, ev, b))

        @pl.when(t == 7)
        def _():
            finish_norm(acc, gains[4:5], shifts[4:5], acc, r4_o, decl)
            move(6).start()
            move(7).start()
            for k in range(4, 8):
                move(k).wait()
            net.finish()


def call_second(tensor, n2, qlow, klow, tgt, pkb, own_c, own_d, gains, shifts, zc, zd1, blob_d):
    def slot(t):
        return jnp.minimum(t, 3)

    def chunk(t):
        return jnp.maximum(t - 4, 0)

    def by_slot(*tail):
        return pl.BlockSpec((1,) + tail, lambda t: (slot(t),) + (0,) * len(tail))

    return pl.pallas_call(
        functools.partial(second_kernel, tensor),
        grid=(8,),
        in_specs=[
            held((1024, 512)), held((1024, 512)), held((1024, 512)), held((1, 1024)),
            held((1024, 128)), held((512, 512)), held((2, 512, 512)), held((5, 512)),
            held((5, 512)), ANY, ANY, ANY,
        ],
        out_specs=[
            by_slot(512, 512), by_slot(4, 1024, 512), by_slot(1024, 128), by_slot(1024, 128),
            by_slot(128, 1024), by_slot(128, 1024),
            pl.BlockSpec((1, 2, 512, 512), lambda t: (chunk(t), 0, 0, 0)),
            pl.BlockSpec((1024, 512), lambda t: (0, chunk(t))),
            kept((1024, 512)), kept((1024, 1)), kept((1024, 1)),
        ] + [ANY] * 4,
        out_shape=[
            SDS((4, 512, 512), bf16), SDS((4, 4, 1024, 512), bf16), SDS((4, 1024, 128), bf16),
            SDS((4, 1024, 128), bf16), SDS((4, 128, 1024), bf16), SDS((4, 128, 1024), bf16),
            SDS((4, 2, 512, 512), bf16), SDS((1024, 2048), bf16), SDS((1024, 512), bf16),
            SDS((1024, 1), f32), SDS((1024, 1), f32),
            SDS((1024, 512), f32), SDS((1024, 512), f32), SDS((1024, 512), bf16),
            SDS((1024, 512), bf16),
        ],
        scratch_shapes=[
            VM((3, 8, 64, 512), f32), VM((3, 8, 128, 512), f32), VM((1024, 512), f32),
            VM((1024, 512), f32), VM((1024, 512), bf16), VM((1024, 512), bf16),
            VM((1024, 128), bf16), VM((128, 1024), bf16), VM((128, 1024), bf16),
            pltpu.SemaphoreType.DMA((6, 9)), pltpu.SemaphoreType.DMA((6, 9)),
            pltpu.SemaphoreType.DMA((8,)),
        ],
        compiler_params=pltpu.CompilerParams(
            collective_id=2, has_side_effects=True, vmem_limit_bytes=VMEM_MB * MB
        ),
    )(n2, qlow, klow, tgt, pkb, own_c, own_d, gains, shifts, zc, zd1, blob_d)


def column(row):
    return jnp.broadcast_to(row, (128, row.shape[1])).T


def prep_kernel(x_e, x_d, masked, embed, src, tgt, qkv_e, wo_e, qkv_s, wo_s, qkv_c, wo_c,
                w1_e, w2_e, w1_d, w2_d, lows, tlow, target, idx, pkb, mcol, own_es, own_c, own_f, own_d,
                blob_e, blob_s, blob_c, blob_f, blob_d, win):
    _, j = plane_index()
    head = pl.multiple_of(lax.rem(j, 2) * 64 + lax.div(j, 2) * 16, 16)
    unit = pl.multiple_of(j * 64, 64)
    for qkv, wo, own, blob in (
        (qkv_e, wo_e, own_es.at[0], blob_e),
        (qkv_s, wo_s, own_es.at[1], blob_s),
        (qkv_c, wo_c, own_c, blob_c),
    ):
        for m in range(3):
            own[m * 128 : (m + 1) * 128] = qkv[m].T
        own[384:] = wo[...]
        for m in range(4):
            piece = own[pl.ds(m * 128 + head, 16)]
            blob[m * 16 : (m + 1) * 16] = piece.astype(f32)
    for w1, w2, own, blob in ((w1_e, w2_e, own_f, blob_f), (w1_d, w2_d, own_d, blob_d)):
        own[0] = w1[...].T
        own[1] = w2[...]
        for m in range(2):
            blob[m * 64 : (m + 1) * 64] = own[m, pl.ds(unit, 64)].astype(f32)
    src_col, tgt_col = column(src[...]), column(tgt[...])
    pkb[0] = src_col
    pkb[1] = tgt_col
    idx[0] = src[...]
    idx[1] = tgt[...]
    m = column(masked[...])
    mcol[...] = m
    m4 = jnp.concatenate([m] * 4, axis=1)
    tv = jnp.where(m4 == 1, embed[...], x_d[...].astype(f32))
    target[...] = tv
    lows[0] = x_e[...]
    lows[1] = tv.astype(bf16)
    tlow[...] = tv.astype(bf16)
    s = src[...]
    for b in range(4):
        cut = tgt[:, b * BLK : (b + 1) * BLK]
        lo, hi = jnp.min(cut), jnp.max(cut)
        begin = jnp.sum((s < lo).astype(jnp.int32))
        end = jnp.sum((s <= hi).astype(jnp.int32))
        start = jnp.minimum(lax.div(begin, 128) * 128, 512)
        win[b] = start
        win[4 + b] = (end - start > 512).astype(jnp.int32)


def call_prep(*args):
    full = pl.BlockSpec(memory_space=pltpu.VMEM)
    return pl.pallas_call(
        prep_kernel,
        in_specs=[full] * len(args),
        out_specs=[full] * 15 + [SMEM_SPEC],
        out_shape=[
            SDS((2, 1024, 512), bf16), SDS((1024, 512), bf16), SDS((1024, 512), f32),
            SDS((2, 1, 1024), jnp.int32),
            SDS((2, 1024, 128), jnp.int32), SDS((1024, 128), jnp.int32),
            SDS((2, 512, 512), bf16), SDS((512, 512), bf16), SDS((2, 512, 512), bf16),
            SDS((2, 512, 512), bf16), SDS((64, 512), f32), SDS((64, 512), f32),
            SDS((64, 512), f32), SDS((128, 512), f32), SDS((128, 512), f32),
            SDS((8,), jnp.int32),
        ],
        compiler_params=pltpu.CompilerParams(vmem_limit_bytes=VMEM_MB * MB),
    )(*args)


def norm_back_all(dy, n, r, gain, gs_o, d_s, g_s):
    gs_o[...] = jnp.zeros_like(gs_o)
    for b in range(4):
        rows = rows_at(b)
        dyv, nv = dy(rows), n[rows]
        gs_o[0:1] += jnp.sum(dyv * nv, axis=0, keepdims=True)
        gs_o[1:2] += jnp.sum(dyv, axis=0, keepdims=True)
        d = layer_norm_back(dyv, nv, r[rows], gain)
        d_s[rows] = d
        g_s[rows] = d.astype(bf16)


def attend_bwd(cross, layer, *refs):
    (win, dy, n, r, gains, w, pt, v, kt, q, ot, alow, blow) = refs[:13]
    refs = refs[13:]
    if cross:
        acc, dkey, dqkv_o, dwo_o, gs_o, g_s, do_s, dot_s, dk_s, dv_s, dqt_s = refs
    else:
        acc, dqkv_o, dwo_o, gs_o, g_s, do_s, dot_s, dk_s, dv_s, dqt_s = refs
    p = pl.program_id(0)

    @pl.when(p == 0)
    def _():
        norm_back_all(lambda rows: dy[rows], n, r, gains[layer : layer + 1], gs_o, acc, g_s)
        if cross:
            dkey[...] = jnp.zeros_like(dkey)

    for b in range(4):
        rows = rows_at(b)
        do_s[rows] = nt(g_s[rows], w[0, 384:]).astype(bf16)
        dot_s[:, rows] = nt(w[0, 384:], g_s[rows]).astype(bf16)
    dk_s[...] = jnp.zeros_like(dk_s)
    dv_s[...] = jnp.zeros_like(dv_s)

    def block(b, start, width):
        rows = rows_at(b)
        keys = pl.ds(start, width)
        prow = keys if cross else slice(None)
        prod = dot_s[:, rows].astype(f32) * ot[0, :, rows].astype(f32)
        delta = jnp.concatenate(
            [jnp.sum(prod[:64], axis=0, keepdims=True), jnp.sum(prod[64:], axis=0, keepdims=True)],
            axis=1,
        )
        dpt = nn(v[0, keys], block_diag(dot_s[:64, rows], dot_s[64:, rows]))
        ptv = pt[0, b, prow]
        dst = (ptv.astype(f32) * (dpt - delta)).astype(bf16)
        dv_s[keys] += nn(ptv, two_heads(do_s[rows]))
        dk_s[keys] += nn(dst, two_heads(q[0, rows]))
        dqt_s[:64, rows] = (nn(kt[0, :64, keys], dst[:, :BLK]) * 0.125).astype(bf16)
        dqt_s[64:, rows] = (nn(kt[0, 64:, keys], dst[:, BLK:]) * 0.125).astype(bf16)

    for b in range(4):
        if cross:
            start = pl.multiple_of(win[b], 128)
            pl.when(win[4 + b] == 0)(lambda b=b, start=start: block(b, start, 512))
            pl.when(win[4 + b] != 0)(lambda b=b: block(b, 0, 1024))
        else:
            block(b, self_start(b), 512)
    for b in range(4):
        rows = rows_at(b)
        dkb, dvb = dk_s[rows].astype(bf16), dv_s[rows].astype(bf16)
        kv = jnp.concatenate([dkb, dvb], axis=1)
        acc[rows] += tn(dqt_s[:, rows], w[0, :128])
        if cross:
            dkey[rows] += nn(kv, w[0, 128:384])
        else:
            acc[rows] += nn(kv, w[0, 128:384])

    @pl.when(p == 0)
    def _():
        dqkv_o[0] = nn(dqt_s[...], alow[...]).T
        dqkv_o[1] = tn(dk_s[...].astype(bf16), blow[...]).T
        dqkv_o[2] = tn(dv_s[...].astype(bf16), blow[...]).T
        dwo_o[...] = nn(ot[0], g_s[...])


def call_attend_bwd(cross, layer, first, win, dy, n, r, gains, saved, alow, blow):
    w, pt, q, v, kt, ot = saved
    width = 1024 if cross else 512

    def by_slot(*tail):
        return pl.BlockSpec((1,) + tail, lambda t: (first + t,) + (0,) * len(tail))

    grads = [SDS((1024, 512), f32)] * (2 if cross else 1)
    return pl.pallas_call(
        functools.partial(attend_bwd, cross, layer),
        grid=(4,),
        in_specs=[
            SMEM_SPEC, held((1024, 512)), held((1024, 512)), held((1024, 1)), held((5, 512)),
            by_slot(512, 512), by_slot(4, width, 512), by_slot(1024, 128), by_slot(128, 1024),
            by_slot(1024, 128), by_slot(128, 1024), held((1024, 512)), held((1024, 512)),
        ],
        out_specs=[kept((1024, 512))] * len(grads)
        + [kept((3, 512, 128)), kept((128, 512)), kept((8, 512))],
        out_shape=grads + [SDS((3, 512, 128), f32), SDS((128, 512), f32), SDS((8, 512), f32)],
        scratch_shapes=[
            VM((1024, 512), bf16), VM((1024, 128), bf16), VM((128, 1024), bf16),
            VM((1024, 128), f32), VM((1024, 128), f32), VM((128, 1024), bf16),
        ],
        compiler_params=pltpu.CompilerParams(vmem_limit_bytes=VMEM_MB * MB),
    )(win, dy, n, r, gains, w, pt, v, kt, q, ot, alow, blow)


def ffn_bwd(count, layer, *refs):
    dys = refs[:count]
    (n, r, gains, alow, w, h, slope, acc, dw1_o, dw2_o, gs_o, g_s, db_s) = refs[count:]
    c = pl.program_id(0)

    @pl.when(c == 0)
    def _():
        def dy(rows):
            total = dys[0][rows].astype(f32)
            return total + dys[1][rows] if count == 2 else total

        norm_back_all(dy, n, r, gains[layer : layer + 1], gs_o, acc, g_s)

    for b in range(4):
        rows = rows_at(b)
        db = (nt(g_s[rows], w[0, 1]) * slope[rows].astype(f32)).astype(bf16)
        db_s[rows] = db
        acc[rows] += nn(db, w[0, 0])

    @pl.when(c == 0)
    def _():
        dw1_o[...] = tn(alow[...], db_s[...])
        dw2_o[...] = tn(h[...], g_s[...])


def call_ffn_bwd(dys, layer, n, r, gains, alow, w, h, slope):
    return pl.pallas_call(
        functools.partial(ffn_bwd, len(dys), layer),
        grid=(4,),
        in_specs=[held((1024, 512))] * len(dys)
        + [
            held((1024, 512)), held((1024, 1)), held((5, 512)), held((1024, 512)),
            pl.BlockSpec((1, 2, 512, 512), lambda t: (t, 0, 0, 0)), held((1024, 512)),
            pl.BlockSpec((1024, 512), lambda t: (0, t)),
        ],
        out_specs=[kept((1024, 512)), kept((512, 512)), kept((512, 512)), kept((8, 512))],
        out_shape=[
            SDS((1024, 512), f32), SDS((512, 512), f32), SDS((512, 512), f32), SDS((8, 512), f32),
        ],
        scratch_shapes=[VM((1024, 512), bf16), VM((1024, 512), bf16)],
        compiler_params=pltpu.CompilerParams(vmem_limit_bytes=VMEM_MB * MB),
    )(*dys, n, r, gains, alow, w, h, slope)


def sum_kernel(count, *refs):
    part, out = refs[:count], refs[count : 2 * count]
    got_c, got_a, got_b, got_a2, got_b2, held = (
        refs[2 * count + k * count : 2 * count + (k + 1) * count] for k in range(6)
    )
    ss, rs = refs[8 * count :]
    dp, j = plane_index()
    z = lax.axis_index("tensor")
    c, x, y = lax.rem(j, 2), lax.rem(lax.div(j, 2), 2), lax.div(j, 4)
    cn, xn, yn = (dp + 1 - 2 * c, z), (dp + 2 - 4 * x, z), (dp + 4 - 8 * y, z)
    barrier_with([cn, xn, yn])

    def copy(k, s, src, dst, dev):
        return pltpu.make_async_remote_copy(
            src_ref=src, dst_ref=dst, send_sem=ss.at[k, s], recv_sem=rs.at[k, s],
            device_id=dev, device_id_type=MESH,
        )

    every = []

    def go(cp):
        cp.start()
        every.append(cp)
        return cp

    halves = []
    for k in range(count):
        h = part[k].shape[3] // 2
        halves.append((pl.ds(0, h), pl.ds(h, h)))
    s0 = [go(copy(k, 0, part[k].at[:, :, 1 - c], got_c[k], cn)) for k in range(count)]
    s1 = []
    for k in range(count):
        a, b = halves[k]
        s0[k].wait_recv()
        held[k][...] = part[k][:, :, c] + got_c[k][...]
        s1.append((
            go(copy(k, 1, held[k].at[:, 1 - x, a], got_a[k], xn)),
            go(copy(k, 2, held[k].at[1 - y, :, b], got_b[k], yn)),
        ))
    s2 = []
    for k in range(count):
        a, b = halves[k]
        s1[k][0].wait_recv()
        held[k][:, x, a] += got_a[k][...]
        s1[k][1].wait_recv()
        held[k][y, :, b] += got_b[k][...]
        s2.append((
            go(copy(k, 3, held[k].at[1 - y, x, a], got_a2[k], yn)),
            go(copy(k, 4, held[k].at[y, 1 - x, b], got_b2[k], xn)),
        ))
    s3 = []
    for k in range(count):
        a, b = halves[k]
        o = out[k]
        s2[k][0].wait_recv()
        o[y, x, c, a] = held[k][y, x, a] + got_a2[k][...]
        s2[k][1].wait_recv()
        o[y, x, c, b] = held[k][y, x, b] + got_b2[k][...]
        s3.append((
            go(copy(k, 5, o.at[y, x, c, a], o.at[y, x, c, a], yn)),
            go(copy(k, 6, o.at[y, x, c, b], o.at[y, x, c, b], xn)),
        ))
    s4 = []
    for k in range(count):
        a, b = halves[k]
        o = out[k]
        s3[k][0].wait_recv()
        s3[k][1].wait_recv()
        s4.append((
            go(copy(k, 7, o.at[:, x, c, a], o.at[:, x, c, a], xn)),
            go(copy(k, 8, o.at[y, :, c, b], o.at[y, :, c, b], yn)),
        ))
    s5 = []
    for k in range(count):
        o = out[k]
        s4[k][0].wait_recv()
        s4[k][1].wait_recv()
        s5.append(go(copy(k, 9, o.at[:, :, c], o.at[:, :, c], cn)))
    for k in range(count):
        s5[k].wait_recv()
    for cp in every:
        cp.wait_send()


def sum_over_plane(parts):
    count = len(parts)
    shapes = [p.shape[3:] for p in parts]

    def bufs(lead, cut):
        return [VM(lead + (r // cut, w), f32) for r, w in shapes]

    return pl.pallas_call(
        functools.partial(sum_kernel, count),
        in_specs=[pl.BlockSpec(memory_space=pltpu.VMEM)] * count,
        out_specs=[pl.BlockSpec(memory_space=pltpu.VMEM)] * count,
        out_shape=[SDS(p.shape, f32) for p in parts],
        scratch_shapes=bufs((2, 2), 1) + bufs((2,), 2) + bufs((2,), 2) + bufs((), 2) + bufs((), 2)
        + bufs((2, 2), 1)
        + [pltpu.SemaphoreType.DMA((count, 10)), pltpu.SemaphoreType.DMA((count, 10))],
        compiler_params=pltpu.CompilerParams(
            collective_id=1, has_side_effects=True, vmem_limit_bytes=60 * MB
        ),
    )(*parts)


def per_device(planes, tensor, enc_in, dec_in, src_idx, tgt_idx, masked, mask_embed, enc_qkv,
               enc_out_w, enc_w1, enc_w2, self_qkv, self_out_w, cross_qkv, cross_out_w, dec_w1,
               dec_w2, gains, shifts, enc_cot, dec_cot):
    (lows, target_low, target, idx, pkb, mcol, own_es, own_c, own_f, own_d, blob_e, blob_s, blob_c, blob_f,
     blob_d, win) = call_prep(
        enc_in[0], dec_in[0], masked, mask_embed[None], src_idx, tgt_idx, enc_qkv, enc_out_w,
        self_qkv, self_out_w, cross_qkv, cross_out_w, enc_w1, enc_w2, dec_w1, dec_w2)
    (w_es, pt_es, q_es, v_es, kt_es, ot_es, w_f, slope_e, h_e, r0, r2, r1, n0, n2, n1, first_low,
     second_low, enc_low, zc, zd1) = call_first(
        tensor, lows, target, idx, pkb, own_es, own_f, gains, shifts,
        (blob_e, blob_s, blob_f, blob_c, blob_d))
    (w_c, pt_c, q_c, v_c, kt_c, ot_c, w_d, slope_d, h_d, r3, r4, n3, n4, third_low,
     dec_low) = call_second(
        tensor, n2, second_low, enc_low, tgt_idx, pkb[0], own_c, own_d, gains, shifts, zc, zd1,
        blob_d)
    save_es = (w_es, pt_es, q_es, v_es, kt_es, ot_es)
    save_c = (w_c, pt_c, q_c, v_c, kt_c, ot_c)

    d_third, dw1_d, dw2_d, gs4 = call_ffn_bwd(
        [dec_cot[0]], 4, n4, r4, gains, third_low, w_d, h_d, slope_d)
    d_second, d_key, dqkv_c, dwo_c, gs3 = call_attend_bwd(
        True, 3, 0, win, d_third, n3, r3, gains, save_c, second_low, enc_low)
    d_target, dqkv_s, dwo_s, gs2 = call_attend_bwd(
        False, 2, 4, win, d_second, n2, r2, gains, save_es, target_low, target_low)
    d_first, dw1_e, dw2_e, gs1 = call_ffn_bwd(
        [enc_cot[0], d_key], 1, n1, r1, gains, first_low, w_f, h_e, slope_e)
    d_enc, dqkv_e, dwo_e, gs0 = call_attend_bwd(
        False, 0, 0, win, d_first, n0, r0, gains, save_es, enc_in[0], enc_in[0])

    is_masked = mcol[:, :1] == 1
    dec_grad = jnp.where(is_masked, 0.0, d_target)
    mask_grad = jnp.sum(jnp.where(is_masked, d_target, 0.0), axis=0)
    small = jnp.concatenate([mask_grad[None]] + [a[:2] for a in (gs0, gs1, gs2, gs3, gs4)])
    small = jnp.pad(small, ((0, 21), (0, 0))).reshape(2, 2, 2, 16, 128)

    def chunks(a):
        return a.reshape(2, 2, 2, a.size // 8 // a.shape[-1], a.shape[-1])

    mats = [dqkv_e, dwo_e, dw1_e, dw2_e, dqkv_s, dwo_s, dqkv_c, dwo_c, dw1_d, dw2_d]
    sums = sum_over_plane([chunks(a) for a in mats] + [small])
    if planes > 1:
        same = [[p * 8 + k for p in range(planes)] for k in range(8)]
        sums = lax.psum(sums, "dp", axis_index_groups=same)
    small = sums[-1].reshape(32, 512)
    return (
        enc_low[None],
        dec_low[None],
        d_enc[None],
        dec_grad[None],
        small[0],
        *[a.reshape(m.shape) for a, m in zip(sums, mats)],
        small[1:11:2],
        small[2:12:2],
    )


def solution(mesh):
    tokens, index = P("dp", None, None), P("dp", None)
    qkv, cols, rows = P(None, None, "tensor"), P(None, "tensor"), P("tensor", None)
    weights = (qkv, rows, cols, rows, qkv, rows, qkv, rows, cols, rows)
    return jax.shard_map(
        functools.partial(per_device, mesh.shape["dp"] // 8, mesh.shape["tensor"]),
        mesh=mesh,
        in_specs=(tokens, tokens, index, index, index, P()) + weights + (P(), P(), tokens, tokens),
        out_specs=(tokens,) * 4 + (P(),) + weights + (P(), P()),
        check_vma=False,
    )
```

```python
import functools

import jax
import jax.numpy as jnp
from jax import lax
from jax.experimental import pallas as pl
from jax.experimental.pallas import tpu as pltpu
from jax.sharding import PartitionSpec as P

f32, bf16 = jnp.float32, jnp.bfloat16
HEAD_DIM = 64
EPS = 1e-05
FLOOR = -1000000000.0
BLK = 256
MB = 1 << 20
VMEM_MB = 60
MESH = pl.DeviceIdType.MESH
VM = pltpu.VMEM


def nt(a, b):
    return lax.dot_general(a, b, (((1,), (1,)), ((), ())), preferred_element_type=f32)


def nn(a, b):
    return lax.dot_general(a, b, (((1,), (0,)), ((), ())), preferred_element_type=f32)


def tn(a, b):
    return lax.dot_general(a, b, (((0,), (0,)), ((), ())), preferred_element_type=f32)


def layer_norm(v):
    c = v - jnp.mean(v, axis=-1, keepdims=True)
    r = lax.rsqrt(jnp.mean(c * c, axis=-1, keepdims=True) + EPS)
    return c * r, r


def layer_norm_back(dy, n, r, gain):
    dn = dy * gain
    m1 = jnp.mean(dn, axis=-1, keepdims=True)
    m2 = jnp.mean(dn * n, axis=-1, keepdims=True)
    return r * (dn - m1 - n * m2)


def block_diag(a, b):
    z = jnp.zeros_like(a)
    return jnp.concatenate(
        [jnp.concatenate([a, z], axis=1), jnp.concatenate([z, b], axis=1)], axis=0
    )


def two_heads(x):
    lane = lax.broadcasted_iota(jnp.int32, x.shape, 1)
    z = jnp.zeros_like(x)
    return jnp.concatenate([jnp.where(lane < HEAD_DIM, x, z), jnp.where(lane < HEAD_DIM, z, x)], 0)


def rows_at(b):
    return slice(b * BLK, (b + 1) * BLK)


def self_start(b):
    return min(max(b * BLK - 128, 0), 512)


def project_slot(w, kinds, get, rows_out):
    for b in range(4):
        xb = get(b)
        nat = nt(xb, w[kinds[0] * 128 : kinds[-1] * 128 + 128])
        tr = nt(w[kinds[0] * 128 : kinds[-1] * 128 + 128], xb)
        for k, kind in enumerate(kinds):
            cut = slice(k * 128, k * 128 + 128)
            for dst, val in rows_out(kind, b, nat[:, cut], tr[cut]):
                dst[...] = val.astype(bf16)


def softmax_block(k_s, qt, keys, pk, pq):
    bias = jnp.where(pk == pq, 0.0, FLOOR).astype(f32)
    s = nn(k_s[keys], block_diag(qt[:64], qt[64:])) + jnp.concatenate([bias, bias], axis=1)
    e = jnp.exp(s - jnp.max(s, axis=0, keepdims=True))
    return (e * (1.0 / jnp.sum(e, axis=0, keepdims=True))).astype(bf16)


def mix_block(vt_s, keys, pt):
    return jnp.concatenate([nn(vt_s[:64, keys], pt[:, :BLK]), nn(vt_s[64:, keys], pt[:, BLK:])], 0)


def wide(pkb):
    return jnp.concatenate([pkb, pkb], axis=1)


def ffn_slot(w, al, acc, slope_o, h_o, first, tick):
    for b in range(4):
        rows = rows_at(b)
        before = nt(al[rows], w[0])
        cdf = 0.5 + 0.5 * lax.erf(before * (0.5**0.5))
        pdf = jnp.exp(before * before * -0.5) * 0.3989422804014327
        slope_o[rows] = (cdf + before * pdf).astype(bf16)
        hidden = (before * cdf).astype(bf16)

        @pl.when(first)
        def _():
            h_o[rows] = hidden

        acc[rows] += nn(hidden, w[1])
        tick(b)


def finish_norm(acc, gain, shift, n_ref, r_o, y_ref):
    for b in range(4):
        rows = rows_at(b)
        n, r = layer_norm(acc[rows])
        n_ref[rows] = n
        r_o[rows] = r
        y_ref[rows] = (n * gain + shift).astype(bf16)


def plane_index():
    dp = lax.axis_index("dp")
    return dp, lax.rem(dp, 8)


def neighbours(tensor):
    dp, j = plane_index()
    z = lax.axis_index("tensor")
    c, x, y = lax.rem(j, 2), lax.rem(lax.div(j, 2), 2), lax.div(j, 4)
    core, xn, yn = (dp + 1 - 2 * c, z), (dp + 2 - 4 * x, z), (dp + 4 - 8 * y, z)
    down = {k: (dp, lax.rem(z + tensor - k, tensor)) for k in range(1, tensor)}
    return (c, x, y), core, xn, yn, down


def barrier_with(peers):
    sem = pltpu.get_barrier_semaphore()
    for peer in peers:
        pl.semaphore_signal(sem, inc=1, device_id=peer, device_id_type=MESH)
    pl.semaphore_wait(sem, len(peers))


class Gather:
    def __init__(self, items, ss, rs, tensor):
        self.items, self.ss, self.rs = items, ss, rs
        _, self.core, self.xn, self.yn, self.down = neighbours(tensor)

    def barrier(self):
        barrier_with([self.core, self.xn, self.yn] + list(self.down.values()))

    def copy(self, t, s, src, dst, dev):
        return lambda: pltpu.make_async_remote_copy(
            src_ref=src, dst_ref=dst, send_sem=self.ss.at[t, s], recv_sem=self.rs.at[t, s],
            device_id=dev, device_id_type=MESH,
        )

    def make(self, t):
        slot, src, land, spread = self.items[t]
        if not spread:
            return [self.copy(t, 0, src, land, self.down[slot])]
        half = land.shape[1] // 2
        a, b = pl.ds(0, half), pl.ds(half, half)
        return [
            self.copy(t, 0, src, land.at[0], self.down[slot]) if src is not None else None,
            self.copy(t, 1, land.at[0], land.at[1], self.xn),
            self.copy(t, 2, land.at[0], land.at[2], self.yn),
            self.copy(t, 3, land.at[0], land.at[4], self.core),
            self.copy(t, 4, land.at[1, a], land.at[3, a], self.yn),
            self.copy(t, 5, land.at[1], land.at[5], self.core),
            self.copy(t, 6, land.at[2, b], land.at[3, b], self.xn),
            self.copy(t, 7, land.at[2], land.at[6], self.core),
            self.copy(t, 8, land.at[3], land.at[7], self.core),
        ]

    def send(self, t):
        self.make(t)[0]().start()

    def spread(self, t):
        c = self.make(t)
        if c[0] is not None:
            c[0]().wait_recv()
        for k in (1, 2, 3):
            c[k]().start()

    def relay(self, t):
        c = self.make(t)
        c[1]().wait_recv()
        c[4]().start()
        c[5]().start()
        c[2]().wait_recv()
        c[6]().start()
        c[7]().start()

    def pair(self, t):
        c = self.make(t)
        c[4]().wait_recv()
        c[6]().wait_recv()
        c[8]().start()

    def advance(self, t, last):
        if t <= last:
            self.spread(t)
        if 0 <= t - 1 <= last:
            self.relay(t - 1)
        if 0 <= t - 2 <= last:
            self.pair(t - 2)

    def done(self, t):
        c = self.make(t)
        for k in (3, 5, 7, 8):
            c[k]().wait_recv()

    def finish(self):
        for t in range(len(self.items)):
            for c in self.make(t):
                if c is not None:
                    c().wait_send()
            if not self.items[t][3]:
                self.make(t)[0]().wait_recv()


def run_events(t, steps, events, point):
    for step in steps:
        acts = events.get((step, point))
        if acts:

            @pl.when(t == step)
            def _(acts=acts):
                for act in acts:
                    act()


def es_of(t):
    kind = jnp.where((t == 1) | (t >= 5), 1, 0)
    p = jnp.where(t < 2, 0, jnp.where(t < 5, t - 1, t - 4))
    return kind, jnp.minimum(p, 3)


def es_block(t):
    kind, p = es_of(t)
    return kind * 4 + p


def first_kernel(tensor, *refs):
    (lows, target, idx, pkb, own_es, own_f, gains, shifts) = refs[:8]
    blob_e, blob_s, blob_f, blob_c, blob_d = refs[8:13]
    (wes_o, pt_o, q_o, v_o, kt_o, ot_o, wf_o, slope_o, h_o, r0_o, r2_o, r1_o, n0_o, n2_o,
     n1_o, y0_o, y2_o, encl_o, zc_o, zd_o) = refs[13:33]
    (land_a, land_f, accs, na, ylow, encl, k_s, qt_s, vt_s, ss, rs, cs) = refs[33:]
    t = pl.program_id(0)
    items = [(k, blob_e, land_a.at[k - 1], True) for k in (1, 2, 3)]
    items += [(k, blob_s, land_a.at[2 + k], True) for k in (1, 2, 3)]
    items += [(k, blob_f, land_f.at[k - 1], True) for k in (1, 2, 3)]
    items += [(k, blob_c, zc_o.at[k - 1], False) for k in (1, 2, 3)]
    items += [(1, blob_d, zd_o, False)]
    net = Gather(items, ss, rs, tensor)
    outs = [
        (na.at[0], n0_o), (ylow.at[0], y0_o), (na.at[1], n2_o), (ylow.at[1], y2_o),
        (accs.at[0], n1_o), (encl, encl_o),
    ]

    def out(k):
        return pltpu.make_async_copy(*outs[k], cs.at[k])

    last = 8
    ev = {}

    def at(step, point, *acts):
        ev.setdefault((step, point), []).extend(acts)

    def adv(k):
        return lambda: net.advance(k, last)

    def send(*ks):
        return lambda: [net.send(k) for k in ks]

    def done(k):
        return lambda: net.done(k)

    at(0, -1, net.barrier, send(0, 1, 2))
    at(1, 3, adv(0), send(3, 4, 5), adv(1))
    at(2, -1, adv(2), done(0))
    at(2, 2, adv(3), send(6, 7, 8))
    at(3, -1, done(1))
    at(3, 2, adv(4))
    at(4, -1, done(2))
    at(4, 2, adv(5))
    at(5, -1, done(3))
    at(5, 2, adv(6), send(9, 10, 11))
    at(6, -1, done(4))
    at(6, 2, adv(7))
    at(7, -1, done(5))
    at(7, 2, adv(8))
    at(8, 0, adv(9), send(12))
    at(8, 3, adv(10))
    at(9, -1, done(6))
    at(10, -1, done(7))
    at(11, -1, done(8))
    kind, p = es_of(t)
    es_steps, f_steps = range(8), range(8, 12)

    @pl.when(t < 8)
    def _():
        run_events(t, es_steps, ev, -1)

        @pl.when(p == 0)
        def _():
            wes_o[0] = own_es[kind]

        @pl.when((p == 0) & (kind == 0))
        def _():
            accs[0] = lows[0].astype(f32)

        @pl.when((p == 0) & (kind == 1))
        def _():
            accs[1] = target[...]

        @pl.when(p > 0)
        def _():
            for m in range(4):
                piece = land_a[kind * 3 + p - 1, :, m * 16 : (m + 1) * 16, :]
                wes_o[0, m * 128 : (m + 1) * 128] = piece.reshape(128, 512).astype(bf16)

        w = wes_o.at[0]

        def outs_of(m, b, nat, tr):
            rows = rows_at(b)
            if m == 0:
                return [(q_o.at[0, rows], nat * 0.125), (qt_s.at[:, rows], tr * 0.125)]
            if m == 1:
                return [(k_s.at[rows], nat), (kt_o.at[0, :, rows], tr)]
            return [(v_o.at[0, rows], nat), (vt_s.at[:, rows], tr)]

        project_slot(w, (0, 1, 2), lambda b: lows[kind, rows_at(b)], outs_of)
        for b in range(4):
            rows = rows_at(b)
            keys = slice(self_start(b), self_start(b) + 512)
            pt = softmax_block(k_s, qt_s[:, rows], keys, wide(pkb[kind, keys]), idx[kind, :, rows])
            pt_o[0, b] = pt
            ot = mix_block(vt_s, keys, pt).astype(bf16)
            ot_o[0, :, rows] = ot
            accs[kind, rows] += tn(ot, w[384:])
            run_events(t, es_steps, ev, b)

        @pl.when(t == 4)
        def _():
            finish_norm(accs.at[0], gains[0:1], shifts[0:1], na.at[0], r0_o, ylow.at[0])
            out(0).start()
            out(1).start()

        @pl.when(t == 7)
        def _():
            finish_norm(accs.at[1], gains[2:3], shifts[2:3], na.at[1], r2_o, ylow.at[1])
            out(2).start()
            out(3).start()

    @pl.when(t >= 8)
    def _():
        run_events(t, f_steps, ev, -1)

        @pl.when(t == 8)
        def _():
            wf_o[0] = own_f[...]
            accs[0] = na[0] * gains[0:1] + shifts[0:1]

        @pl.when(t > 8)
        def _():
            for m in range(2):
                piece = land_f[t - 9, :, m * 64 : (m + 1) * 64, :]
                wf_o[0, m] = piece.reshape(512, 512).astype(bf16)

        ffn_slot(wf_o.at[0], ylow.at[0], accs.at[0], slope_o, h_o, t == 8,
                 lambda b: run_events(t, f_steps, ev, b))

        @pl.when(t == 11)
        def _():
            finish_norm(accs.at[0], gains[1:2], shifts[1:2], accs.at[0], r1_o, encl)
            out(4).start()
            out(5).start()
            for k in range(6):
                out(k).wait()
            net.finish()


def held(shape):
    return pl.BlockSpec(shape, lambda t: (0,) * len(shape), pipeline_mode=pl.Buffered(1))


def kept(shape):
    return pl.BlockSpec(shape, lambda t: (0,) * len(shape))


ANY = pl.BlockSpec(memory_space=pl.ANY)
SMEM_SPEC = pl.BlockSpec(memory_space=pltpu.SMEM)
SDS = jax.ShapeDtypeStruct


def by_es(*tail):
    return pl.BlockSpec((1,) + tail, lambda t: (es_block(t),) + (0,) * len(tail))


def call_first(tensor, lows, target, idx, pkb, own_es, own_f, gains, shifts, blobs):
    def chunk(t):
        return jnp.maximum(t - 8, 0)

    n_items = 13
    return pl.pallas_call(
        functools.partial(first_kernel, tensor),
        grid=(12,),
        in_specs=[
            held((2, 1024, 512)), held((1024, 512)), held((2, 1, 1024)), held((2, 1024, 128)),
            held((2, 512, 512)), held((2, 512, 512)), held((5, 512)), held((5, 512)),
        ] + [ANY] * 5,
        out_specs=[
            by_es(512, 512), by_es(4, 512, 512), by_es(1024, 128), by_es(1024, 128),
            by_es(128, 1024), by_es(128, 1024),
            pl.BlockSpec((1, 2, 512, 512), lambda t: (chunk(t), 0, 0, 0)),
            pl.BlockSpec((1024, 512), lambda t: (0, chunk(t))),
            kept((1024, 512)), kept((1024, 1)), kept((1024, 1)), kept((1024, 1)),
        ] + [ANY] * 8,
        out_shape=[
            SDS((8, 512, 512), bf16), SDS((8, 4, 512, 512), bf16), SDS((8, 1024, 128), bf16),
            SDS((8, 1024, 128), bf16), SDS((8, 128, 1024), bf16), SDS((8, 128, 1024), bf16),
            SDS((4, 2, 512, 512), bf16), SDS((1024, 2048), bf16), SDS((1024, 512), bf16),
            SDS((1024, 1), f32), SDS((1024, 1), f32), SDS((1024, 1), f32),
            SDS((1024, 512), f32), SDS((1024, 512), f32), SDS((1024, 512), f32),
            SDS((1024, 512), bf16), SDS((1024, 512), bf16), SDS((1024, 512), bf16), SDS((3, 64, 512), f32), SDS((128, 512), f32),
        ],
        scratch_shapes=[
            VM((6, 8, 64, 512), f32), VM((3, 8, 128, 512), f32), VM((2, 1024, 512), f32),
            VM((2, 1024, 512), f32), VM((2, 1024, 512), bf16), VM((1024, 512), bf16),
            VM((1024, 128), bf16), VM((128, 1024), bf16), VM((128, 1024), bf16),
            pltpu.SemaphoreType.DMA((n_items, 9)), pltpu.SemaphoreType.DMA((n_items, 9)),
            pltpu.SemaphoreType.DMA((6,)),
        ],
        compiler_params=pltpu.CompilerParams(
            collective_id=0, has_side_effects=True, vmem_limit_bytes=VMEM_MB * MB
        ),
    )(lows, target, idx, pkb, own_es, own_f, gains, shifts, *blobs)


def second_kernel(tensor, *refs):
    (n2, qlow, klow, tgt, pkb, own_c, own_d, gains, shifts) = refs[:9]
    zc, zd1, blob_d = refs[9:12]
    (wc_o, pt_o, q_o, v_o, kt_o, ot_o, wd_o, slope_o, h_o, r3_o, r4_o, n3_o, n4_o, y3_o,
     dec_o) = refs[12:27]
    (land_c, land_d, acc, n3, ylow, decl, k_s, qt_s, vt_s, ss, rs, cs) = refs[27:]
    t = pl.program_id(0)
    items = [(k, None, land_c.at[k - 1], True) for k in (1, 2, 3)]
    items += [(1, None, land_d.at[0], True)]
    items += [(k, blob_d, land_d.at[k - 1], True) for k in (2, 3)]
    net = Gather(items, ss, rs, tensor)
    moves = [(zc.at[k], land_c.at[k, 0]) for k in range(3)] + [(zd1, land_d.at[0, 0])]
    moves += [(n3, n3_o), (ylow, y3_o), (acc, n4_o), (decl, dec_o)]

    def move(k):
        return pltpu.make_async_copy(*moves[k], cs.at[k])

    last = 5
    ev = {}

    def at(step, point, *acts):
        ev.setdefault((step, point), []).extend(acts)

    def adv(k):
        return lambda: net.advance(k, last)

    def done(k):
        return lambda: net.done(k)

    def begin():
        for k in range(4):
            move(k).start()
        net.barrier()
        net.send(4)
        for k in range(4):
            move(k).wait()

    at(0, -1, begin, adv(0))
    at(0, 1, adv(1))
    at(0, 3, adv(2))
    at(1, -1, done(0))
    at(1, 0, adv(3), lambda: net.send(5))
    at(2, -1, done(1))
    at(2, 0, adv(4))
    at(3, -1, done(2))
    at(3, 0, adv(5))
    at(3, 3, adv(6))
    at(4, 3, adv(7))
    at(5, -1, done(3))
    at(6, -1, done(4))
    at(7, -1, done(5))
    c_steps, d_steps = range(4), range(4, 8)

    @pl.when(t < 4)
    def _():
        run_events(t, c_steps, ev, -1)

        @pl.when(t == 0)
        def _():
            wc_o[0] = own_c[...]
            acc[...] = n2[...] * gains[2:3] + shifts[2:3]

        @pl.when(t > 0)
        def _():
            for m in range(4):
                piece = land_c[t - 1, :, m * 16 : (m + 1) * 16, :]
                wc_o[0, m * 128 : (m + 1) * 128] = piece.reshape(128, 512).astype(bf16)

        w = wc_o.at[0]

        def outs_of(m, b, nat, tr):
            rows = rows_at(b)
            if m == 0:
                return [(q_o.at[0, rows], nat * 0.125), (qt_s.at[:, rows], tr * 0.125)]
            if m == 1:
                return [(k_s.at[rows], nat), (kt_o.at[0, :, rows], tr)]
            return [(v_o.at[0, rows], nat), (vt_s.at[:, rows], tr)]

        project_slot(w, (0,), lambda b: qlow[rows_at(b)], outs_of)
        project_slot(w, (1, 2), lambda b: klow[rows_at(b)], outs_of)
        for b in range(4):
            rows = rows_at(b)
            keys = slice(0, 1024)
            pt = softmax_block(k_s, qt_s[:, rows], keys, wide(pkb[...]), tgt[:, rows])
            pt_o[0, b] = pt
            ot = mix_block(vt_s, keys, pt).astype(bf16)
            ot_o[0, :, rows] = ot
            acc[rows] += tn(ot, w[384:])
            run_events(t, c_steps, ev, b)

        @pl.when(t == 3)
        def _():
            finish_norm(acc, gains[3:4], shifts[3:4], n3, r3_o, ylow)
            move(4).start()
            move(5).start()

    @pl.when(t >= 4)
    def _():
        run_events(t, d_steps, ev, -1)

        @pl.when(t == 4)
        def _():
            wd_o[0] = own_d[...]
            acc[...] = n3[...] * gains[3:4] + shifts[3:4]

        @pl.when(t > 4)
        def _():
            for m in range(2):
                piece = land_d[t - 5, :, m * 64 : (m + 1) * 64, :]
                wd_o[0, m] = piece.reshape(512, 512).astype(bf16)

        ffn_slot(wd_o.at[0], ylow, acc, slope_o, h_o, t == 4,
                 lambda b: run_events(t, d_steps, ev, b))

        @pl.when(t == 7)
        def _():
            finish_norm(acc, gains[4:5], shifts[4:5], acc, r4_o, decl)
            move(6).start()
            move(7).start()
            for k in range(4, 8):
                move(k).wait()
            net.finish()


def call_second(tensor, n2, qlow, klow, tgt, pkb, own_c, own_d, gains, shifts, zc, zd1, blob_d):
    def slot(t):
        return jnp.minimum(t, 3)

    def chunk(t):
        return jnp.maximum(t - 4, 0)

    def by_slot(*tail):
        return pl.BlockSpec((1,) + tail, lambda t: (slot(t),) + (0,) * len(tail))

    return pl.pallas_call(
        functools.partial(second_kernel, tensor),
        grid=(8,),
        in_specs=[
            held((1024, 512)), held((1024, 512)), held((1024, 512)), held((1, 1024)),
            held((1024, 128)), held((512, 512)), held((2, 512, 512)), held((5, 512)),
            held((5, 512)), ANY, ANY, ANY,
        ],
        out_specs=[
            by_slot(512, 512), by_slot(4, 1024, 512), by_slot(1024, 128), by_slot(1024, 128),
            by_slot(128, 1024), by_slot(128, 1024),
            pl.BlockSpec((1, 2, 512, 512), lambda t: (chunk(t), 0, 0, 0)),
            pl.BlockSpec((1024, 512), lambda t: (0, chunk(t))),
            kept((1024, 512)), kept((1024, 1)), kept((1024, 1)),
        ] + [ANY] * 4,
        out_shape=[
            SDS((4, 512, 512), bf16), SDS((4, 4, 1024, 512), bf16), SDS((4, 1024, 128), bf16),
            SDS((4, 1024, 128), bf16), SDS((4, 128, 1024), bf16), SDS((4, 128, 1024), bf16),
            SDS((4, 2, 512, 512), bf16), SDS((1024, 2048), bf16), SDS((1024, 512), bf16),
            SDS((1024, 1), f32), SDS((1024, 1), f32),
            SDS((1024, 512), f32), SDS((1024, 512), f32), SDS((1024, 512), bf16),
            SDS((1024, 512), bf16),
        ],
        scratch_shapes=[
            VM((3, 8, 64, 512), f32), VM((3, 8, 128, 512), f32), VM((1024, 512), f32),
            VM((1024, 512), f32), VM((1024, 512), bf16), VM((1024, 512), bf16),
            VM((1024, 128), bf16), VM((128, 1024), bf16), VM((128, 1024), bf16),
            pltpu.SemaphoreType.DMA((6, 9)), pltpu.SemaphoreType.DMA((6, 9)),
            pltpu.SemaphoreType.DMA((8,)),
        ],
        compiler_params=pltpu.CompilerParams(
            collective_id=2, has_side_effects=True, vmem_limit_bytes=VMEM_MB * MB
        ),
    )(n2, qlow, klow, tgt, pkb, own_c, own_d, gains, shifts, zc, zd1, blob_d)


def column(row):
    return jnp.broadcast_to(row, (128, row.shape[1])).T


def prep_kernel(x_e, x_d, masked, embed, src, tgt, qkv_e, wo_e, qkv_s, wo_s, qkv_c, wo_c,
                w1_e, w2_e, w1_d, w2_d, lows, tlow, target, idx, pkb, src_c, mcol, own_es, own_c, own_f, own_d,
                blob_e, blob_s, blob_c, blob_f, blob_d, win):
    _, j = plane_index()
    head = pl.multiple_of(lax.rem(j, 2) * 64 + lax.div(j, 2) * 16, 16)
    unit = pl.multiple_of(j * 64, 64)
    for qkv, wo, own, blob in (
        (qkv_e, wo_e, own_es.at[0], blob_e),
        (qkv_s, wo_s, own_es.at[1], blob_s),
        (qkv_c, wo_c, own_c, blob_c),
    ):
        for m in range(3):
            own[m * 128 : (m + 1) * 128] = qkv[m].T
        own[384:] = wo[...]
        for m in range(4):
            piece = own[pl.ds(m * 128 + head, 16)]
            blob[m * 16 : (m + 1) * 16] = piece.astype(f32)
    for w1, w2, own, blob in ((w1_e, w2_e, own_f, blob_f), (w1_d, w2_d, own_d, blob_d)):
        own[0] = w1[...].T
        own[1] = w2[...]
        for m in range(2):
            blob[m * 64 : (m + 1) * 64] = own[m, pl.ds(unit, 64)].astype(f32)
    src_col, tgt_col = column(src[...]), column(tgt[...])
    pkb[0] = src_col
    src_c[...] = src_col
    pkb[1] = tgt_col
    idx[0] = src[...]
    idx[1] = tgt[...]
    m = column(masked[...])
    mcol[...] = m
    m4 = jnp.concatenate([m] * 4, axis=1)
    tv = jnp.where(m4 == 1, embed[...], x_d[...].astype(f32))
    target[...] = tv
    lows[0] = x_e[...]
    lows[1] = tv.astype(bf16)
    tlow[...] = tv.astype(bf16)
    s = src[...]
    for b in range(4):
        cut = tgt[:, b * BLK : (b + 1) * BLK]
        lo, hi = jnp.min(cut), jnp.max(cut)
        begin = jnp.sum((s < lo).astype(jnp.int32))
        end = jnp.sum((s <= hi).astype(jnp.int32))
        start = jnp.minimum(lax.div(begin, 128) * 128, 512)
        win[b] = start
        win[4 + b] = (end - start > 512).astype(jnp.int32)


def call_prep(*args):
    full = pl.BlockSpec(memory_space=pltpu.VMEM)
    return pl.pallas_call(
        prep_kernel,
        in_specs=[full] * len(args),
        out_specs=[full] * 16 + [SMEM_SPEC],
        out_shape=[
            SDS((2, 1024, 512), bf16), SDS((1024, 512), bf16), SDS((1024, 512), f32),
            SDS((2, 1, 1024), jnp.int32),
            SDS((2, 1024, 128), jnp.int32), SDS((1024, 128), jnp.int32),
            SDS((1024, 128), jnp.int32),
            SDS((2, 512, 512), bf16), SDS((512, 512), bf16), SDS((2, 512, 512), bf16),
            SDS((2, 512, 512), bf16), SDS((64, 512), f32), SDS((64, 512), f32),
            SDS((64, 512), f32), SDS((128, 512), f32), SDS((128, 512), f32),
            SDS((8,), jnp.int32),
        ],
        compiler_params=pltpu.CompilerParams(vmem_limit_bytes=VMEM_MB * MB),
    )(*args)


class PlaneSum:
    def __init__(self, parts, reds, outs, bufs, ss, rs, ls, far=False):
        self.far = far
        self.parts, self.reds, self.outs, self.bufs = parts, reds, outs, bufs
        self.ss, self.rs, self.ls = ss, rs, ls
        self.place, self.core, self.xn, self.yn, _ = neighbours(1)

    def copy(self, k, s):
        c, x, y = self.place
        h = self.reds[k].shape[0] // 2
        a, b = pl.ds(0, h), pl.ds(h, h)
        red = self.reds[k]
        if s < 5:
            got_c, held, got_a, got_b, got_a2, got_b2 = self.bufs[k]
            src, dst, dev = [
                lambda: (self.parts[k].at[:, :, 1 - c], got_c, self.core),
                lambda: (held.at[:, 1 - x, a], got_a, self.xn),
                lambda: (held.at[1 - y, :, b], got_b, self.yn),
                lambda: (held.at[1 - y, x, a], got_a2, self.yn),
                lambda: (held.at[y, 1 - x, b], got_b2, self.xn),
            ][s]()
        else:
            o = self.outs[k]
            src, dst, dev = [
                lambda: (red.at[a], o.at[y, x, c, a], self.yn),
                lambda: (red.at[b], o.at[y, x, c, b], self.xn),
                lambda: (o.at[:, x, c, a], o.at[:, x, c, a], self.xn),
                lambda: (o.at[y, :, c, b], o.at[y, :, c, b], self.yn),
                lambda: (o.at[:, :, c], o.at[:, :, c], self.core),
            ][s - 5]()
        return pltpu.make_async_remote_copy(
            src_ref=src, dst_ref=dst, send_sem=self.ss.at[k, s], recv_sem=self.rs.at[k, s],
            device_id=dev, device_id_type=MESH,
        )

    def local(self, k):
        c, x, y = self.place
        return pltpu.make_async_copy(self.reds[k], self.outs[k].at[y, x, c], self.ls.at[k])

    def halves(self, k):
        h = self.reds[k].shape[0] // 2
        return slice(0, h), slice(h, 2 * h)

    def each(self, act):
        def run():
            for k in range(len(self.reds)):
                act(k)

        return run

    def fetch(self, k):
        src = self.parts[k].at[:, :, self.place[0]]
        return pltpu.make_async_copy(src, self.bufs[k][1], self.ls.at[k])

    def p1(self):
        def act(k):
            self.copy(k, 0).start()
            if self.far:
                self.fetch(k).start()

        return self.each(act)

    def p2(self):
        def act(k):
            got_c, held = self.bufs[k][:2]
            self.copy(k, 0).wait_recv()
            if self.far:
                self.fetch(k).wait()
                held[...] += got_c[...]
            else:
                held[...] = self.parts[k][:, :, self.place[0]] + got_c[...]
            self.copy(k, 1).start()
            self.copy(k, 2).start()

        return self.each(act)

    def p3(self):
        def act(k):
            c, x, y = self.place
            a, b = self.halves(k)
            _, held, got_a, got_b, _, _ = self.bufs[k]
            self.copy(k, 1).wait_recv()
            held[:, x, a] += got_a[...]
            self.copy(k, 2).wait_recv()
            held[y, :, b] += got_b[...]
            self.copy(k, 3).start()
            self.copy(k, 4).start()

        return self.each(act)

    def p4(self):
        def act(k):
            c, x, y = self.place
            a, b = self.halves(k)
            _, held, _, _, got_a2, got_b2 = self.bufs[k]
            self.copy(k, 3).wait_recv()
            self.reds[k][a] = held[y, x, a] + got_a2[...]
            self.copy(k, 4).wait_recv()
            self.reds[k][b] = held[y, x, b] + got_b2[...]

        return self.each(act)

    def g1(self):
        def act(k):
            self.local(k).start()
            self.copy(k, 5).start()
            self.copy(k, 6).start()

        return self.each(act)

    def g2(self):
        def act(k):
            self.local(k).wait()
            self.copy(k, 5).wait_recv()
            self.copy(k, 6).wait_recv()
            self.copy(k, 7).start()
            self.copy(k, 8).start()

        return self.each(act)

    def g3(self):
        def act(k):
            self.copy(k, 7).wait_recv()
            self.copy(k, 8).wait_recv()
            self.copy(k, 9).start()

        return self.each(act)

    def g4(self):
        return self.each(lambda k: self.copy(k, 9).wait_recv())

    def sent(self, slots):
        def act(k):
            for s in slots:
                self.copy(k, s).wait_send()

        return self.each(act)


REDUCE, SPREAD = range(5), range(5, 10)


def sum_bufs(shapes):
    out = []
    for r, w in shapes:
        out += [VM((2, 2, r, w), f32), VM((2, 2, r, w), f32), VM((2, r // 2, w), f32),
                VM((2, r // 2, w), f32), VM((r // 2, w), f32), VM((r // 2, w), f32)]
    return out


def take_bufs(refs, count):
    return [refs[6 * k : 6 * k + 6] for k in range(count)], refs[6 * count :]


def sum_sems(count):
    return [pltpu.SemaphoreType.DMA((count, 10)), pltpu.SemaphoreType.DMA((count, 10)),
            pltpu.SemaphoreType.DMA((count,))]


def plane_barrier():
    _, core, xn, yn, _ = neighbours(1)
    barrier_with([core, xn, yn])


FFN_CHUNKS = [(64, 512), (64, 512)]
ATTN_CHUNKS = [(192, 128), (16, 512)]


def chunked(r, w):
    return (2, 2, 2, r, w)


def norm_back_all(dy, n, r, gain, gs_o, d_s, g_s):
    gs_o[...] = jnp.zeros_like(gs_o)
    for b in range(4):
        rows = rows_at(b)
        dyv, nv = dy(rows), n[rows]
        gs_o[0:1] += jnp.sum(dyv * nv, axis=0, keepdims=True)
        gs_o[1:2] += jnp.sum(dyv, axis=0, keepdims=True)
        d = layer_norm_back(dyv, nv, r[rows], gain)
        d_s[rows] = d
        g_s[rows] = d.astype(bf16)


def attend_slot(cross, win, w, pt, v, kt, q, ot, g_s, acc, dkey, scratch, tick):
    do_s, dot_s, dk_s, dv_s, dqt_s = scratch
    for b in range(4):
        rows = rows_at(b)
        do_s[rows] = nt(g_s[rows], w[0, 384:]).astype(bf16)
        dot_s[:, rows] = nt(w[0, 384:], g_s[rows]).astype(bf16)
    dk_s[...] = jnp.zeros_like(dk_s)
    dv_s[...] = jnp.zeros_like(dv_s)

    def block(b, start, width):
        rows = rows_at(b)
        keys = pl.ds(start, width)
        prow = keys if cross else slice(None)
        prod = dot_s[:, rows].astype(f32) * ot[0, :, rows].astype(f32)
        delta = jnp.concatenate(
            [jnp.sum(prod[:64], axis=0, keepdims=True), jnp.sum(prod[64:], axis=0, keepdims=True)],
            axis=1,
        )
        dpt = nn(v[0, keys], block_diag(dot_s[:64, rows], dot_s[64:, rows]))
        ptv = pt[0, b, prow]
        dst = (ptv.astype(f32) * (dpt - delta)).astype(bf16)
        dv_s[keys] += nn(ptv, two_heads(do_s[rows]))
        dk_s[keys] += nn(dst, two_heads(q[0, rows]))
        dqt_s[:64, rows] = (nn(kt[0, :64, keys], dst[:, :BLK]) * 0.125).astype(bf16)
        dqt_s[64:, rows] = (nn(kt[0, 64:, keys], dst[:, BLK:]) * 0.125).astype(bf16)

    for b in range(4):
        if cross:
            start = pl.multiple_of(win[b], 128)
            pl.when(win[4 + b] == 0)(lambda b=b, start=start: block(b, start, 512))
            pl.when(win[4 + b] != 0)(lambda b=b: block(b, 0, 1024))
        else:
            block(b, self_start(b), 512)
        tick(b)
    for b in range(4):
        rows = rows_at(b)
        dkb, dvb = dk_s[rows].astype(bf16), dv_s[rows].astype(bf16)
        kv = jnp.concatenate([dkb, dvb], axis=1)
        acc[rows] += tn(dqt_s[:, rows], w[0, :128])
        if cross:
            dkey[rows] += nn(kv, w[0, 128:384])
        else:
            acc[rows] += nn(kv, w[0, 128:384])


def attend_weights(dqkv_o, dwo_o, ot, g_s, alow, blow, scratch):
    _, _, dk_s, dv_s, dqt_s = scratch

    def put(m, val):
        dqkv_o[:, :, :, m * 64 : (m + 1) * 64] = val.T.reshape(2, 2, 2, 64, 128)

    put(0, nn(dqt_s[...], alow[...]))
    put(1, tn(dk_s[...].astype(bf16), blow[...]))
    put(2, tn(dv_s[...].astype(bf16), blow[...]))
    dwo_o[...] = nn(ot[0], g_s[...]).reshape(2, 2, 2, 16, 512)


ATTN_SCRATCH = [
    VM((1024, 128), bf16), VM((128, 1024), bf16), VM((1024, 128), f32), VM((1024, 128), f32),
    VM((128, 1024), bf16),
]


def cross_bwd_kernel(*refs):
    (win, dy, n, r, gains, w, pt, v, kt, q, ot, alow, blow) = refs[:13]
    acc, dkey, dqkv_o, dwo_o, gs_o, g_s = refs[13:19]
    scratch = refs[19:]
    p = pl.program_id(0)

    @pl.when(p == 0)
    def _():
        norm_back_all(lambda rows: dy[rows], n, r, gains[3:4], gs_o, acc, g_s)
        dkey[...] = jnp.zeros_like(dkey)

    attend_slot(True, win, w, pt, v, kt, q, ot, g_s, acc, dkey, scratch, lambda b: None)

    @pl.when(p == 0)
    def _():
        attend_weights(dqkv_o, dwo_o, ot, g_s, alow, blow, scratch)


def call_cross_bwd(win, dy, n, r, gains, saved, alow, blow):
    w, pt, q, v, kt, ot = saved
    a, b = [chunked(*s) for s in ATTN_CHUNKS]

    def by_slot(*tail):
        return pl.BlockSpec((1,) + tail, lambda t: (t,) + (0,) * len(tail))

    return pl.pallas_call(
        cross_bwd_kernel,
        grid=(4,),
        in_specs=[
            SMEM_SPEC, held((1024, 512)), held((1024, 512)), held((1024, 1)), held((5, 512)),
            by_slot(512, 512), by_slot(4, 1024, 512), by_slot(1024, 128), by_slot(128, 1024),
            by_slot(1024, 128), by_slot(128, 1024), held((1024, 512)), held((1024, 512)),
        ],
        out_specs=[kept((1024, 512)), kept((1024, 512)), kept(a), kept(b), kept((8, 512))],
        out_shape=[SDS((1024, 512), f32), SDS((1024, 512), f32), SDS(a, f32), SDS(b, f32),
                   SDS((8, 512), f32)],
        scratch_shapes=[VM((1024, 512), bf16)] + ATTN_SCRATCH,
        compiler_params=pltpu.CompilerParams(vmem_limit_bytes=VMEM_MB * MB),
    )(win, dy, n, r, gains, w, pt, v, kt, q, ot, alow, blow)


def ffn_back_slot(w, slope, g_s, db_s, acc, tick):
    for b in range(4):
        rows = rows_at(b)
        db = (nt(g_s[rows], w[0, 1]) * slope[rows].astype(f32)).astype(bf16)
        db_s[rows] = db
        acc[rows] += nn(db, w[0, 0])
        tick(b)


def ffn_weights(dw1_o, dw2_o, alow, db_s, h, g_s):
    dw1_o[...] = tn(alow[...], db_s[...]).reshape(2, 2, 2, 64, 512)
    dw2_o[...] = tn(h[...], g_s[...]).reshape(2, 2, 2, 64, 512)


def dec_ffn_bwd_kernel(dy, n, r, gains, alow, w, h, slope, acc, gs_o, dw1_o, dw2_o, g_s, db_s):
    c = pl.program_id(0)

    @pl.when(c == 0)
    def _():
        norm_back_all(lambda rows: dy[rows].astype(f32), n, r, gains[4:5], gs_o, acc, g_s)

    ffn_back_slot(w, slope, g_s, db_s, acc, lambda b: None)

    @pl.when(c == 0)
    def _():
        ffn_weights(dw1_o, dw2_o, alow, db_s, h, g_s)


def call_dec_ffn_bwd(dy, n, r, gains, alow, w, h, slope):
    shapes = [chunked(*s) for s in FFN_CHUNKS]
    return pl.pallas_call(
        dec_ffn_bwd_kernel,
        grid=(4,),
        in_specs=[
            held((1024, 512)), held((1024, 512)), held((1024, 1)), held((5, 512)),
            held((1024, 512)), pl.BlockSpec((1, 2, 512, 512), lambda t: (t, 0, 0, 0)),
            held((1024, 512)), pl.BlockSpec((1024, 512), lambda t: (0, t)),
        ],
        out_specs=[kept((1024, 512)), kept((8, 512))] + [kept(s) for s in shapes],
        out_shape=[SDS((1024, 512), f32), SDS((8, 512), f32)] + [SDS(s, f32) for s in shapes],
        scratch_shapes=[VM((1024, 512), bf16), VM((1024, 512), bf16)],
        compiler_params=pltpu.CompilerParams(vmem_limit_bytes=VMEM_MB * MB),
    )(dy, n, r, gains, alow, w, h, slope)


def last_of(t):
    kind = jnp.where((t == 0) | ((t >= 6) & (t <= 8)), 1, 0)
    block = jnp.where(t < 5, 4, jnp.where(t == 5, 0, jnp.where(t < 9, t - 1, t - 8)))
    return kind, block


def last_kernel(*refs):
    n2, r2, gains, alow_s, mcol, gs3, gs4 = refs[:7]
    w, pt, v, kt, q, ot, wf, slope = refs[7:15]
    far, refs = refs[15:24], refs[24:]
    x_far, parts_d, parts_c, refs = refs[0], refs[1:3], refs[3:5], refs[5:]
    mask_o, gain_o, shift_o, dec_o, enc_o, refs = *refs[:5], refs[5:]
    outs = [refs[2 * k : 2 * k + 2] for k in range(5)]
    refs = refs[10:]
    acc2, n1, r1, cot, alow_f, h, n0, r0, x_e, refs = *refs[:9], refs[9:]
    gs0, gs1, gs2, g2, db_s, small, got, refs = *refs[:7], refs[7:]
    scratch, refs = refs[:5], refs[5:]
    dws, refs = [None, None, refs[:2], refs[2:4], refs[4:6]], refs[6:]
    ls, ss, rs, refs = refs[0], refs[1], refs[2], refs[3:]
    sums = []
    for k, chunks in enumerate((FFN_CHUNKS, ATTN_CHUNKS, ATTN_CHUNKS, FFN_CHUNKS, ATTN_CHUNKS)):
        reds, refs = refs[:2], refs[2:]
        bufs, refs = take_bufs(refs, 2)
        parts = (parts_d, parts_c, *dws[2:])[k]
        sums.append(PlaneSum(parts, reds, outs[k], bufs, *refs[:3], far=k < 2))
        refs = refs[3:]
    d, c, s, f, e = sums
    loads = list(zip(far, (acc2.at[1], acc2.at[0], n1, r1, cot, alow_f, h, n0, r0)))
    loads += [(x_far, x_e), (acc2.at[1], dec_o), (acc2.at[0], enc_o)]
    t = pl.program_id(0)
    kind, _ = last_of(t)

    def load(k):
        return pltpu.make_async_copy(*loads[k], ls.at[k])

    _, core, xn, yn, _ = neighbours(1)

    def swap(k):
        return pltpu.make_async_remote_copy(
            src_ref=small.at[k], dst_ref=got.at[k], send_sem=ss.at[k], recv_sem=rs.at[k],
            device_id=(core, xn, yn)[k], device_id_type=MESH,
        )

    def small_first():
        small[0] = jnp.zeros_like(small[0])
        small[0, 0:1] = gs2[2:3]
        for k, g in enumerate((gs0, gs1, gs2, gs3, gs4)):
            small[0, 1 + k : 2 + k] = g[0:1]
            small[0, 6 + k : 7 + k] = g[1:2]
        swap(0).start()

    def small_next(k):
        def run():
            swap(k).wait_recv()
            small[k + 1] = small[k] + got[k]
            if k < 2:
                swap(k + 1).start()

        return run

    def small_last():
        mask_o[...] = small[3, 0:1]
        gain_o[...] = small[3, 1:6]
        shift_o[...] = small[3, 6:11]
        for k in range(3):
            swap(k).wait_send()

    def end():
        for x in sums:
            x.sent(REDUCE)()
            x.sent(SPREAD)()

    ev = {
        (0, -1): [plane_barrier, d.p1(), c.p1()],
        (0, 1): [d.p2()],
        (0, 2): [c.p2()],
        (0, 4): [s.p1()],
        (1, 0): [d.p3()],
        (1, 2): [c.p3()],
        (1, 4): [f.p1(), s.p2()],
        (2, 1): [d.p4(), d.g1()],
        (2, 3): [f.p2()],
        (3, 0): [c.p4(), c.g1()],
        (3, 2): [d.g2()],
        (4, 0): [s.p3()],
        (4, 2): [f.p3()],
        (5, 0): [c.g2()],
        (5, 1): [d.g3()],
        (5, 2): [s.p4(), s.g1()],
        (5, 4): [e.p1()],
        (6, 0): [f.p4(), f.g1()],
        (6, 1): [c.g3()],
        (6, 2): [e.p2()],
        (7, 0): [s.g2()],
        (7, 1): [d.g4()],
        (7, 2): [f.g2()],
        (8, 0): [e.p3()],
        (8, 1): [c.g4()],
        (8, 2): [s.g3()],
        (8, 4): [small_first],
        (9, 0): [e.p4(), e.g1()],
        (9, 1): [f.g3()],
        (9, 2): [small_next(0)],
        (10, 0): [e.g2()],
        (10, 1): [small_next(1)],
        (10, 2): [s.g4()],
        (11, 0): [e.g3()],
        (11, 1): [small_next(2)],
        (11, 2): [f.g4()],
    }
    attn_steps, ffn_steps = (0, 5, 6, 7, 8, 9, 10, 11), (1, 2, 3, 4)

    @pl.when((t == 0) | (t > 4))
    def _():
        @pl.when(t == 0)
        def _():
            for k in range(10):
                load(k).start()
            load(0).wait()

        run_events(t, attn_steps, ev, -1)

        @pl.when(t == 0)
        def _():
            a = acc2.at[1]
            norm_back_all(lambda rows: a[rows], n2, r2, gains[2:3], gs2, a, g2.at[1])

        @pl.when(t == 5)
        def _():
            for k in (7, 8, 9):
                load(k).wait()
            a = acc2.at[0]
            norm_back_all(lambda rows: a[rows], n0, r0, gains[0:1], gs0, a, g2.at[0])

        attend_slot(False, None, w, pt, v, kt, q, ot, g2.at[kind], acc2.at[kind], None, scratch,
                    lambda b: run_events(t, attn_steps, ev, b))

        @pl.when(t == 0)
        def _():
            attend_weights(*dws[2], ot, g2.at[1], alow_s, alow_s, scratch)

        @pl.when(t == 5)
        def _():
            attend_weights(*dws[4], ot, g2.at[0], x_e, x_e, scratch)

        @pl.when(t == 8)
        def _():
            total = jnp.zeros((1, 512), f32)
            for b in range(4):
                rows = rows_at(b)
                hit = jnp.concatenate([mcol[rows]] * 4, axis=1) == 1
                dx = acc2[1, rows]
                total += jnp.sum(jnp.where(hit, dx, 0.0), axis=0, keepdims=True)
                acc2[1, rows] = jnp.where(hit, 0.0, dx)
            gs2[2:3] = total
            load(10).start()

        run_events(t, attn_steps, ev, 4)

        @pl.when(t == 11)
        def _():
            load(11).start()
            e.g4()()
            small_last()
            end()
            load(10).wait()
            load(11).wait()

    @pl.when((t > 0) & (t < 5))
    def _():
        @pl.when(t == 1)
        def _():
            for k in range(1, 7):
                load(k).wait()
            a = acc2.at[0]
            norm_back_all(lambda rows: a[rows] + cot[rows].astype(f32), n1, r1, gains[1:2], gs1, a,
                          g2.at[0])

        ffn_back_slot(wf, slope, g2.at[0], db_s, acc2.at[0],
                      lambda b: run_events(t, ffn_steps, ev, b))

        @pl.when(t == 1)
        def _():
            ffn_weights(*dws[3], alow_f, db_s, h, g2.at[0])

        run_events(t, ffn_steps, ev, 4)


def call_last(n2, r2, gains, alow_s, mcol, gs3, gs4, saved, wf, slope, far, parts_d, parts_c):
    w, pt, q, v, kt, ot = saved
    groups = (FFN_CHUNKS, ATTN_CHUNKS, ATTN_CHUNKS, FFN_CHUNKS, ATTN_CHUNKS)

    def by_es(*tail):
        return pl.BlockSpec((1,) + tail, lambda t: (last_of(t)[1],) + (0,) * len(tail))

    def chunk(t):
        return jnp.clip(t - 1, 0, 3)

    net = []
    for g in groups:
        net += [VM(s, f32) for s in g] + sum_bufs(g) + sum_sems(2)
    results = [chunked(*s) for g in groups for s in g]
    return pl.pallas_call(
        last_kernel,
        grid=(12,),
        in_specs=[
            held((1024, 512)), held((1024, 1)), held((5, 512)), held((1024, 512)),
            held((1024, 128)), held((8, 512)), held((8, 512)), by_es(512, 512),
            by_es(4, 512, 512), by_es(1024, 128), by_es(128, 1024), by_es(1024, 128),
            by_es(128, 1024), pl.BlockSpec((1, 2, 512, 512), lambda t: (chunk(t), 0, 0, 0)),
            pl.BlockSpec((1024, 512), lambda t: (0, chunk(t))),
        ] + [ANY] * 14,
        out_specs=[kept((1, 512)), kept((5, 512)), kept((5, 512))] + [ANY] * 12,
        out_shape=[SDS((1, 512), f32), SDS((5, 512), f32), SDS((5, 512), f32),
                   SDS((1024, 512), f32), SDS((1024, 512), f32)] + [SDS(s, f32) for s in results],
        scratch_shapes=[
            VM((2, 1024, 512), f32), VM((1024, 512), f32), VM((1024, 1), f32), VM((1024, 512), bf16),
            VM((1024, 512), bf16), VM((1024, 512), bf16), VM((1024, 512), f32), VM((1024, 1), f32),
            VM((1024, 512), bf16), VM((8, 512), f32), VM((8, 512), f32), VM((8, 512), f32),
            VM((2, 1024, 512), bf16), VM((1024, 512), bf16), VM((4, 16, 512), f32),
            VM((3, 16, 512), f32),
        ] + ATTN_SCRATCH + [VM(chunked(*s), f32) for g in groups[2:] for s in g]
        + [pltpu.SemaphoreType.DMA((12,)), pltpu.SemaphoreType.DMA((3,)),
           pltpu.SemaphoreType.DMA((3,))] + net,
        compiler_params=pltpu.CompilerParams(
            collective_id=3, has_side_effects=True, vmem_limit_bytes=VMEM_MB * MB
        ),
    )(n2, r2, gains, alow_s, mcol, gs3, gs4, w, pt, v, kt, q, ot, wf, slope, *far, *parts_d,
      *parts_c)


def deliver_kernel(count, *refs):
    srcs, dsts, bufs = refs[:count], refs[count : 2 * count], refs[2 * count : 3 * count]
    ins, outs = refs[3 * count :]

    def load(k):
        return pltpu.make_async_copy(srcs[k], bufs[k], ins.at[k])

    def store(k):
        if len(dsts[k].shape) < 6:
            return [pltpu.make_async_copy(bufs[k], dsts[k], outs.at[k, 0])]
        return [
            pltpu.make_async_copy(bufs[k].at[:, :, :, pl.ds(m * 64, 64)], dsts[k].at[m], outs.at[k, m])
            for m in range(3)
        ]

    for k in range(count):
        load(k).start()
    for k in range(count):
        load(k).wait()
        for c in store(k):
            c.start()
    for k in range(count):
        for c in store(k):
            c.wait()


def deliver(arrays):
    shapes = [(3, 2, 2, 2, 64, 128) if a.shape[-1] == 128 else a.shape for a in arrays]
    count = len(arrays)
    return pl.pallas_call(
        functools.partial(deliver_kernel, count),
        in_specs=[ANY] * count,
        out_specs=[ANY] * count,
        out_shape=[SDS(s, a.dtype) for s, a in zip(shapes, arrays)],
        scratch_shapes=[VM(a.shape, a.dtype) for a in arrays]
        + [pltpu.SemaphoreType.DMA((count,)), pltpu.SemaphoreType.DMA((count, 3))],
        compiler_params=pltpu.CompilerParams(vmem_limit_bytes=VMEM_MB * MB),
    )(*arrays)


def per_device(planes, tensor, enc_in, dec_in, src_idx, tgt_idx, masked, mask_embed, enc_qkv,
               enc_out_w, enc_w1, enc_w2, self_qkv, self_out_w, cross_qkv, cross_out_w, dec_w1,
               dec_w2, gains, shifts, enc_cot, dec_cot):
    (lows, target_low, target, idx, pkb, src_col, mcol, own_es, own_c, own_f, own_d, blob_e, blob_s, blob_c, blob_f,
     blob_d, win) = call_prep(
        enc_in[0], dec_in[0], masked, mask_embed[None], src_idx, tgt_idx, enc_qkv, enc_out_w,
        self_qkv, self_out_w, cross_qkv, cross_out_w, enc_w1, enc_w2, dec_w1, dec_w2)
    (w_es, pt_es, q_es, v_es, kt_es, ot_es, w_f, slope_e, h_e, r0, r2, r1, n0, n2, n1, first_low,
     second_low, enc_low, zc, zd1) = call_first(
        tensor, lows, target, idx, pkb, own_es, own_f, gains, shifts,
        (blob_e, blob_s, blob_f, blob_c, blob_d))
    (w_c, pt_c, q_c, v_c, kt_c, ot_c, w_d, slope_d, h_d, r3, r4, n3, n4, third_low,
     dec_low) = call_second(
        tensor, n2, second_low, enc_low, tgt_idx, src_col, own_c, own_d, gains, shifts, zc, zd1,
        blob_d)
    save_es = (w_es, pt_es, q_es, v_es, kt_es, ot_es)
    save_c = (w_c, pt_c, q_c, v_c, kt_c, ot_c)

    d_third, gs4, *parts_d = call_dec_ffn_bwd(
        dec_cot[0], n4, r4, gains, third_low, w_d, h_d, slope_d)
    d_second, d_key, *parts_c, gs3 = call_cross_bwd(
        win, d_third, n3, r3, gains, save_c, second_low, enc_low)
    far = (d_second, d_key, n1, r1, enc_cot[0], first_low, h_e, n0, r0, enc_in[0])
    (mask_grad, gain_grad, shift_grad, dec_grad, d_enc, dw1_d, dw2_d, dqkv_c, dwo_c, dqkv_s, dwo_s,
     dw1_e, dw2_e, dqkv_e, dwo_e) = call_last(
        n2, r2, gains, target_low, mcol, gs3, gs4, save_es, w_f, slope_e, far, parts_d, parts_c)

    sums = (mask_grad, gain_grad, shift_grad, dqkv_e, dwo_e, dw1_e, dw2_e, dqkv_s, dwo_s, dqkv_c,
            dwo_c, dw1_d, dw2_d)
    if planes > 1:
        same = [[p * 8 + k for p in range(planes)] for k in range(8)]
        sums = lax.psum(sums, "dp", axis_index_groups=same)
    enc_low, dec_low, d_enc, dec_grad, mask_grad, gain_grad, shift_grad, *mats = deliver(
        [enc_low, dec_low, d_enc, dec_grad, *sums])
    mats = [m.reshape(3, 512, 128) if m.ndim == 6 else m.reshape(-1, 512) for m in mats]
    return (enc_low[None], dec_low[None], d_enc[None], dec_grad[None], mask_grad[0], *mats,
            gain_grad, shift_grad)


def solution(mesh):
    tokens, index = P("dp", None, None), P("dp", None)
    qkv, cols, rows = P(None, None, "tensor"), P(None, "tensor"), P("tensor", None)
    weights = (qkv, rows, cols, rows, qkv, rows, qkv, rows, cols, rows)
    return jax.shard_map(
        functools.partial(per_device, mesh.shape["dp"] // 8, mesh.shape["tensor"]),
        mesh=mesh,
        in_specs=(tokens, tokens, index, index, index, P()) + weights + (P(), P(), tokens, tokens),
        out_specs=(tokens,) * 4 + (P(),) + weights + (P(), P()),
        check_vma=False,
    )
```

```python
import functools

import jax
import jax.numpy as jnp
from jax import lax
from jax.experimental import pallas as pl
from jax.experimental.pallas import tpu as pltpu
from jax.sharding import PartitionSpec as P

f32, bf16 = jnp.float32, jnp.bfloat16
HEAD_DIM = 64
EPS = 1e-05
FLOOR = -1000000000.0
BLK = 256
MB = 1 << 20
VMEM_MB = 60
MESH = pl.DeviceIdType.MESH
VM = pltpu.VMEM


def nt(a, b):
    return lax.dot_general(a, b, (((1,), (1,)), ((), ())), preferred_element_type=f32)


def nn(a, b):
    return lax.dot_general(a, b, (((1,), (0,)), ((), ())), preferred_element_type=f32)


def tn(a, b):
    return lax.dot_general(a, b, (((0,), (0,)), ((), ())), preferred_element_type=f32)


def layer_norm(v):
    c = v - jnp.mean(v, axis=-1, keepdims=True)
    r = lax.rsqrt(jnp.mean(c * c, axis=-1, keepdims=True) + EPS)
    return c * r, r


def layer_norm_back(dy, n, r, gain):
    dn = dy * gain
    m1 = jnp.mean(dn, axis=-1, keepdims=True)
    m2 = jnp.mean(dn * n, axis=-1, keepdims=True)
    return r * (dn - m1 - n * m2)


def block_diag(a, b):
    z = jnp.zeros_like(a)
    return jnp.concatenate(
        [jnp.concatenate([a, z], axis=1), jnp.concatenate([z, b], axis=1)], axis=0
    )


def two_heads(x):
    lane = lax.broadcasted_iota(jnp.int32, x.shape, 1)
    z = jnp.zeros_like(x)
    return jnp.concatenate([jnp.where(lane < HEAD_DIM, x, z), jnp.where(lane < HEAD_DIM, z, x)], 0)


def rows_at(b):
    return slice(b * BLK, (b + 1) * BLK)


def self_start(b):
    return min(max(b * BLK - 128, 0), 512)


def project_slot(w, kinds, get, rows_out):
    for b in range(4):
        xb = get(b)
        nat = nt(xb, w[kinds[0] * 128 : kinds[-1] * 128 + 128])
        tr = nt(w[kinds[0] * 128 : kinds[-1] * 128 + 128], xb)
        for k, kind in enumerate(kinds):
            cut = slice(k * 128, k * 128 + 128)
            for dst, val in rows_out(kind, b, nat[:, cut], tr[cut]):
                dst[...] = val.astype(bf16)


def softmax_block(k_s, qt, keys, pk, pq):
    bias = jnp.where(pk == pq, 0.0, FLOOR).astype(f32)
    s = nn(k_s[keys], block_diag(qt[:64], qt[64:])) + jnp.concatenate([bias, bias], axis=1)
    e = jnp.exp(s - jnp.max(s, axis=0, keepdims=True))
    return (e * (1.0 / jnp.sum(e, axis=0, keepdims=True))).astype(bf16)


def mix_block(vt_s, keys, pt):
    return jnp.concatenate([nn(vt_s[:64, keys], pt[:, :BLK]), nn(vt_s[64:, keys], pt[:, BLK:])], 0)


def wide(pkb):
    return jnp.concatenate([pkb, pkb], axis=1)


def ffn_slot(w, al, acc, slope_o, h_o, first, tick):
    for b in range(4):
        rows = rows_at(b)
        before = nt(al[rows], w[0])
        cdf = 0.5 + 0.5 * lax.erf(before * (0.5**0.5))
        pdf = jnp.exp(before * before * -0.5) * 0.3989422804014327
        slope_o[rows] = (cdf + before * pdf).astype(bf16)
        hidden = (before * cdf).astype(bf16)

        @pl.when(first)
        def _():
            h_o[rows] = hidden

        acc[rows] += nn(hidden, w[1])
        tick(b)


def finish_norm(acc, gain, shift, n_ref, r_o, y_ref):
    for b in range(4):
        rows = rows_at(b)
        n, r = layer_norm(acc[rows])
        n_ref[rows] = n
        r_o[rows] = r
        y_ref[rows] = (n * gain + shift).astype(bf16)


def plane_index():
    dp = lax.axis_index("dp")
    return dp, lax.rem(dp, 8)


def neighbours(tensor):
    dp, j = plane_index()
    z = lax.axis_index("tensor")
    c, x, y = lax.rem(j, 2), lax.rem(lax.div(j, 2), 2), lax.div(j, 4)
    core, xn, yn = (dp + 1 - 2 * c, z), (dp + 2 - 4 * x, z), (dp + 4 - 8 * y, z)
    down = {k: (dp, lax.rem(z + tensor - k, tensor)) for k in range(1, tensor)}
    return (c, x, y), core, xn, yn, down


def barrier_with(peers):
    sem = pltpu.get_barrier_semaphore()
    for peer in peers:
        pl.semaphore_signal(sem, inc=1, device_id=peer, device_id_type=MESH)
    pl.semaphore_wait(sem, len(peers))


class Gather:
    def __init__(self, items, ss, rs, tensor):
        assert tensor == 4
        self.items, self.ss, self.rs = items, ss, rs
        _, self.core, self.xn, self.yn, self.down = neighbours(tensor)
        self.dp, self.z = lax.axis_index("dp"), lax.axis_index("tensor")

    def barrier(self):
        barrier_with([self.core, self.xn, self.yn] + list(self.down.values()))

    def copy(self, t, s, src, dst, dev, r=None):
        return lambda: pltpu.make_async_remote_copy(
            src_ref=src, dst_ref=dst, send_sem=self.ss.at[t, s],
            recv_sem=self.rs.at[t, s if r is None else r], device_id=dev, device_id_type=MESH,
        )

    def along(self, t):
        rnd, src, land = self.items[t]
        z, dp = self.z, self.dp
        inner = (z == 1) | (z == 2)
        if rnd == 1:
            left, right = jnp.maximum(z - 1, 0), jnp.minimum(z + 1, 3)
            return [
                (inner, self.copy(t, 0, src, land.at[0], (dp, left), 0)),
                (inner, self.copy(t, 9, src, land.at[0], (dp, right), 0)),
            ], None
        if rnd == 2:
            return [(None, self.copy(t, 0, src, land.at[0], (dp, lax.rem(2 * z + 1, 5)), 0))], None
        outer = (z == 0) | (z == 3)
        to, on = jnp.where(z == 0, 2, 1), jnp.where(z == 1, 0, 3)
        return [(outer, self.copy(t, 0, src, land.at[0], (dp, to), 0))], (
            inner, self.copy(t, 9, land.at[0], land.at[0], (dp, on), 0))

    def make(self, t):
        land = self.items[t][2]
        half = land.shape[1] // 2
        a, b = pl.ds(0, half), pl.ds(half, half)
        return [
            self.copy(t, 0, land.at[0], land.at[0], self.down[1]),
            self.copy(t, 1, land.at[0], land.at[1], self.xn),
            self.copy(t, 2, land.at[0], land.at[2], self.yn),
            self.copy(t, 3, land.at[0], land.at[4], self.core),
            self.copy(t, 4, land.at[1, a], land.at[3, a], self.yn),
            self.copy(t, 5, land.at[1], land.at[5], self.core),
            self.copy(t, 6, land.at[2, b], land.at[3, b], self.xn),
            self.copy(t, 7, land.at[2], land.at[6], self.core),
            self.copy(t, 8, land.at[3], land.at[7], self.core),
        ]

    def send(self, t):
        for cond, c in self.along(t)[0]:
            if cond is None:
                c().start()
            else:
                pl.when(cond)(lambda c=c: c().start())

    def onward(self, t):
        inner, c = self.along(t)[1]

        @pl.when(inner)
        def _():
            self.make(t)[0]().wait_recv()
            c().start()

    def spread(self, t):
        c = self.make(t)
        if self.items[t][0] < 3:
            c[0]().wait_recv()
        else:
            pl.when((self.z == 0) | (self.z == 3))(lambda: c[0]().wait_recv())
        for k in (1, 2, 3):
            c[k]().start()

    def relay(self, t):
        c = self.make(t)
        c[1]().wait_recv()
        c[4]().start()
        c[5]().start()
        c[2]().wait_recv()
        c[6]().start()
        c[7]().start()

    def pair(self, t):
        c = self.make(t)
        c[4]().wait_recv()
        c[6]().wait_recv()
        c[8]().start()

    def done(self, t):
        c = self.make(t)
        for k in (3, 5, 7, 8):
            c[k]().wait_recv()

    def finish(self):
        for t in range(len(self.items)):
            first, on = self.along(t)
            for cond, c in first + ([on] if on else []):
                if cond is None:
                    c().wait_send()
                else:
                    pl.when(cond)(lambda c=c: c().wait_send())
            for c in self.make(t)[1:]:
                c().wait_send()

    def plan(self, text):
        acts = {"Z": self.send, "Y": self.onward, "S": self.spread, "R": self.relay, "P": self.pair, "D": self.done}
        ev = {}
        for step, point, words in text:
            row = ev.setdefault((step, point), [])
            for word in words.split():
                row.append(functools.partial(acts[word[0]], int(word[1:])))
        return ev


FIRST_PLAN = (
    (0, -1, "Z2 Z0 Z1 Z5 Z3 Z4 Z8 Z6 Z7 Z11 Z9 Z10"),
    (1, 0, "S0"),
    (1, 2, "S1 Y2"),
    (2, -1, "R0 S2 S3 R1 P0 S4 Y5 D0"),
    (2, 1, "R2"),
    (2, 2, "S5"),
    (2, 3, "R3"),
    (3, -1, "P1 S6 R4 D1"),
    (3, 1, "P2"),
    (3, 3, "R5 S7 Y8"),
    (4, -1, "D2"),
    (4, 0, "P3"),
    (5, -1, "D3"),
    (5, 0, "R6"),
    (5, 1, "S8 P4 S9"),
    (5, 2, "P5"),
    (5, 3, "S10 Y11"),
    (6, -1, "D4"),
    (6, 2, "R7"),
    (6, 3, "S11"),
    (7, -1, "D5"),
    (7, 0, "P6"),
    (8, 1, "R8"),
    (9, -1, "D6"),
    (9, 0, "R9"),
    (9, 3, "R10"),
    (10, -1, "P7 D7"),
    (10, 1, "R11"),
    (11, -1, "P8 P9 P10 D8"),
    (11, 2, "P11"),
    (11, 3, "D9 D10 D11"),
)
SECOND_PLAN = (
    (0, -1, "Z2 Z0 Z1"),
    (1, 0, "S0"),
    (1, 3, "S1 Y2"),
    (2, 1, "R0"),
    (2, 2, "S2"),
    (3, 0, "R1"),
    (3, 1, "P0"),
    (4, 0, "R2"),
    (5, -1, "D0"),
    (5, 0, "P1"),
    (5, 3, "P2"),
    (6, -1, "D1"),
    (7, -1, "D2"),
)


def run_events(t, steps, events, point):
    for step in steps:
        acts = events.get((step, point))
        if acts:

            @pl.when(t == step)
            def _(acts=acts):
                for act in acts:
                    act()


def es_of(t):
    kind = jnp.where((t == 1) | (t >= 5), 1, 0)
    p = jnp.where(t < 2, 0, jnp.where(t < 5, t - 1, t - 4))
    return kind, jnp.minimum(p, 3)


def es_block(t):
    kind, p = es_of(t)
    return kind * 4 + p


def first_kernel(tensor, *refs):
    (lows, target, idx, pkb, own_es, own_f, gains, shifts) = refs[:8]
    blob_e, blob_s, blob_f, blob_c = refs[8:12]
    (wes_o, pt_o, q_o, v_o, kt_o, ot_o, wf_o, slope_o, h_o, r0_o, r2_o, r1_o, n0_o, n2_o,
     n1_o, y0_o, y2_o, encl_o, zc_o) = refs[12:31]
    (land_a, land_f, accs, na, ylow, encl, k_s, qt_s, vt_s, ss, rs, cs) = refs[31:]
    t = pl.program_id(0)
    items = [(k, blob_e, land_a.at[k - 1]) for k in (1, 2, 3)]
    items += [(k, blob_s, land_a.at[2 + k]) for k in (1, 2, 3)]
    items += [(k, blob_f, land_f.at[k - 1]) for k in (1, 2, 3)]
    items += [(k, blob_c, zc_o.at[k - 1]) for k in (1, 2, 3)]
    net = Gather(items, ss, rs, tensor)
    outs = [
        (na.at[0], n0_o), (ylow.at[0], y0_o), (na.at[1], n2_o), (ylow.at[1], y2_o),
        (accs.at[0], n1_o), (encl, encl_o),
    ]

    def out(k):
        return pltpu.make_async_copy(*outs[k], cs.at[k])

    ev = net.plan(FIRST_PLAN)
    kind, p = es_of(t)
    es_steps, f_steps = range(8), range(8, 12)

    @pl.when(t < 8)
    def _():
        pl.when(t == 0)(net.barrier)
        run_events(t, es_steps, ev, -1)

        @pl.when(p == 0)
        def _():
            wes_o[0] = own_es[kind]

        @pl.when((p == 0) & (kind == 0))
        def _():
            accs[0] = lows[0].astype(f32)

        @pl.when((p == 0) & (kind == 1))
        def _():
            accs[1] = target[...]

        @pl.when(p > 0)
        def _():
            for m in range(4):
                piece = land_a[kind * 3 + p - 1, :, m * 16 : (m + 1) * 16, :]
                wes_o[0, m * 128 : (m + 1) * 128] = piece.reshape(128, 512).astype(bf16)

        w = wes_o.at[0]

        def outs_of(m, b, nat, tr):
            rows = rows_at(b)
            if m == 0:
                return [(q_o.at[0, rows], nat * 0.125), (qt_s.at[:, rows], tr * 0.125)]
            if m == 1:
                return [(k_s.at[rows], nat), (kt_o.at[0, :, rows], tr)]
            return [(v_o.at[0, rows], nat), (vt_s.at[:, rows], tr)]

        project_slot(w, (0, 1, 2), lambda b: lows[kind, rows_at(b)], outs_of)
        for b in range(4):
            rows = rows_at(b)
            keys = slice(self_start(b), self_start(b) + 512)
            pt = softmax_block(k_s, qt_s[:, rows], keys, wide(pkb[kind, keys]), idx[kind, :, rows])
            pt_o[0, b] = pt
            ot = mix_block(vt_s, keys, pt).astype(bf16)
            ot_o[0, :, rows] = ot
            accs[kind, rows] += tn(ot, w[384:])
            run_events(t, es_steps, ev, b)

        @pl.when(t == 4)
        def _():
            finish_norm(accs.at[0], gains[0:1], shifts[0:1], na.at[0], r0_o, ylow.at[0])
            out(0).start()
            out(1).start()

        @pl.when(t == 7)
        def _():
            finish_norm(accs.at[1], gains[2:3], shifts[2:3], na.at[1], r2_o, ylow.at[1])
            out(2).start()
            out(3).start()

    @pl.when(t >= 8)
    def _():
        run_events(t, f_steps, ev, -1)

        @pl.when(t == 8)
        def _():
            wf_o[0] = own_f[...]
            accs[0] = na[0] * gains[0:1] + shifts[0:1]

        @pl.when(t > 8)
        def _():
            for m in range(2):
                piece = land_f[t - 9, :, m * 64 : (m + 1) * 64, :]
                wf_o[0, m] = piece.reshape(512, 512).astype(bf16)

        ffn_slot(wf_o.at[0], ylow.at[0], accs.at[0], slope_o, h_o, t == 8,
                 lambda b: run_events(t, f_steps, ev, b))

        @pl.when(t == 11)
        def _():
            finish_norm(accs.at[0], gains[1:2], shifts[1:2], accs.at[0], r1_o, encl)
            out(4).start()
            out(5).start()
            for k in range(6):
                out(k).wait()
            net.finish()


def held(shape):
    return pl.BlockSpec(shape, lambda t: (0,) * len(shape), pipeline_mode=pl.Buffered(1))


def kept(shape):
    return pl.BlockSpec(shape, lambda t: (0,) * len(shape))


ANY = pl.BlockSpec(memory_space=pl.ANY)
SMEM_SPEC = pl.BlockSpec(memory_space=pltpu.SMEM)
SDS = jax.ShapeDtypeStruct


def by_es(*tail):
    return pl.BlockSpec((1,) + tail, lambda t: (es_block(t),) + (0,) * len(tail))


def call_first(tensor, lows, target, idx, pkb, own_es, own_f, gains, shifts, blobs):
    def chunk(t):
        return jnp.maximum(t - 8, 0)

    n_items = 12
    return pl.pallas_call(
        functools.partial(first_kernel, tensor),
        grid=(12,),
        in_specs=[
            held((2, 1024, 512)), held((1024, 512)), held((2, 1, 1024)), held((2, 1024, 128)),
            held((2, 512, 512)), held((2, 512, 512)), held((5, 512)), held((5, 512)),
        ] + [ANY] * 4,
        out_specs=[
            by_es(512, 512), by_es(4, 512, 512), by_es(1024, 128), by_es(1024, 128),
            by_es(128, 1024), by_es(128, 1024),
            pl.BlockSpec((1, 2, 512, 512), lambda t: (chunk(t), 0, 0, 0)),
            pl.BlockSpec((1024, 512), lambda t: (0, chunk(t))),
            kept((1024, 512)), kept((1024, 1)), kept((1024, 1)), kept((1024, 1)),
        ] + [ANY] * 7,
        out_shape=[
            SDS((8, 512, 512), bf16), SDS((8, 4, 512, 512), bf16), SDS((8, 1024, 128), bf16),
            SDS((8, 1024, 128), bf16), SDS((8, 128, 1024), bf16), SDS((8, 128, 1024), bf16),
            SDS((4, 2, 512, 512), bf16), SDS((1024, 2048), bf16), SDS((1024, 512), bf16),
            SDS((1024, 1), f32), SDS((1024, 1), f32), SDS((1024, 1), f32),
            SDS((1024, 512), f32), SDS((1024, 512), f32), SDS((1024, 512), f32),
            SDS((1024, 512), bf16), SDS((1024, 512), bf16), SDS((1024, 512), bf16), SDS((3, 8, 64, 512), f32),
        ],
        scratch_shapes=[
            VM((6, 8, 64, 512), f32), VM((3, 8, 128, 512), f32), VM((2, 1024, 512), f32),
            VM((2, 1024, 512), f32), VM((2, 1024, 512), bf16), VM((1024, 512), bf16),
            VM((1024, 128), bf16), VM((128, 1024), bf16), VM((128, 1024), bf16),
            pltpu.SemaphoreType.DMA((n_items, 10)), pltpu.SemaphoreType.DMA((n_items, 10)),
            pltpu.SemaphoreType.DMA((6,)),
        ],
        compiler_params=pltpu.CompilerParams(
            collective_id=0, has_side_effects=True, vmem_limit_bytes=VMEM_MB * MB
        ),
    )(lows, target, idx, pkb, own_es, own_f, gains, shifts, *blobs)


def second_kernel(tensor, *refs):
    (n2, qlow, klow, tgt, pkb, own_c, own_d, gains, shifts, far_c) = refs[:10]
    (blob_d,) = refs[10:11]
    (wc_o, pt_o, q_o, v_o, kt_o, ot_o, wd_o, slope_o, h_o, r3_o, r4_o, n3_o, n4_o, y3_o,
     dec_o) = refs[11:26]
    (land_c, land_d, acc, n3, ylow, decl, k_s, qt_s, vt_s, ss, rs, cs) = refs[26:]
    t = pl.program_id(0)
    items = [(k, blob_d, land_d.at[k - 1]) for k in (1, 2, 3)]
    net = Gather(items, ss, rs, tensor)
    moves = [(n3, n3_o), (ylow, y3_o), (acc, n4_o), (decl, dec_o), (far_c, land_c)]

    def move(k):
        return pltpu.make_async_copy(*moves[k], cs.at[k])

    ev = net.plan(SECOND_PLAN)
    c_steps, d_steps = range(4), range(4, 8)

    @pl.when(t < 4)
    def _():
        pl.when(t == 0)(lambda: move(4).start())
        pl.when(t == 0)(net.barrier)
        run_events(t, c_steps, ev, -1)
        pl.when(t == 1)(lambda: move(4).wait())

        @pl.when(t == 0)
        def _():
            wc_o[0] = own_c[...]
            acc[...] = n2[...] * gains[2:3] + shifts[2:3]

        @pl.when(t > 0)
        def _():
            for m in range(4):
                piece = land_c[t - 1, :, m * 16 : (m + 1) * 16, :]
                wc_o[0, m * 128 : (m + 1) * 128] = piece.reshape(128, 512).astype(bf16)

        w = wc_o.at[0]

        def outs_of(m, b, nat, tr):
            rows = rows_at(b)
            if m == 0:
                return [(q_o.at[0, rows], nat * 0.125), (qt_s.at[:, rows], tr * 0.125)]
            if m == 1:
                return [(k_s.at[rows], nat), (kt_o.at[0, :, rows], tr)]
            return [(v_o.at[0, rows], nat), (vt_s.at[:, rows], tr)]

        project_slot(w, (0,), lambda b: qlow[rows_at(b)], outs_of)
        project_slot(w, (1, 2), lambda b: klow[rows_at(b)], outs_of)
        for b in range(4):
            rows = rows_at(b)
            keys = slice(0, 1024)
            pt = softmax_block(k_s, qt_s[:, rows], keys, wide(pkb[...]), tgt[:, rows])
            pt_o[0, b] = pt
            ot = mix_block(vt_s, keys, pt).astype(bf16)
            ot_o[0, :, rows] = ot
            acc[rows] += tn(ot, w[384:])
            run_events(t, c_steps, ev, b)

        @pl.when(t == 3)
        def _():
            finish_norm(acc, gains[3:4], shifts[3:4], n3, r3_o, ylow)
            move(0).start()
            move(1).start()

    @pl.when(t >= 4)
    def _():
        run_events(t, d_steps, ev, -1)

        @pl.when(t == 4)
        def _():
            wd_o[0] = own_d[...]
            acc[...] = n3[...] * gains[3:4] + shifts[3:4]

        @pl.when(t > 4)
        def _():
            for m in range(2):
                piece = land_d[t - 5, :, m * 64 : (m + 1) * 64, :]
                wd_o[0, m] = piece.reshape(512, 512).astype(bf16)

        ffn_slot(wd_o.at[0], ylow, acc, slope_o, h_o, t == 4,
                 lambda b: run_events(t, d_steps, ev, b))

        @pl.when(t == 7)
        def _():
            finish_norm(acc, gains[4:5], shifts[4:5], acc, r4_o, decl)
            move(2).start()
            move(3).start()
            for k in range(4):
                move(k).wait()
            net.finish()


def call_second(tensor, n2, qlow, klow, tgt, pkb, own_c, own_d, gains, shifts, land_c, blob_d):
    def slot(t):
        return jnp.minimum(t, 3)

    def chunk(t):
        return jnp.maximum(t - 4, 0)

    def by_slot(*tail):
        return pl.BlockSpec((1,) + tail, lambda t: (slot(t),) + (0,) * len(tail))

    return pl.pallas_call(
        functools.partial(second_kernel, tensor),
        grid=(8,),
        in_specs=[
            held((1024, 512)), held((1024, 512)), held((1024, 512)), held((1, 1024)),
            held((1024, 128)), held((512, 512)), held((2, 512, 512)), held((5, 512)),
            held((5, 512)), ANY, ANY,
        ],
        out_specs=[
            by_slot(512, 512), by_slot(4, 1024, 512), by_slot(1024, 128), by_slot(1024, 128),
            by_slot(128, 1024), by_slot(128, 1024),
            pl.BlockSpec((1, 2, 512, 512), lambda t: (chunk(t), 0, 0, 0)),
            pl.BlockSpec((1024, 512), lambda t: (0, chunk(t))),
            kept((1024, 512)), kept((1024, 1)), kept((1024, 1)),
        ] + [ANY] * 4,
        out_shape=[
            SDS((4, 512, 512), bf16), SDS((4, 4, 1024, 512), bf16), SDS((4, 1024, 128), bf16),
            SDS((4, 1024, 128), bf16), SDS((4, 128, 1024), bf16), SDS((4, 128, 1024), bf16),
            SDS((4, 2, 512, 512), bf16), SDS((1024, 2048), bf16), SDS((1024, 512), bf16),
            SDS((1024, 1), f32), SDS((1024, 1), f32),
            SDS((1024, 512), f32), SDS((1024, 512), f32), SDS((1024, 512), bf16),
            SDS((1024, 512), bf16),
        ],
        scratch_shapes=[
            VM((3, 8, 64, 512), f32), VM((3, 8, 128, 512), f32), VM((1024, 512), f32),
            VM((1024, 512), f32), VM((1024, 512), bf16), VM((1024, 512), bf16),
            VM((1024, 128), bf16), VM((128, 1024), bf16), VM((128, 1024), bf16),
            pltpu.SemaphoreType.DMA((3, 10)), pltpu.SemaphoreType.DMA((3, 10)),
            pltpu.SemaphoreType.DMA((5,)),
        ],
        compiler_params=pltpu.CompilerParams(
            collective_id=2, has_side_effects=True, vmem_limit_bytes=VMEM_MB * MB
        ),
    )(n2, qlow, klow, tgt, pkb, own_c, own_d, gains, shifts, land_c, blob_d)


def column(row):
    return jnp.broadcast_to(row, (128, row.shape[1])).T


def prep_kernel(x_e, x_d, masked, embed, src, tgt, qkv_e, wo_e, qkv_s, wo_s, qkv_c, wo_c,
                w1_e, w2_e, w1_d, w2_d, lows, tlow, target, idx, pkb, src_c, mcol, own_es, own_c, own_f, own_d,
                blob_e, blob_s, blob_c, blob_f, blob_d, win):
    _, j = plane_index()
    head = pl.multiple_of(lax.rem(j, 2) * 64 + lax.div(j, 2) * 16, 16)
    unit = pl.multiple_of(j * 64, 64)
    for qkv, wo, own, blob in (
        (qkv_e, wo_e, own_es.at[0], blob_e),
        (qkv_s, wo_s, own_es.at[1], blob_s),
        (qkv_c, wo_c, own_c, blob_c),
    ):
        for m in range(3):
            own[m * 128 : (m + 1) * 128] = qkv[m].T
        own[384:] = wo[...]
        for m in range(4):
            piece = own[pl.ds(m * 128 + head, 16)]
            blob[m * 16 : (m + 1) * 16] = piece.astype(f32)
    for w1, w2, own, blob in ((w1_e, w2_e, own_f, blob_f), (w1_d, w2_d, own_d, blob_d)):
        own[0] = w1[...].T
        own[1] = w2[...]
        for m in range(2):
            blob[m * 64 : (m + 1) * 64] = own[m, pl.ds(unit, 64)].astype(f32)
    src_col, tgt_col = column(src[...]), column(tgt[...])
    pkb[0] = src_col
    src_c[...] = src_col
    pkb[1] = tgt_col
    idx[0] = src[...]
    idx[1] = tgt[...]
    m = column(masked[...])
    mcol[...] = m
    m4 = jnp.concatenate([m] * 4, axis=1)
    tv = jnp.where(m4 == 1, embed[...], x_d[...].astype(f32))
    target[...] = tv
    lows[0] = x_e[...]
    lows[1] = tv.astype(bf16)
    tlow[...] = tv.astype(bf16)
    s = src[...]
    for b in range(4):
        cut = tgt[:, b * BLK : (b + 1) * BLK]
        lo, hi = jnp.min(cut), jnp.max(cut)
        begin = jnp.sum((s < lo).astype(jnp.int32))
        end = jnp.sum((s <= hi).astype(jnp.int32))
        start = jnp.minimum(lax.div(begin, 128) * 128, 512)
        win[b] = start
        win[4 + b] = (end - start > 512).astype(jnp.int32)


def call_prep(*args):
    full = pl.BlockSpec(memory_space=pltpu.VMEM)
    return pl.pallas_call(
        prep_kernel,
        in_specs=[full] * len(args),
        out_specs=[full] * 16 + [SMEM_SPEC],
        out_shape=[
            SDS((2, 1024, 512), bf16), SDS((1024, 512), bf16), SDS((1024, 512), f32),
            SDS((2, 1, 1024), jnp.int32),
            SDS((2, 1024, 128), jnp.int32), SDS((1024, 128), jnp.int32),
            SDS((1024, 128), jnp.int32),
            SDS((2, 512, 512), bf16), SDS((512, 512), bf16), SDS((2, 512, 512), bf16),
            SDS((2, 512, 512), bf16), SDS((64, 512), f32), SDS((64, 512), f32),
            SDS((64, 512), f32), SDS((128, 512), f32), SDS((128, 512), f32),
            SDS((8,), jnp.int32),
        ],
        compiler_params=pltpu.CompilerParams(vmem_limit_bytes=VMEM_MB * MB),
    )(*args)


class PlaneSum:
    def __init__(self, parts, reds, outs, bufs, ss, rs, ls, far=False):
        self.far = far
        self.parts, self.reds, self.outs, self.bufs = parts, reds, outs, bufs
        self.ss, self.rs, self.ls = ss, rs, ls
        self.place, self.core, self.xn, self.yn, _ = neighbours(1)

    def copy(self, k, s):
        c, x, y = self.place
        h = self.reds[k].shape[0] // 2
        a, b = pl.ds(0, h), pl.ds(h, h)
        red = self.reds[k]
        if s < 5:
            got_c, held, got_a, got_b, got_a2, got_b2 = self.bufs[k]
            src, dst, dev = [
                lambda: (self.parts[k].at[:, :, 1 - c], got_c, self.core),
                lambda: (held.at[:, 1 - x, a], got_a, self.xn),
                lambda: (held.at[1 - y, :, b], got_b, self.yn),
                lambda: (held.at[1 - y, x, a], got_a2, self.yn),
                lambda: (held.at[y, 1 - x, b], got_b2, self.xn),
            ][s]()
        else:
            o = self.outs[k]
            src, dst, dev = [
                lambda: (red.at[a], o.at[y, x, c, a], self.yn),
                lambda: (red.at[b], o.at[y, x, c, b], self.xn),
                lambda: (o.at[:, x, c, a], o.at[:, x, c, a], self.xn),
                lambda: (o.at[y, :, c, b], o.at[y, :, c, b], self.yn),
                lambda: (o.at[:, :, c], o.at[:, :, c], self.core),
            ][s - 5]()
        return pltpu.make_async_remote_copy(
            src_ref=src, dst_ref=dst, send_sem=self.ss.at[k, s], recv_sem=self.rs.at[k, s],
            device_id=dev, device_id_type=MESH,
        )

    def local(self, k):
        c, x, y = self.place
        return pltpu.make_async_copy(self.reds[k], self.outs[k].at[y, x, c], self.ls.at[k])

    def halves(self, k):
        h = self.reds[k].shape[0] // 2
        return slice(0, h), slice(h, 2 * h)

    def each(self, act):
        def run():
            for k in range(len(self.reds)):
                act(k)

        return run

    def fetch(self, k):
        src = self.parts[k].at[:, :, self.place[0]]
        return pltpu.make_async_copy(src, self.bufs[k][1], self.ls.at[k])

    def p1(self):
        def act(k):
            self.copy(k, 0).start()
            if self.far:
                self.fetch(k).start()

        return self.each(act)

    def p2(self):
        def act(k):
            got_c, held = self.bufs[k][:2]
            self.copy(k, 0).wait_recv()
            if self.far:
                self.fetch(k).wait()
                held[...] += got_c[...]
            else:
                held[...] = self.parts[k][:, :, self.place[0]] + got_c[...]
            self.copy(k, 1).start()
            self.copy(k, 2).start()

        return self.each(act)

    def p3(self):
        def act(k):
            c, x, y = self.place
            a, b = self.halves(k)
            _, held, got_a, got_b, _, _ = self.bufs[k]
            self.copy(k, 1).wait_recv()
            held[:, x, a] += got_a[...]
            self.copy(k, 2).wait_recv()
            held[y, :, b] += got_b[...]
            self.copy(k, 3).start()
            self.copy(k, 4).start()

        return self.each(act)

    def p4(self):
        def act(k):
            c, x, y = self.place
            a, b = self.halves(k)
            _, held, _, _, got_a2, got_b2 = self.bufs[k]
            self.copy(k, 3).wait_recv()
            self.reds[k][a] = held[y, x, a] + got_a2[...]
            self.copy(k, 4).wait_recv()
            self.reds[k][b] = held[y, x, b] + got_b2[...]

        return self.each(act)

    def g1(self):
        def act(k):
            self.local(k).start()
            self.copy(k, 5).start()
            self.copy(k, 6).start()

        return self.each(act)

    def g2(self):
        def act(k):
            self.local(k).wait()
            self.copy(k, 5).wait_recv()
            self.copy(k, 6).wait_recv()
            self.copy(k, 7).start()
            self.copy(k, 8).start()

        return self.each(act)

    def g3(self):
        def act(k):
            self.copy(k, 7).wait_recv()
            self.copy(k, 8).wait_recv()
            self.copy(k, 9).start()

        return self.each(act)

    def g4(self):
        return self.each(lambda k: self.copy(k, 9).wait_recv())

    def sent(self, slots):
        def act(k):
            for s in slots:
                self.copy(k, s).wait_send()

        return self.each(act)


REDUCE, SPREAD = range(5), range(5, 10)


def sum_bufs(shapes):
    out = []
    for r, w in shapes:
        out += [VM((2, 2, r, w), f32), VM((2, 2, r, w), f32), VM((2, r // 2, w), f32),
                VM((2, r // 2, w), f32), VM((r // 2, w), f32), VM((r // 2, w), f32)]
    return out


def take_bufs(refs, count):
    return [refs[6 * k : 6 * k + 6] for k in range(count)], refs[6 * count :]


def sum_sems(count):
    return [pltpu.SemaphoreType.DMA((count, 10)), pltpu.SemaphoreType.DMA((count, 10)),
            pltpu.SemaphoreType.DMA((count,))]


def plane_barrier():
    _, core, xn, yn, _ = neighbours(1)
    barrier_with([core, xn, yn])


FFN_CHUNKS = [(64, 512), (64, 512)]
ATTN_CHUNKS = [(192, 128), (16, 512)]


def chunked(r, w):
    return (2, 2, 2, r, w)


def norm_back_all(dy, n, r, gain, gs_o, d_s, g_s):
    gs_o[...] = jnp.zeros_like(gs_o)
    for b in range(4):
        rows = rows_at(b)
        dyv, nv = dy(rows), n[rows]
        gs_o[0:1] += jnp.sum(dyv * nv, axis=0, keepdims=True)
        gs_o[1:2] += jnp.sum(dyv, axis=0, keepdims=True)
        d = layer_norm_back(dyv, nv, r[rows], gain)
        d_s[rows] = d
        g_s[rows] = d.astype(bf16)


def attend_slot(cross, win, w, pt, v, kt, q, ot, g_s, acc, dkey, scratch, tick):
    do_s, dot_s, dk_s, dv_s, dqt_s = scratch
    for b in range(4):
        rows = rows_at(b)
        do_s[rows] = nt(g_s[rows], w[0, 384:]).astype(bf16)
        dot_s[:, rows] = nt(w[0, 384:], g_s[rows]).astype(bf16)
    dk_s[...] = jnp.zeros_like(dk_s)
    dv_s[...] = jnp.zeros_like(dv_s)

    def block(b, start, width):
        rows = rows_at(b)
        keys = pl.ds(start, width)
        prow = keys if cross else slice(None)
        prod = dot_s[:, rows].astype(f32) * ot[0, :, rows].astype(f32)
        delta = jnp.concatenate(
            [jnp.sum(prod[:64], axis=0, keepdims=True), jnp.sum(prod[64:], axis=0, keepdims=True)],
            axis=1,
        )
        dpt = nn(v[0, keys], block_diag(dot_s[:64, rows], dot_s[64:, rows]))
        ptv = pt[0, b, prow]
        dst = (ptv.astype(f32) * (dpt - delta)).astype(bf16)
        dv_s[keys] += nn(ptv, two_heads(do_s[rows]))
        dk_s[keys] += nn(dst, two_heads(q[0, rows]))
        dqt_s[:64, rows] = (nn(kt[0, :64, keys], dst[:, :BLK]) * 0.125).astype(bf16)
        dqt_s[64:, rows] = (nn(kt[0, 64:, keys], dst[:, BLK:]) * 0.125).astype(bf16)

    for b in range(4):
        if cross:
            start = pl.multiple_of(win[b], 128)
            pl.when(win[4 + b] == 0)(lambda b=b, start=start: block(b, start, 512))
            pl.when(win[4 + b] != 0)(lambda b=b: block(b, 0, 1024))
        else:
            block(b, self_start(b), 512)
        tick(b)
    for b in range(4):
        rows = rows_at(b)
        dkb, dvb = dk_s[rows].astype(bf16), dv_s[rows].astype(bf16)
        kv = jnp.concatenate([dkb, dvb], axis=1)
        acc[rows] += tn(dqt_s[:, rows], w[0, :128])
        if cross:
            dkey[rows] += nn(kv, w[0, 128:384])
        else:
            acc[rows] += nn(kv, w[0, 128:384])


def attend_weights(dqkv_o, dwo_o, ot, g_s, alow, blow, scratch):
    _, _, dk_s, dv_s, dqt_s = scratch

    def put(m, val):
        dqkv_o[:, :, :, m * 64 : (m + 1) * 64] = val.T.reshape(2, 2, 2, 64, 128)

    put(0, nn(dqt_s[...], alow[...]))
    put(1, tn(dk_s[...].astype(bf16), blow[...]))
    put(2, tn(dv_s[...].astype(bf16), blow[...]))
    dwo_o[...] = nn(ot[0], g_s[...]).reshape(2, 2, 2, 16, 512)


ATTN_SCRATCH = [
    VM((1024, 128), bf16), VM((128, 1024), bf16), VM((1024, 128), f32), VM((1024, 128), f32),
    VM((128, 1024), bf16),
]


def cross_bwd_kernel(*refs):
    (win, dy, n, r, gains, w, pt, v, kt, q, ot, alow, blow, dec_low) = refs[:14]
    acc, dkey, dqkv_o, dwo_o, gs_o, enc_o, dec_o, g_s, dec_s, cs = refs[14:24]
    scratch = refs[24:]
    p = pl.program_id(0)
    moves = [(dec_low, dec_s), (dec_s, dec_o), (blow, enc_o)]

    def move(k):
        return pltpu.make_async_copy(*moves[k], cs.at[k])

    @pl.when(p == 0)
    def _():
        move(0).start()
        move(2).start()

    @pl.when(p == 2)
    def _():
        move(0).wait()
        move(1).start()

    @pl.when(p == 3)
    def _():
        move(1).wait()
        move(2).wait()

    @pl.when(p == 0)
    def _():
        norm_back_all(lambda rows: dy[rows], n, r, gains[3:4], gs_o, acc, g_s)
        dkey[...] = jnp.zeros_like(dkey)

    attend_slot(True, win, w, pt, v, kt, q, ot, g_s, acc, dkey, scratch, lambda b: None)

    @pl.when(p == 0)
    def _():
        attend_weights(dqkv_o, dwo_o, ot, g_s, alow, blow, scratch)


def call_cross_bwd(win, dy, n, r, gains, saved, alow, blow, dec_low):
    w, pt, q, v, kt, ot = saved
    a, b = [chunked(*s) for s in ATTN_CHUNKS]

    def by_slot(*tail):
        return pl.BlockSpec((1,) + tail, lambda t: (t,) + (0,) * len(tail))

    return pl.pallas_call(
        cross_bwd_kernel,
        grid=(4,),
        in_specs=[
            SMEM_SPEC, held((1024, 512)), held((1024, 512)), held((1024, 1)), held((5, 512)),
            by_slot(512, 512), by_slot(4, 1024, 512), by_slot(1024, 128), by_slot(128, 1024),
            by_slot(1024, 128), by_slot(128, 1024), held((1024, 512)), held((1024, 512)), ANY,
        ],
        out_specs=[kept((1024, 512)), kept((1024, 512)), kept(a), kept(b), kept((8, 512)), ANY, ANY],
        out_shape=[SDS((1024, 512), f32), SDS((1024, 512), f32), SDS(a, f32), SDS(b, f32),
                   SDS((8, 512), f32), SDS((1024, 512), bf16), SDS((1024, 512), bf16)],
        scratch_shapes=[VM((1024, 512), bf16), VM((1024, 512), bf16), pltpu.SemaphoreType.DMA((3,))]
        + ATTN_SCRATCH,
        compiler_params=pltpu.CompilerParams(vmem_limit_bytes=VMEM_MB * MB),
    )(win, dy, n, r, gains, w, pt, v, kt, q, ot, alow, blow, dec_low)


def ffn_back_slot(w, slope, g_s, db_s, acc, tick):
    for b in range(4):
        rows = rows_at(b)
        db = (nt(g_s[rows], w[0, 1]) * slope[rows].astype(f32)).astype(bf16)
        db_s[rows] = db
        acc[rows] += nn(db, w[0, 0])
        tick(b)


def ffn_weights(dw1_o, dw2_o, alow, db_s, h, g_s):
    dw1_o[...] = tn(alow[...], db_s[...]).reshape(2, 2, 2, 64, 512)
    dw2_o[...] = tn(h[...], g_s[...]).reshape(2, 2, 2, 64, 512)


def dec_ffn_bwd_kernel(dy, n, r, gains, alow, w, h, slope, acc, gs_o, dw1_o, dw2_o, g_s, db_s):
    c = pl.program_id(0)

    @pl.when(c == 0)
    def _():
        norm_back_all(lambda rows: dy[rows].astype(f32), n, r, gains[4:5], gs_o, acc, g_s)

    ffn_back_slot(w, slope, g_s, db_s, acc, lambda b: None)

    @pl.when(c == 0)
    def _():
        ffn_weights(dw1_o, dw2_o, alow, db_s, h, g_s)


def call_dec_ffn_bwd(dy, n, r, gains, alow, w, h, slope):
    shapes = [chunked(*s) for s in FFN_CHUNKS]
    return pl.pallas_call(
        dec_ffn_bwd_kernel,
        grid=(4,),
        in_specs=[
            held((1024, 512)), held((1024, 512)), held((1024, 1)), held((5, 512)),
            held((1024, 512)), pl.BlockSpec((1, 2, 512, 512), lambda t: (t, 0, 0, 0)),
            held((1024, 512)), pl.BlockSpec((1024, 512), lambda t: (0, t)),
        ],
        out_specs=[kept((1024, 512)), kept((8, 512))] + [kept(s) for s in shapes],
        out_shape=[SDS((1024, 512), f32), SDS((8, 512), f32)] + [SDS(s, f32) for s in shapes],
        scratch_shapes=[VM((1024, 512), bf16), VM((1024, 512), bf16)],
        compiler_params=pltpu.CompilerParams(vmem_limit_bytes=VMEM_MB * MB),
    )(dy, n, r, gains, alow, w, h, slope)


def last_of(t):
    kind = jnp.where((t == 0) | ((t >= 6) & (t <= 8)), 1, 0)
    block = jnp.where(t < 5, 4, jnp.where(t == 5, 0, jnp.where(t < 9, t - 1, t - 8)))
    return kind, block


def last_kernel(*refs):
    n2, r2, gains, alow_s, mcol, gs3, gs4 = refs[:7]
    w, pt, v, kt, q, ot, wf, slope = refs[7:15]
    far, refs = refs[15:24], refs[24:]
    x_far, parts_d, parts_c, refs = refs[0], refs[1:3], refs[3:5], refs[5:]
    mask_o, gain_o, shift_o, dec_o, enc_o, refs = *refs[:5], refs[5:]
    outs = [refs[2 * k : 2 * k + 2] for k in range(5)]
    refs = refs[10:]
    acc2, n1, r1, cot, alow_f, h, n0, r0, x_e, refs = *refs[:9], refs[9:]
    gs0, gs1, gs2, g2, db_s, small, got, refs = *refs[:7], refs[7:]
    scratch, refs = refs[:5], refs[5:]
    dws, refs = [None, None, refs[:2], refs[2:4], refs[4:6]], refs[6:]
    ls, ss, rs, refs = refs[0], refs[1], refs[2], refs[3:]
    sums = []
    for k, chunks in enumerate((FFN_CHUNKS, ATTN_CHUNKS, ATTN_CHUNKS, FFN_CHUNKS, ATTN_CHUNKS)):
        reds, refs = refs[:2], refs[2:]
        bufs, refs = take_bufs(refs, 2)
        parts = (parts_d, parts_c, *dws[2:])[k]
        sums.append(PlaneSum(parts, reds, outs[k], bufs, *refs[:3], far=k < 2))
        refs = refs[3:]
    d, c, s, f, e = sums
    loads = list(zip(far, (acc2.at[1], acc2.at[0], n1, r1, cot, alow_f, h, n0, r0)))
    loads += [(x_far, x_e), (acc2.at[1], dec_o), (acc2.at[0], enc_o)]
    t = pl.program_id(0)
    kind, _ = last_of(t)

    def load(k):
        return pltpu.make_async_copy(*loads[k], ls.at[k])

    _, core, xn, yn, _ = neighbours(1)

    def swap(k):
        return pltpu.make_async_remote_copy(
            src_ref=small.at[k], dst_ref=got.at[k], send_sem=ss.at[k], recv_sem=rs.at[k],
            device_id=(core, xn, yn)[k], device_id_type=MESH,
        )

    def small_first():
        small[0] = jnp.zeros_like(small[0])
        small[0, 0:1] = gs2[2:3]
        for k, g in enumerate((gs0, gs1, gs2, gs3, gs4)):
            small[0, 1 + k : 2 + k] = g[0:1]
            small[0, 6 + k : 7 + k] = g[1:2]
        swap(0).start()

    def small_next(k):
        def run():
            swap(k).wait_recv()
            small[k + 1] = small[k] + got[k]
            if k < 2:
                swap(k + 1).start()

        return run

    def small_last():
        mask_o[...] = small[3, 0:1]
        gain_o[...] = small[3, 1:6]
        shift_o[...] = small[3, 6:11]
        for k in range(3):
            swap(k).wait_send()

    def end():
        for x in sums:
            x.sent(REDUCE)()
            x.sent(SPREAD)()

    ev = {
        (0, -1): [plane_barrier, d.p1(), c.p1()],
        (0, 1): [d.p2()],
        (0, 2): [c.p2()],
        (0, 4): [s.p1()],
        (1, 0): [d.p3()],
        (1, 2): [c.p3()],
        (1, 4): [f.p1(), s.p2()],
        (2, 1): [d.p4(), d.g1()],
        (2, 3): [f.p2()],
        (3, 0): [c.p4(), c.g1()],
        (3, 2): [d.g2()],
        (4, 0): [s.p3()],
        (4, 2): [f.p3()],
        (5, 0): [c.g2()],
        (5, 1): [d.g3()],
        (5, 2): [s.p4(), s.g1()],
        (5, 4): [e.p1()],
        (6, 0): [f.p4(), f.g1()],
        (6, 1): [c.g3()],
        (6, 2): [e.p2()],
        (7, 0): [s.g2()],
        (7, 1): [d.g4()],
        (7, 2): [f.g2()],
        (8, 0): [e.p3()],
        (8, 1): [c.g4()],
        (8, 2): [s.g3()],
        (8, 4): [small_first],
        (9, 0): [e.p4(), e.g1()],
        (9, 1): [f.g3()],
        (9, 2): [small_next(0)],
        (10, 0): [e.g2()],
        (10, 1): [small_next(1)],
        (10, 2): [s.g4()],
        (11, 0): [e.g3()],
        (11, 1): [small_next(2)],
        (11, 2): [f.g4()],
    }
    attn_steps, ffn_steps = (0, 5, 6, 7, 8, 9, 10, 11), (1, 2, 3, 4)

    @pl.when((t == 0) | (t > 4))
    def _():
        @pl.when(t == 0)
        def _():
            for k in range(10):
                load(k).start()
            load(0).wait()

        run_events(t, attn_steps, ev, -1)

        @pl.when(t == 0)
        def _():
            a = acc2.at[1]
            norm_back_all(lambda rows: a[rows], n2, r2, gains[2:3], gs2, a, g2.at[1])

        @pl.when(t == 5)
        def _():
            for k in (7, 8, 9):
                load(k).wait()
            a = acc2.at[0]
            norm_back_all(lambda rows: a[rows], n0, r0, gains[0:1], gs0, a, g2.at[0])

        attend_slot(False, None, w, pt, v, kt, q, ot, g2.at[kind], acc2.at[kind], None, scratch,
                    lambda b: run_events(t, attn_steps, ev, b))

        @pl.when(t == 0)
        def _():
            attend_weights(*dws[2], ot, g2.at[1], alow_s, alow_s, scratch)

        @pl.when(t == 5)
        def _():
            attend_weights(*dws[4], ot, g2.at[0], x_e, x_e, scratch)

        @pl.when(t == 8)
        def _():
            total = jnp.zeros((1, 512), f32)
            for b in range(4):
                rows = rows_at(b)
                hit = jnp.concatenate([mcol[rows]] * 4, axis=1) == 1
                dx = acc2[1, rows]
                total += jnp.sum(jnp.where(hit, dx, 0.0), axis=0, keepdims=True)
                acc2[1, rows] = jnp.where(hit, 0.0, dx)
            gs2[2:3] = total
            load(10).start()

        run_events(t, attn_steps, ev, 4)

        @pl.when(t == 11)
        def _():
            load(11).start()
            e.g4()()
            small_last()
            end()
            load(10).wait()
            load(11).wait()

    @pl.when((t > 0) & (t < 5))
    def _():
        @pl.when(t == 1)
        def _():
            for k in range(1, 7):
                load(k).wait()
            a = acc2.at[0]
            norm_back_all(lambda rows: a[rows] + cot[rows].astype(f32), n1, r1, gains[1:2], gs1, a,
                          g2.at[0])

        ffn_back_slot(wf, slope, g2.at[0], db_s, acc2.at[0],
                      lambda b: run_events(t, ffn_steps, ev, b))

        @pl.when(t == 1)
        def _():
            ffn_weights(*dws[3], alow_f, db_s, h, g2.at[0])

        run_events(t, ffn_steps, ev, 4)


def call_last(n2, r2, gains, alow_s, mcol, gs3, gs4, saved, wf, slope, far, parts_d, parts_c):
    w, pt, q, v, kt, ot = saved
    groups = (FFN_CHUNKS, ATTN_CHUNKS, ATTN_CHUNKS, FFN_CHUNKS, ATTN_CHUNKS)

    def by_es(*tail):
        return pl.BlockSpec((1,) + tail, lambda t: (last_of(t)[1],) + (0,) * len(tail))

    def chunk(t):
        return jnp.clip(t - 1, 0, 3)

    net = []
    for g in groups:
        net += [VM(s, f32) for s in g] + sum_bufs(g) + sum_sems(2)
    results = [chunked(*s) for g in groups for s in g]
    return pl.pallas_call(
        last_kernel,
        grid=(12,),
        in_specs=[
            held((1024, 512)), held((1024, 1)), held((5, 512)), held((1024, 512)),
            held((1024, 128)), held((8, 512)), held((8, 512)), by_es(512, 512),
            by_es(4, 512, 512), by_es(1024, 128), by_es(128, 1024), by_es(1024, 128),
            by_es(128, 1024), pl.BlockSpec((1, 2, 512, 512), lambda t: (chunk(t), 0, 0, 0)),
            pl.BlockSpec((1024, 512), lambda t: (0, chunk(t))),
        ] + [ANY] * 14,
        out_specs=[kept((1, 512)), kept((5, 512)), kept((5, 512))] + [ANY] * 12,
        out_shape=[SDS((1, 512), f32), SDS((5, 512), f32), SDS((5, 512), f32),
                   SDS((1024, 512), f32), SDS((1024, 512), f32)] + [SDS(s, f32) for s in results],
        scratch_shapes=[
            VM((2, 1024, 512), f32), VM((1024, 512), f32), VM((1024, 1), f32), VM((1024, 512), bf16),
            VM((1024, 512), bf16), VM((1024, 512), bf16), VM((1024, 512), f32), VM((1024, 1), f32),
            VM((1024, 512), bf16), VM((8, 512), f32), VM((8, 512), f32), VM((8, 512), f32),
            VM((2, 1024, 512), bf16), VM((1024, 512), bf16), VM((4, 16, 512), f32),
            VM((3, 16, 512), f32),
        ] + ATTN_SCRATCH + [VM(chunked(*s), f32) for g in groups[2:] for s in g]
        + [pltpu.SemaphoreType.DMA((12,)), pltpu.SemaphoreType.DMA((3,)),
           pltpu.SemaphoreType.DMA((3,))] + net,
        compiler_params=pltpu.CompilerParams(
            collective_id=3, has_side_effects=True, vmem_limit_bytes=VMEM_MB * MB
        ),
    )(n2, r2, gains, alow_s, mcol, gs3, gs4, w, pt, v, kt, q, ot, wf, slope, *far, *parts_d,
      *parts_c)


def deliver_kernel(count, *refs):
    srcs, dsts, bufs = refs[:count], refs[count : 2 * count], refs[2 * count : 3 * count]
    ins, outs = refs[3 * count :]

    def load(k):
        return pltpu.make_async_copy(srcs[k], bufs[k], ins.at[k])

    def store(k):
        if len(dsts[k].shape) < 6:
            return [pltpu.make_async_copy(bufs[k], dsts[k], outs.at[k, 0])]
        return [
            pltpu.make_async_copy(bufs[k].at[:, :, :, pl.ds(m * 64, 64)], dsts[k].at[m], outs.at[k, m])
            for m in range(3)
        ]

    for k in range(count):
        load(k).start()
    for k in range(count):
        load(k).wait()
        for c in store(k):
            c.start()
    for k in range(count):
        for c in store(k):
            c.wait()


def deliver(arrays):
    shapes = [(3, 2, 2, 2, 64, 128) if a.shape[-1] == 128 else a.shape for a in arrays]
    count = len(arrays)
    return pl.pallas_call(
        functools.partial(deliver_kernel, count),
        in_specs=[ANY] * count,
        out_specs=[ANY] * count,
        out_shape=[SDS(s, a.dtype) for s, a in zip(shapes, arrays)],
        scratch_shapes=[VM(a.shape, a.dtype) for a in arrays]
        + [pltpu.SemaphoreType.DMA((count,)), pltpu.SemaphoreType.DMA((count, 3))],
        compiler_params=pltpu.CompilerParams(vmem_limit_bytes=VMEM_MB * MB),
    )(*arrays)


def per_device(planes, tensor, enc_in, dec_in, src_idx, tgt_idx, masked, mask_embed, enc_qkv,
               enc_out_w, enc_w1, enc_w2, self_qkv, self_out_w, cross_qkv, cross_out_w, dec_w1,
               dec_w2, gains, shifts, enc_cot, dec_cot):
    (lows, target_low, target, idx, pkb, src_col, mcol, own_es, own_c, own_f, own_d, blob_e, blob_s, blob_c, blob_f,
     blob_d, win) = call_prep(
        enc_in[0], dec_in[0], masked, mask_embed[None], src_idx, tgt_idx, enc_qkv, enc_out_w,
        self_qkv, self_out_w, cross_qkv, cross_out_w, enc_w1, enc_w2, dec_w1, dec_w2)
    (w_es, pt_es, q_es, v_es, kt_es, ot_es, w_f, slope_e, h_e, r0, r2, r1, n0, n2, n1, first_low,
     second_low, enc_low, land_c) = call_first(
        tensor, lows, target, idx, pkb, own_es, own_f, gains, shifts,
        (blob_e, blob_s, blob_f, blob_c))
    (w_c, pt_c, q_c, v_c, kt_c, ot_c, w_d, slope_d, h_d, r3, r4, n3, n4, third_low,
     dec_low) = call_second(
        tensor, n2, second_low, enc_low, tgt_idx, src_col, own_c, own_d, gains, shifts, land_c, blob_d)
    save_es = (w_es, pt_es, q_es, v_es, kt_es, ot_es)
    save_c = (w_c, pt_c, q_c, v_c, kt_c, ot_c)

    d_third, gs4, *parts_d = call_dec_ffn_bwd(
        dec_cot[0], n4, r4, gains, third_low, w_d, h_d, slope_d)
    d_second, d_key, *parts_c, gs3, enc_out, dec_out = call_cross_bwd(
        win, d_third, n3, r3, gains, save_c, second_low, enc_low, dec_low)
    far = (d_second, d_key, n1, r1, enc_cot[0], first_low, h_e, n0, r0, enc_in[0])
    (mask_grad, gain_grad, shift_grad, dec_grad, d_enc, dw1_d, dw2_d, dqkv_c, dwo_c, dqkv_s, dwo_s,
     dw1_e, dw2_e, dqkv_e, dwo_e) = call_last(
        n2, r2, gains, target_low, mcol, gs3, gs4, save_es, w_f, slope_e, far, parts_d, parts_c)

    sums = (mask_grad, gain_grad, shift_grad, dqkv_e, dwo_e, dw1_e, dw2_e, dqkv_s, dwo_s, dqkv_c,
            dwo_c, dw1_d, dw2_d)
    if planes > 1:
        same = [[p * 8 + k for p in range(planes)] for k in range(8)]
        sums = lax.psum(sums, "dp", axis_index_groups=same)
    d_enc, dec_grad, mask_grad, gain_grad, shift_grad, *mats = deliver([d_enc, dec_grad, *sums])
    mats = [m.reshape(3, 512, 128) if m.ndim == 6 else m.reshape(-1, 512) for m in mats]
    return (enc_out[None], dec_out[None], d_enc[None], dec_grad[None], mask_grad[0], *mats,
            gain_grad, shift_grad)


def solution(mesh):
    tokens, index = P("dp", None, None), P("dp", None)
    qkv, cols, rows = P(None, None, "tensor"), P(None, "tensor"), P("tensor", None)
    weights = (qkv, rows, cols, rows, qkv, rows, qkv, rows, cols, rows)
    return jax.shard_map(
        functools.partial(per_device, mesh.shape["dp"] // 8, mesh.shape["tensor"]),
        mesh=mesh,
        in_specs=(tokens, tokens, index, index, index, P()) + weights + (P(), P(), tokens, tokens),
        out_specs=(tokens,) * 4 + (P(),) + weights + (P(), P()),
        check_vma=False,
    )
```

```python
import functools

import jax
import jax.numpy as jnp
from jax import lax
from jax.experimental import pallas as pl
from jax.experimental.pallas import tpu as pltpu
from jax.sharding import PartitionSpec as P

f32, bf16 = jnp.float32, jnp.bfloat16
HEAD_DIM = 64
EPS = 1e-05
FLOOR = -1000000000.0
BLK = 256
MB = 1 << 20
VMEM_MB = 60
MESH = pl.DeviceIdType.MESH
VM = pltpu.VMEM


def nt(a, b):
    return lax.dot_general(a, b, (((1,), (1,)), ((), ())), preferred_element_type=f32)


def nn(a, b):
    return lax.dot_general(a, b, (((1,), (0,)), ((), ())), preferred_element_type=f32)


def tn(a, b):
    return lax.dot_general(a, b, (((0,), (0,)), ((), ())), preferred_element_type=f32)


def layer_norm(v):
    c = v - jnp.mean(v, axis=-1, keepdims=True)
    r = lax.rsqrt(jnp.mean(c * c, axis=-1, keepdims=True) + EPS)
    return c * r, r


def layer_norm_back(dy, n, r, gain):
    dn = dy * gain
    m1 = jnp.mean(dn, axis=-1, keepdims=True)
    m2 = jnp.mean(dn * n, axis=-1, keepdims=True)
    return r * (dn - m1 - n * m2)


def block_diag(a, b):
    z = jnp.zeros_like(a)
    return jnp.concatenate(
        [jnp.concatenate([a, z], axis=1), jnp.concatenate([z, b], axis=1)], axis=0
    )


def two_heads(x):
    lane = lax.broadcasted_iota(jnp.int32, x.shape, 1)
    z = jnp.zeros_like(x)
    return jnp.concatenate([jnp.where(lane < HEAD_DIM, x, z), jnp.where(lane < HEAD_DIM, z, x)], 0)


def rows_at(b):
    return slice(b * BLK, (b + 1) * BLK)


def self_start(b):
    return min(max(b * BLK - 128, 0), 512)


def project_slot(w, kinds, get, rows_out):
    for b in range(4):
        xb = get(b)
        nat = nt(xb, w[kinds[0] * 128 : kinds[-1] * 128 + 128])
        tr = nt(w[kinds[0] * 128 : kinds[-1] * 128 + 128], xb)
        for k, kind in enumerate(kinds):
            cut = slice(k * 128, k * 128 + 128)
            for dst, val in rows_out(kind, b, nat[:, cut], tr[cut]):
                dst[...] = val.astype(bf16)


def softmax_block(k_s, koh, mq, qt):
    lhs = jnp.concatenate([k_s, koh], axis=1)
    rhs = jnp.concatenate([block_diag(qt[:64], qt[64:]), jnp.concatenate([mq, mq], axis=1)], axis=0)
    s = nn(lhs, rhs)
    e = jnp.exp(s - jnp.max(s, axis=0, keepdims=True))
    return (e * (1.0 / jnp.sum(e, axis=0, keepdims=True))).astype(bf16)


def mix_block(vt_s, keys, pt):
    return jnp.concatenate([nn(vt_s[:64, keys], pt[:, :BLK]), nn(vt_s[64:, keys], pt[:, BLK:])], 0)


def ffn_slot(w, al, acc, slope_o, h_o, first, tick):
    for b in range(4):
        rows = rows_at(b)
        before = nt(al[rows], w[0])
        cdf = 0.5 + 0.5 * lax.erf(before * (0.5**0.5))
        pdf = jnp.exp(before * before * -0.5) * 0.3989422804014327
        slope_o[rows] = (cdf + before * pdf).astype(bf16)
        hidden = (before * cdf).astype(bf16)

        @pl.when(first)
        def _():
            h_o[rows] = hidden

        acc[rows] += nn(hidden, w[1])
        tick(b)


def finish_norm(acc, gain, shift, n_ref, r_o, y_ref):
    for b in range(4):
        rows = rows_at(b)
        n, r = layer_norm(acc[rows])
        n_ref[rows] = n
        r_o[rows] = r
        y_ref[rows] = (n * gain + shift).astype(bf16)


def plane_index():
    dp = lax.axis_index("dp")
    return dp, lax.rem(dp, 8)


def neighbours(tensor):
    dp, j = plane_index()
    z = lax.axis_index("tensor")
    c, x, y = lax.rem(j, 2), lax.rem(lax.div(j, 2), 2), lax.div(j, 4)
    core, xn, yn = (dp + 1 - 2 * c, z), (dp + 2 - 4 * x, z), (dp + 4 - 8 * y, z)
    down = {k: (dp, lax.rem(z + tensor - k, tensor)) for k in range(1, tensor)}
    return (c, x, y), core, xn, yn, down


def barrier_with(peers):
    sem = pltpu.get_barrier_semaphore()
    for peer in peers:
        pl.semaphore_signal(sem, inc=1, device_id=peer, device_id_type=MESH)
    pl.semaphore_wait(sem, len(peers))


class Gather:
    def __init__(self, items, ss, rs, tensor):
        assert tensor == 4
        self.items, self.ss, self.rs = items, ss, rs
        _, self.core, self.xn, self.yn, self.down = neighbours(tensor)
        self.dp, self.z = lax.axis_index("dp"), lax.axis_index("tensor")

    def barrier(self):
        barrier_with([self.core, self.xn, self.yn] + list(self.down.values()))

    def copy(self, t, s, src, dst, dev, r=None):
        return lambda: pltpu.make_async_remote_copy(
            src_ref=src, dst_ref=dst, send_sem=self.ss.at[t, s],
            recv_sem=self.rs.at[t, s if r is None else r], device_id=dev, device_id_type=MESH,
        )

    def along(self, t):
        rnd, src, land = self.items[t]
        z, dp = self.z, self.dp
        inner = (z == 1) | (z == 2)
        if rnd == 1:
            left, right = jnp.maximum(z - 1, 0), jnp.minimum(z + 1, 3)
            return [
                (inner, self.copy(t, 0, src, land.at[0], (dp, left), 0)),
                (inner, self.copy(t, 9, src, land.at[0], (dp, right), 0)),
            ], None
        if rnd == 2:
            return [(None, self.copy(t, 0, src, land.at[0], (dp, lax.rem(2 * z + 1, 5)), 0))], None
        outer = (z == 0) | (z == 3)
        to, on = jnp.where(z == 0, 2, 1), jnp.where(z == 1, 0, 3)
        return [(outer, self.copy(t, 0, src, land.at[0], (dp, to), 0))], (
            inner, self.copy(t, 9, land.at[0], land.at[0], (dp, on), 0))

    def make(self, t):
        land = self.items[t][2]
        half = land.shape[1] // 2
        a, b = pl.ds(0, half), pl.ds(half, half)
        return [
            self.copy(t, 0, land.at[0], land.at[0], self.down[1]),
            self.copy(t, 1, land.at[0], land.at[1], self.xn),
            self.copy(t, 2, land.at[0], land.at[2], self.yn),
            self.copy(t, 3, land.at[0], land.at[4], self.core),
            self.copy(t, 4, land.at[1, a], land.at[3, a], self.yn),
            self.copy(t, 5, land.at[1], land.at[5], self.core),
            self.copy(t, 6, land.at[2, b], land.at[3, b], self.xn),
            self.copy(t, 7, land.at[2], land.at[6], self.core),
            self.copy(t, 8, land.at[3], land.at[7], self.core),
        ]

    def send(self, t):
        for cond, c in self.along(t)[0]:
            if cond is None:
                c().start()
            else:
                pl.when(cond)(lambda c=c: c().start())

    def onward(self, t):
        inner, c = self.along(t)[1]

        @pl.when(inner)
        def _():
            self.make(t)[0]().wait_recv()
            c().start()

    def spread(self, t):
        c = self.make(t)
        if self.items[t][0] < 3:
            c[0]().wait_recv()
        else:
            pl.when((self.z == 0) | (self.z == 3))(lambda: c[0]().wait_recv())
        for k in (1, 2, 3):
            c[k]().start()

    def relay(self, t):
        c = self.make(t)
        c[1]().wait_recv()
        c[4]().start()
        c[5]().start()
        c[2]().wait_recv()
        c[6]().start()
        c[7]().start()

    def pair(self, t):
        c = self.make(t)
        c[4]().wait_recv()
        c[6]().wait_recv()
        c[8]().start()

    def done(self, t):
        c = self.make(t)
        for k in (3, 5, 7, 8):
            c[k]().wait_recv()

    def finish(self):
        for t in range(len(self.items)):
            first, on = self.along(t)
            for cond, c in first + ([on] if on else []):
                if cond is None:
                    c().wait_send()
                else:
                    pl.when(cond)(lambda c=c: c().wait_send())
            for c in self.make(t)[1:]:
                c().wait_send()

    def plan(self, text):
        acts = {"Z": self.send, "Y": self.onward, "S": self.spread, "R": self.relay, "P": self.pair, "D": self.done}
        ev = {}
        for step, point, *words in text:
            row = ev.setdefault((step, point), [])
            for word in words:
                row.append(functools.partial(acts[word[0]], int(word[1:])))
        return ev


FIRST_PLAN = (
    (0, -1, "Z2", "Z0", "Z1", "Z5", "Z3", "Z4", "Z8", "Z6", "Z7", "Z11",
     "Z9", "Z10"),
    (1, 0, "S0"),
    (1, 2, "S1", "Y2"),
    (2, -1, "R0", "S2", "S3", "R1", "P0", "S4", "Y5", "D0"),
    (2, 1, "R2"),
    (2, 2, "S5"),
    (2, 3, "R3"),
    (3, -1, "P1", "S6", "R4", "D1"),
    (3, 1, "P2"),
    (3, 3, "R5", "S7", "Y8"),
    (4, -1, "D2"),
    (4, 0, "P3"),
    (5, -1, "D3"),
    (5, 0, "R6"),
    (5, 1, "S8", "P4", "S9"),
    (5, 2, "P5"),
    (5, 3, "S10", "Y11"),
    (6, -1, "D4"),
    (6, 2, "R7"),
    (6, 3, "S11"),
    (7, -1, "D5"),
    (7, 0, "P6"),
    (8, 1, "R8"),
    (9, -1, "D6"),
    (9, 0, "R9"),
    (9, 3, "R10"),
    (10, -1, "P7", "D7"),
    (10, 1, "R11"),
    (11, -1, "P8", "P9", "P10", "D8"),
    (11, 2, "P11"),
    (11, 3, "D9", "D10", "D11"),
)
SECOND_PLAN = (
    (0, -1, "Z2", "Z0", "Z1"),
    (1, 0, "S0"),
    (1, 3, "Y2"),
    (2, 1, "R0"),
    (2, 2, "S1"),
    (3, 0, "P0"),
    (3, 1, "S2"),
    (3, 3, "R1"),
    (5, -1, "D0"),
    (5, 0, "R2"),
    (5, 3, "P1"),
    (6, -1, "D1"),
    (6, 2, "P2"),
    (7, -1, "D2"),
)


def run_events(t, steps, events, point):
    for step in steps:
        acts = events.get((step, point))
        if acts:

            @pl.when(t == step)
            def _(acts=acts):
                for act in acts:
                    act()


def es_of(t):
    kind = jnp.where((t == 1) | (t >= 5), 1, 0)
    p = jnp.where(t < 2, 0, jnp.where(t < 5, t - 1, t - 4))
    return kind, jnp.minimum(p, 3)


def es_block(t):
    kind, p = es_of(t)
    return kind * 4 + p


def first_kernel(tensor, *refs):
    (x_far, t_far, target, koh, mq, own_es, own_f, gains, shifts) = refs[:9]
    blob_e, blob_s, blob_f, blob_c = refs[9:13]
    (wes_o, pt_o, q_o, v_o, kt_o, ot_o, wf_o, slope_o, h_o, r0_o, r2_o, r1_o, n0_o, n2_o,
     n1_o, y0_o, y2_o, encl_o, zc_o) = refs[13:32]
    (lows, land_a, land_f, accs, na, ylow, encl, k_s, qt_s, vt_s, ss, rs, cs) = refs[32:]
    t = pl.program_id(0)
    items = [(k, blob_e, land_a.at[k - 1]) for k in (1, 2, 3)]
    items += [(k, blob_s, land_a.at[2 + k]) for k in (1, 2, 3)]
    items += [(k, blob_f, land_f.at[k - 1]) for k in (1, 2, 3)]
    items += [(k, blob_c, zc_o.at[k - 1]) for k in (1, 2, 3)]
    net = Gather(items, ss, rs, tensor)
    outs = [
        (na.at[0], n0_o), (ylow.at[0], y0_o), (na.at[1], n2_o), (ylow.at[1], y2_o),
        (accs.at[0], n1_o), (encl, encl_o), (x_far, lows.at[0]), (t_far, lows.at[1]),
        (target, accs.at[1]),
    ]

    def out(k):
        return pltpu.make_async_copy(*outs[k], cs.at[k])

    ev = net.plan(FIRST_PLAN)
    kind, p = es_of(t)
    es_steps, f_steps = range(8), range(8, 12)

    @pl.when(t < 8)
    def _():
        @pl.when(t == 0)
        def _():
            for k in (6, 7, 8):
                out(k).start()
            net.barrier()

        run_events(t, es_steps, ev, -1)
        pl.when(t == 0)(lambda: out(6).wait())

        @pl.when(t == 1)
        def _():
            out(7).wait()
            out(8).wait()


        @pl.when(p == 0)
        def _():
            wes_o[0] = own_es[kind]

        @pl.when((p == 0) & (kind == 0))
        def _():
            accs[0] = lows[0].astype(f32)

        @pl.when(p > 0)
        def _():
            for m in range(4):
                piece = land_a[kind * 3 + p - 1, :, m * 16 : (m + 1) * 16, :]
                wes_o[0, m * 128 : (m + 1) * 128] = piece.reshape(128, 512).astype(bf16)

        w = wes_o.at[0]

        def outs_of(m, b, nat, tr):
            rows = rows_at(b)
            if m == 0:
                return [(q_o.at[0, rows], nat * 0.125), (qt_s.at[:, rows], tr * 0.125)]
            if m == 1:
                return [(k_s.at[rows], nat), (kt_o.at[0, :, rows], tr)]
            return [(v_o.at[0, rows], nat), (vt_s.at[:, rows], tr)]

        project_slot(w, (0, 1, 2), lambda b: lows[kind, rows_at(b)], outs_of)
        for b in range(4):
            rows = rows_at(b)
            keys = slice(self_start(b), self_start(b) + 512)
            pt = softmax_block(k_s[keys], koh[kind, keys], mq[kind, :, rows], qt_s[:, rows])
            pt_o[0, b] = pt
            ot = mix_block(vt_s, keys, pt).astype(bf16)
            ot_o[0, :, rows] = ot
            accs[kind, rows] += tn(ot, w[384:])
            run_events(t, es_steps, ev, b)

        @pl.when(t == 4)
        def _():
            finish_norm(accs.at[0], gains[0:1], shifts[0:1], na.at[0], r0_o, ylow.at[0])
            out(0).start()
            out(1).start()

        @pl.when(t == 7)
        def _():
            finish_norm(accs.at[1], gains[2:3], shifts[2:3], na.at[1], r2_o, ylow.at[1])
            out(2).start()
            out(3).start()

    @pl.when(t >= 8)
    def _():
        run_events(t, f_steps, ev, -1)

        @pl.when(t == 8)
        def _():
            wf_o[0] = own_f[...]
            accs[0] = na[0] * gains[0:1] + shifts[0:1]

        @pl.when(t > 8)
        def _():
            for m in range(2):
                piece = land_f[t - 9, :, m * 64 : (m + 1) * 64, :]
                wf_o[0, m] = piece.reshape(512, 512).astype(bf16)

        ffn_slot(wf_o.at[0], ylow.at[0], accs.at[0], slope_o, h_o, t == 8,
                 lambda b: run_events(t, f_steps, ev, b))

        @pl.when(t == 11)
        def _():
            finish_norm(accs.at[0], gains[1:2], shifts[1:2], accs.at[0], r1_o, encl)
            out(4).start()
            out(5).start()
            for k in range(6):
                out(k).wait()
            net.finish()


def held(shape):
    return pl.BlockSpec(shape, lambda t: (0,) * len(shape), pipeline_mode=pl.Buffered(1))


def picked(k, *tail):
    return pl.BlockSpec((1,) + tail, lambda t: (k, 0, 0), pipeline_mode=pl.Buffered(1))


def kept(shape):
    return pl.BlockSpec(shape, lambda t: (0,) * len(shape))


ANY = pl.BlockSpec(memory_space=pl.ANY)
SMEM_SPEC = pl.BlockSpec(memory_space=pltpu.SMEM)
SDS = jax.ShapeDtypeStruct


def by_es(*tail):
    return pl.BlockSpec((1,) + tail, lambda t: (es_block(t),) + (0,) * len(tail))


def call_first(tensor, x_e, tlow, target, koh, mq, own_es, own_f, gains, shifts, blobs):
    def chunk(t):
        return jnp.maximum(t - 8, 0)

    n_items = 12
    return pl.pallas_call(
        functools.partial(first_kernel, tensor),
        grid=(12,),
        in_specs=[
            ANY, ANY, ANY, held((2, 1024, 128)), held((2, 128, 1024)),
            held((2, 512, 512)), held((2, 512, 512)), held((5, 512)), held((5, 512)),
        ] + [ANY] * 4,
        out_specs=[
            by_es(512, 512), by_es(4, 512, 512), by_es(1024, 128), by_es(1024, 128),
            by_es(128, 1024), by_es(128, 1024),
            pl.BlockSpec((1, 2, 512, 512), lambda t: (chunk(t), 0, 0, 0)),
            pl.BlockSpec((1024, 512), lambda t: (0, chunk(t))),
            kept((1024, 512)), kept((1024, 1)), kept((1024, 1)), kept((1024, 1)),
        ] + [ANY] * 7,
        out_shape=[
            SDS((8, 512, 512), bf16), SDS((8, 4, 512, 512), bf16), SDS((8, 1024, 128), bf16),
            SDS((8, 1024, 128), bf16), SDS((8, 128, 1024), bf16), SDS((8, 128, 1024), bf16),
            SDS((4, 2, 512, 512), bf16), SDS((1024, 2048), bf16), SDS((1024, 512), bf16),
            SDS((1024, 1), f32), SDS((1024, 1), f32), SDS((1024, 1), f32),
            SDS((1024, 512), f32), SDS((1024, 512), f32), SDS((1024, 512), f32),
            SDS((1024, 512), bf16), SDS((1024, 512), bf16), SDS((1024, 512), bf16), SDS((3, 8, 64, 512), f32),
        ],
        scratch_shapes=[
            VM((2, 1024, 512), bf16), VM((6, 8, 64, 512), f32), VM((3, 8, 128, 512), f32),
            VM((2, 1024, 512), f32),
            VM((2, 1024, 512), f32), VM((2, 1024, 512), bf16), VM((1024, 512), bf16),
            VM((1024, 128), bf16), VM((128, 1024), bf16), VM((128, 1024), bf16),
            pltpu.SemaphoreType.DMA((n_items, 10)), pltpu.SemaphoreType.DMA((n_items, 10)),
            pltpu.SemaphoreType.DMA((9,)),
        ],
        compiler_params=pltpu.CompilerParams(
            collective_id=0, has_side_effects=True, vmem_limit_bytes=VMEM_MB * MB
        ),
    )(x_e, tlow, target, koh, mq, own_es, own_f, gains, shifts, *blobs)


def second_kernel(tensor, *refs):
    (n2, qlow, klow, koh, mq, own_c, own_d, gains, shifts, far_c) = refs[:10]
    (blob_d,) = refs[10:11]
    (wc_o, pt_o, q_o, v_o, kt_o, ot_o, wd_o, slope_o, h_o, r3_o, r4_o, n3_o, n4_o, y3_o,
     dec_o) = refs[11:26]
    (land_c, land_d, acc, n3, ylow, decl, k_s, qt_s, vt_s, ss, rs, cs) = refs[26:]
    t = pl.program_id(0)
    items = [(k, blob_d, land_d.at[k - 1]) for k in (1, 2, 3)]
    net = Gather(items, ss, rs, tensor)
    moves = [(n3, n3_o), (ylow, y3_o), (acc, n4_o), (decl, dec_o), (far_c, land_c)]

    def move(k):
        return pltpu.make_async_copy(*moves[k], cs.at[k])

    ev = net.plan(SECOND_PLAN)
    c_steps, d_steps = range(4), range(4, 8)

    @pl.when(t < 4)
    def _():
        pl.when(t == 0)(lambda: move(4).start())
        pl.when(t == 0)(net.barrier)
        run_events(t, c_steps, ev, -1)
        pl.when(t == 1)(lambda: move(4).wait())

        @pl.when(t == 0)
        def _():
            wc_o[0] = own_c[...]
            acc[...] = n2[...] * gains[2:3] + shifts[2:3]

        @pl.when(t > 0)
        def _():
            for m in range(4):
                piece = land_c[t - 1, :, m * 16 : (m + 1) * 16, :]
                wc_o[0, m * 128 : (m + 1) * 128] = piece.reshape(128, 512).astype(bf16)

        w = wc_o.at[0]

        def outs_of(m, b, nat, tr):
            rows = rows_at(b)
            if m == 0:
                return [(q_o.at[0, rows], nat * 0.125), (qt_s.at[:, rows], tr * 0.125)]
            if m == 1:
                return [(k_s.at[rows], nat), (kt_o.at[0, :, rows], tr)]
            return [(v_o.at[0, rows], nat), (vt_s.at[:, rows], tr)]

        project_slot(w, (0,), lambda b: qlow[rows_at(b)], outs_of)
        project_slot(w, (1, 2), lambda b: klow[rows_at(b)], outs_of)
        for b in range(4):
            rows = rows_at(b)
            keys = slice(0, 1024)
            pt = softmax_block(k_s[...], koh[0], mq[0, :, rows], qt_s[:, rows])
            pt_o[0, b] = pt
            ot = mix_block(vt_s, keys, pt).astype(bf16)
            ot_o[0, :, rows] = ot
            acc[rows] += tn(ot, w[384:])
            run_events(t, c_steps, ev, b)

        @pl.when(t == 3)
        def _():
            finish_norm(acc, gains[3:4], shifts[3:4], n3, r3_o, ylow)
            move(0).start()
            move(1).start()

    @pl.when(t >= 4)
    def _():
        run_events(t, d_steps, ev, -1)

        @pl.when(t == 4)
        def _():
            wd_o[0] = own_d[...]
            acc[...] = n3[...] * gains[3:4] + shifts[3:4]

        @pl.when(t > 4)
        def _():
            for m in range(2):
                piece = land_d[t - 5, :, m * 64 : (m + 1) * 64, :]
                wd_o[0, m] = piece.reshape(512, 512).astype(bf16)

        ffn_slot(wd_o.at[0], ylow, acc, slope_o, h_o, t == 4,
                 lambda b: run_events(t, d_steps, ev, b))

        @pl.when(t == 7)
        def _():
            finish_norm(acc, gains[4:5], shifts[4:5], acc, r4_o, decl)
            move(2).start()
            move(3).start()
            for k in range(4):
                move(k).wait()
            net.finish()


def call_second(tensor, n2, qlow, klow, koh, mq, own_c, own_d, gains, shifts, land_c, blob_d):
    def slot(t):
        return jnp.minimum(t, 3)

    def chunk(t):
        return jnp.maximum(t - 4, 0)

    def by_slot(*tail):
        return pl.BlockSpec((1,) + tail, lambda t: (slot(t),) + (0,) * len(tail))

    return pl.pallas_call(
        functools.partial(second_kernel, tensor),
        grid=(8,),
        in_specs=[
            held((1024, 512)), held((1024, 512)), held((1024, 512)), picked(0, 1024, 128),
            picked(1, 128, 1024), held((512, 512)), held((2, 512, 512)), held((5, 512)),
            held((5, 512)), ANY, ANY,
        ],
        out_specs=[
            by_slot(512, 512), by_slot(4, 1024, 512), by_slot(1024, 128), by_slot(1024, 128),
            by_slot(128, 1024), by_slot(128, 1024),
            pl.BlockSpec((1, 2, 512, 512), lambda t: (chunk(t), 0, 0, 0)),
            pl.BlockSpec((1024, 512), lambda t: (0, chunk(t))),
            kept((1024, 512)), kept((1024, 1)), kept((1024, 1)),
        ] + [ANY] * 4,
        out_shape=[
            SDS((4, 512, 512), bf16), SDS((4, 4, 1024, 512), bf16), SDS((4, 1024, 128), bf16),
            SDS((4, 1024, 128), bf16), SDS((4, 128, 1024), bf16), SDS((4, 128, 1024), bf16),
            SDS((4, 2, 512, 512), bf16), SDS((1024, 2048), bf16), SDS((1024, 512), bf16),
            SDS((1024, 1), f32), SDS((1024, 1), f32),
            SDS((1024, 512), f32), SDS((1024, 512), f32), SDS((1024, 512), bf16),
            SDS((1024, 512), bf16),
        ],
        scratch_shapes=[
            VM((3, 8, 64, 512), f32), VM((3, 8, 128, 512), f32), VM((1024, 512), f32),
            VM((1024, 512), f32), VM((1024, 512), bf16), VM((1024, 512), bf16),
            VM((1024, 128), bf16), VM((128, 1024), bf16), VM((128, 1024), bf16),
            pltpu.SemaphoreType.DMA((3, 10)), pltpu.SemaphoreType.DMA((3, 10)),
            pltpu.SemaphoreType.DMA((5,)),
        ],
        compiler_params=pltpu.CompilerParams(
            collective_id=2, has_side_effects=True, vmem_limit_bytes=VMEM_MB * MB
        ),
    )(n2, qlow, klow, koh, mq, own_c, own_d, gains, shifts, land_c, blob_d)


def column(row):
    return jnp.broadcast_to(row, (128, row.shape[1])).T


def prep_kernel(x_d, masked, embed, src, tgt, qkv_e, wo_e, qkv_s, wo_s, qkv_c, wo_c,
                w1_e, w2_e, w1_d, w2_d, tlow, target, koh, mq, mcol, own_es, own_c, own_f, own_d,
                blob_e, blob_s, blob_c, blob_f, blob_d, win):
    _, j = plane_index()
    head = pl.multiple_of(lax.rem(j, 2) * 64 + lax.div(j, 2) * 16, 16)
    unit = pl.multiple_of(j * 64, 64)
    for qkv, wo, own, blob in (
        (qkv_e, wo_e, own_es.at[0], blob_e),
        (qkv_s, wo_s, own_es.at[1], blob_s),
        (qkv_c, wo_c, own_c, blob_c),
    ):
        for m in range(3):
            own[m * 128 : (m + 1) * 128] = qkv[m].T
        own[384:] = wo[...]
        for m in range(4):
            piece = own[pl.ds(m * 128 + head, 16)]
            blob[m * 16 : (m + 1) * 16] = piece.astype(f32)
    for w1, w2, own, blob in ((w1_e, w2_e, own_f, blob_f), (w1_d, w2_d, own_d, blob_d)):
        own[0] = w1[...].T
        own[1] = w2[...]
        for m in range(2):
            blob[m * 64 : (m + 1) * 64] = own[m, pl.ds(unit, 64)].astype(f32)
    for k, ids in enumerate((src[...], tgt[...])):
        lane = lax.broadcasted_iota(jnp.int32, (1024, 128), 1)
        koh[k] = jnp.where(column(ids) == lane, 1.0, 0.0).astype(bf16)
        pair = lax.broadcasted_iota(jnp.int32, (128, 1024), 0)
        mq[k] = jnp.where(ids == pair, 0.0, FLOOR).astype(bf16)
    m = column(masked[...])
    mcol[...] = m
    m4 = jnp.concatenate([m] * 4, axis=1)
    tv = jnp.where(m4 == 1, embed[...], x_d[...].astype(f32))
    target[...] = tv
    tlow[...] = tv.astype(bf16)
    s = src[...]
    for b in range(4):
        cut = tgt[:, b * BLK : (b + 1) * BLK]
        lo, hi = jnp.min(cut), jnp.max(cut)
        begin = jnp.sum((s < lo).astype(jnp.int32))
        end = jnp.sum((s <= hi).astype(jnp.int32))
        start = jnp.minimum(lax.div(begin, 128) * 128, 512)
        win[b] = start
        win[4 + b] = (end - start > 512).astype(jnp.int32)


def call_prep(*args):
    full = pl.BlockSpec(memory_space=pltpu.VMEM)
    return pl.pallas_call(
        prep_kernel,
        in_specs=[full] * len(args),
        out_specs=[full] * 14 + [SMEM_SPEC],
        out_shape=[
            SDS((1024, 512), bf16), SDS((1024, 512), f32), SDS((2, 1024, 128), bf16),
            SDS((2, 128, 1024), bf16), SDS((1024, 128), jnp.int32),
            SDS((2, 512, 512), bf16), SDS((512, 512), bf16), SDS((2, 512, 512), bf16),
            SDS((2, 512, 512), bf16), SDS((64, 512), f32), SDS((64, 512), f32),
            SDS((64, 512), f32), SDS((128, 512), f32), SDS((128, 512), f32),
            SDS((8,), jnp.int32),
        ],
        compiler_params=pltpu.CompilerParams(vmem_limit_bytes=VMEM_MB * MB),
    )(*args)


class PlaneSum:
    def __init__(self, parts, reds, outs, bufs, ss, rs, ls, far=False):
        self.far = far
        self.parts, self.reds, self.outs, self.bufs = parts, reds, outs, bufs
        self.ss, self.rs, self.ls = ss, rs, ls
        self.place, self.core, self.xn, self.yn, _ = neighbours(1)

    def copy(self, k, s):
        c, x, y = self.place
        h = self.reds[k].shape[0] // 2
        a, b = pl.ds(0, h), pl.ds(h, h)
        red = self.reds[k]
        if s < 5:
            got_c, held, got_a, got_b, got_a2, got_b2 = self.bufs[k]
            src, dst, dev = [
                lambda: (self.parts[k].at[:, :, 1 - c], got_c, self.core),
                lambda: (held.at[:, 1 - x, a], got_a, self.xn),
                lambda: (held.at[1 - y, :, b], got_b, self.yn),
                lambda: (held.at[1 - y, x, a], got_a2, self.yn),
                lambda: (held.at[y, 1 - x, b], got_b2, self.xn),
            ][s]()
        else:
            o = self.outs[k]
            src, dst, dev = [
                lambda: (red.at[a], o.at[y, x, c, a], self.yn),
                lambda: (red.at[b], o.at[y, x, c, b], self.xn),
                lambda: (o.at[:, x, c, a], o.at[:, x, c, a], self.xn),
                lambda: (o.at[y, :, c, b], o.at[y, :, c, b], self.yn),
                lambda: (o.at[:, :, c], o.at[:, :, c], self.core),
            ][s - 5]()
        return pltpu.make_async_remote_copy(
            src_ref=src, dst_ref=dst, send_sem=self.ss.at[k, s], recv_sem=self.rs.at[k, s],
            device_id=dev, device_id_type=MESH,
        )

    def local(self, k):
        c, x, y = self.place
        return pltpu.make_async_copy(self.reds[k], self.outs[k].at[y, x, c], self.ls.at[k])

    def halves(self, k):
        h = self.reds[k].shape[0] // 2
        return slice(0, h), slice(h, 2 * h)

    def each(self, act):
        def run():
            for k in range(len(self.reds)):
                act(k)

        return run

    def fetch(self, k):
        src = self.parts[k].at[:, :, self.place[0]]
        return pltpu.make_async_copy(src, self.bufs[k][1], self.ls.at[k])

    def p1(self):
        def act(k):
            self.copy(k, 0).start()
            if self.far:
                self.fetch(k).start()

        return self.each(act)

    def p2(self):
        def act(k):
            got_c, held = self.bufs[k][:2]
            self.copy(k, 0).wait_recv()
            if self.far:
                self.fetch(k).wait()
                held[...] += got_c[...]
            else:
                held[...] = self.parts[k][:, :, self.place[0]] + got_c[...]
            self.copy(k, 1).start()
            self.copy(k, 2).start()

        return self.each(act)

    def p3(self):
        def act(k):
            c, x, y = self.place
            a, b = self.halves(k)
            _, held, got_a, got_b, _, _ = self.bufs[k]
            self.copy(k, 1).wait_recv()
            held[:, x, a] += got_a[...]
            self.copy(k, 2).wait_recv()
            held[y, :, b] += got_b[...]
            self.copy(k, 3).start()
            self.copy(k, 4).start()

        return self.each(act)

    def p4(self):
        def act(k):
            c, x, y = self.place
            a, b = self.halves(k)
            _, held, _, _, got_a2, got_b2 = self.bufs[k]
            self.copy(k, 3).wait_recv()
            self.reds[k][a] = held[y, x, a] + got_a2[...]
            self.copy(k, 4).wait_recv()
            self.reds[k][b] = held[y, x, b] + got_b2[...]

        return self.each(act)

    def g1(self):
        def act(k):
            self.local(k).start()
            self.copy(k, 5).start()
            self.copy(k, 6).start()

        return self.each(act)

    def g2(self):
        def act(k):
            self.local(k).wait()
            self.copy(k, 5).wait_recv()
            self.copy(k, 6).wait_recv()
            self.copy(k, 7).start()
            self.copy(k, 8).start()

        return self.each(act)

    def g3(self):
        def act(k):
            self.copy(k, 7).wait_recv()
            self.copy(k, 8).wait_recv()
            self.copy(k, 9).start()

        return self.each(act)

    def g4(self):
        return self.each(lambda k: self.copy(k, 9).wait_recv())

    def sent(self, slots):
        def act(k):
            for s in slots:
                self.copy(k, s).wait_send()

        return self.each(act)


REDUCE, SPREAD = range(5), range(5, 10)


def sum_bufs(shapes):
    out = []
    for r, w in shapes:
        out += [VM((2, 2, r, w), f32), VM((2, 2, r, w), f32), VM((2, r // 2, w), f32),
                VM((2, r // 2, w), f32), VM((r // 2, w), f32), VM((r // 2, w), f32)]
    return out


def take_bufs(refs, count):
    return [refs[6 * k : 6 * k + 6] for k in range(count)], refs[6 * count :]


def sum_sems(count):
    return [pltpu.SemaphoreType.DMA((count, 10)), pltpu.SemaphoreType.DMA((count, 10)),
            pltpu.SemaphoreType.DMA((count,))]


def plane_barrier():
    _, core, xn, yn, _ = neighbours(1)
    barrier_with([core, xn, yn])


FFN_CHUNKS = [(64, 512), (64, 512)]
ATTN_CHUNKS = [(192, 128), (16, 512)]


def chunked(r, w):
    return (2, 2, 2, r, w)


def norm_back_all(dy, n, r, gain, gs_o, d_s, g_s):
    gs_o[...] = jnp.zeros_like(gs_o)
    for b in range(4):
        rows = rows_at(b)
        dyv, nv = dy(rows), n[rows]
        gs_o[0:1] += jnp.sum(dyv * nv, axis=0, keepdims=True)
        gs_o[1:2] += jnp.sum(dyv, axis=0, keepdims=True)
        d = layer_norm_back(dyv, nv, r[rows], gain)
        d_s[rows] = d
        g_s[rows] = d.astype(bf16)


def attend_slot(cross, win, w, pt, v, kt, q, ot, g_s, acc, dkey, scratch, tick):
    do_s, dot_s, dk_s, dv_s, dqt_s = scratch
    for b in range(4):
        rows = rows_at(b)
        do_s[rows] = nt(g_s[rows], w[0, 384:]).astype(bf16)
        dot_s[:, rows] = nt(w[0, 384:], g_s[rows]).astype(bf16)
    dk_s[...] = jnp.zeros_like(dk_s)
    dv_s[...] = jnp.zeros_like(dv_s)

    def block(b, start, width):
        rows = rows_at(b)
        keys = pl.ds(start, width)
        prow = keys if cross else slice(None)
        prod = dot_s[:, rows].astype(f32) * ot[0, :, rows].astype(f32)
        delta = jnp.concatenate(
            [jnp.sum(prod[:64], axis=0, keepdims=True), jnp.sum(prod[64:], axis=0, keepdims=True)],
            axis=1,
        )
        dpt = nn(v[0, keys], block_diag(dot_s[:64, rows], dot_s[64:, rows]))
        ptv = pt[0, b, prow]
        dst = (ptv.astype(f32) * (dpt - delta)).astype(bf16)
        dv_s[keys] += nn(ptv, two_heads(do_s[rows]))
        dk_s[keys] += nn(dst, two_heads(q[0, rows]))
        dqt_s[:64, rows] = (nn(kt[0, :64, keys], dst[:, :BLK]) * 0.125).astype(bf16)
        dqt_s[64:, rows] = (nn(kt[0, 64:, keys], dst[:, BLK:]) * 0.125).astype(bf16)

    for b in range(4):
        if cross:
            start = pl.multiple_of(win[b], 128)
            pl.when(win[4 + b] == 0)(lambda b=b, start=start: block(b, start, 512))
            pl.when(win[4 + b] != 0)(lambda b=b: block(b, 0, 1024))
        else:
            block(b, self_start(b), 512)
        tick(b)
    for b in range(4):
        rows = rows_at(b)
        dkb, dvb = dk_s[rows].astype(bf16), dv_s[rows].astype(bf16)
        kv = jnp.concatenate([dkb, dvb], axis=1)
        acc[rows] += tn(dqt_s[:, rows], w[0, :128])
        if cross:
            dkey[rows] += nn(kv, w[0, 128:384])
        else:
            acc[rows] += nn(kv, w[0, 128:384])


def attend_weights(dqkv_o, dwo_o, ot, g_s, alow, blow, scratch):
    _, _, dk_s, dv_s, dqt_s = scratch

    def put(m, val):
        dqkv_o[:, :, :, m * 64 : (m + 1) * 64] = val.T.reshape(2, 2, 2, 64, 128)

    put(0, nn(dqt_s[...], alow[...]))
    put(1, tn(dk_s[...].astype(bf16), blow[...]))
    put(2, tn(dv_s[...].astype(bf16), blow[...]))
    dwo_o[...] = nn(ot[0], g_s[...]).reshape(2, 2, 2, 16, 512)


ATTN_SCRATCH = [
    VM((1024, 128), bf16), VM((128, 1024), bf16), VM((1024, 128), f32), VM((1024, 128), f32),
    VM((128, 1024), bf16),
]


def cross_bwd_kernel(*refs):
    (win, dy, n, r, gains, w, pt, v, kt, q, ot, alow, blow, dec_low) = refs[:14]
    acc, dkey, dqkv_o, dwo_o, gs_o, enc_o, dec_o, g_s, dec_s, cs = refs[14:24]
    scratch = refs[24:]
    p = pl.program_id(0)
    moves = [(dec_low, dec_s), (dec_s, dec_o), (blow, enc_o)]

    def move(k):
        return pltpu.make_async_copy(*moves[k], cs.at[k])

    @pl.when(p == 0)
    def _():
        move(0).start()
        move(2).start()

    @pl.when(p == 2)
    def _():
        move(0).wait()
        move(1).start()

    @pl.when(p == 3)
    def _():
        move(1).wait()
        move(2).wait()

    @pl.when(p == 0)
    def _():
        norm_back_all(lambda rows: dy[rows], n, r, gains[3:4], gs_o, acc, g_s)
        dkey[...] = jnp.zeros_like(dkey)

    attend_slot(True, win, w, pt, v, kt, q, ot, g_s, acc, dkey, scratch, lambda b: None)

    @pl.when(p == 0)
    def _():
        attend_weights(dqkv_o, dwo_o, ot, g_s, alow, blow, scratch)


def call_cross_bwd(win, dy, n, r, gains, saved, alow, blow, dec_low):
    w, pt, q, v, kt, ot = saved
    a, b = [chunked(*s) for s in ATTN_CHUNKS]

    def by_slot(*tail):
        return pl.BlockSpec((1,) + tail, lambda t: (t,) + (0,) * len(tail))

    return pl.pallas_call(
        cross_bwd_kernel,
        grid=(4,),
        in_specs=[
            SMEM_SPEC, held((1024, 512)), held((1024, 512)), held((1024, 1)), held((5, 512)),
            by_slot(512, 512), by_slot(4, 1024, 512), by_slot(1024, 128), by_slot(128, 1024),
            by_slot(1024, 128), by_slot(128, 1024), held((1024, 512)), held((1024, 512)), ANY,
        ],
        out_specs=[kept((1024, 512)), kept((1024, 512)), kept(a), kept(b), kept((8, 512)), ANY, ANY],
        out_shape=[SDS((1024, 512), f32), SDS((1024, 512), f32), SDS(a, f32), SDS(b, f32),
                   SDS((8, 512), f32), SDS((1024, 512), bf16), SDS((1024, 512), bf16)],
        scratch_shapes=[VM((1024, 512), bf16), VM((1024, 512), bf16), pltpu.SemaphoreType.DMA((3,))]
        + ATTN_SCRATCH,
        compiler_params=pltpu.CompilerParams(vmem_limit_bytes=VMEM_MB * MB),
    )(win, dy, n, r, gains, w, pt, v, kt, q, ot, alow, blow, dec_low)


def ffn_back_slot(w, slope, g_s, db_s, acc, tick):
    for b in range(4):
        rows = rows_at(b)
        db = (nt(g_s[rows], w[0, 1]) * slope[rows].astype(f32)).astype(bf16)
        db_s[rows] = db
        acc[rows] += nn(db, w[0, 0])
        tick(b)


def ffn_weights(dw1_o, dw2_o, alow, db_s, h, g_s):
    dw1_o[...] = tn(alow[...], db_s[...]).reshape(2, 2, 2, 64, 512)
    dw2_o[...] = tn(h[...], g_s[...]).reshape(2, 2, 2, 64, 512)


def dec_ffn_bwd_kernel(dy, n, r, gains, alow, w, h, slope, acc, gs_o, dw1_o, dw2_o, g_s, db_s):
    c = pl.program_id(0)

    @pl.when(c == 0)
    def _():
        norm_back_all(lambda rows: dy[rows].astype(f32), n, r, gains[4:5], gs_o, acc, g_s)

    ffn_back_slot(w, slope, g_s, db_s, acc, lambda b: None)

    @pl.when(c == 0)
    def _():
        ffn_weights(dw1_o, dw2_o, alow, db_s, h, g_s)


def call_dec_ffn_bwd(dy, n, r, gains, alow, w, h, slope):
    shapes = [chunked(*s) for s in FFN_CHUNKS]
    return pl.pallas_call(
        dec_ffn_bwd_kernel,
        grid=(4,),
        in_specs=[
            held((1024, 512)), held((1024, 512)), held((1024, 1)), held((5, 512)),
            held((1024, 512)), pl.BlockSpec((1, 2, 512, 512), lambda t: (t, 0, 0, 0)),
            held((1024, 512)), pl.BlockSpec((1024, 512), lambda t: (0, t)),
        ],
        out_specs=[kept((1024, 512)), kept((8, 512))] + [kept(s) for s in shapes],
        out_shape=[SDS((1024, 512), f32), SDS((8, 512), f32)] + [SDS(s, f32) for s in shapes],
        scratch_shapes=[VM((1024, 512), bf16), VM((1024, 512), bf16)],
        compiler_params=pltpu.CompilerParams(vmem_limit_bytes=VMEM_MB * MB),
    )(dy, n, r, gains, alow, w, h, slope)


def last_of(t):
    kind = jnp.where((t == 0) | ((t >= 6) & (t <= 8)), 1, 0)
    block = jnp.where(t < 5, 4, jnp.where(t == 5, 0, jnp.where(t < 9, t - 1, t - 8)))
    return kind, block


def last_kernel(*refs):
    n2, r2, gains, alow_s, mcol, gs3, gs4 = refs[:7]
    w, pt, v, kt, q, ot, wf, slope = refs[7:15]
    far, refs = refs[15:24], refs[24:]
    x_far, parts_d, parts_c, refs = refs[0], refs[1:3], refs[3:5], refs[5:]
    mask_o, gain_o, shift_o, dec_o, enc_o, refs = *refs[:5], refs[5:]
    outs = [refs[2 * k : 2 * k + 2] for k in range(5)]
    refs = refs[10:]
    acc2, n1, r1, cot, alow_f, h, n0, r0, x_e, refs = *refs[:9], refs[9:]
    gs0, gs1, gs2, g2, db_s, small, got, refs = *refs[:7], refs[7:]
    scratch, refs = refs[:5], refs[5:]
    dws, refs = [None, None, refs[:2], refs[2:4], refs[4:6]], refs[6:]
    ls, ss, rs, refs = refs[0], refs[1], refs[2], refs[3:]
    sums = []
    for k, chunks in enumerate((FFN_CHUNKS, ATTN_CHUNKS, ATTN_CHUNKS, FFN_CHUNKS, ATTN_CHUNKS)):
        reds, refs = refs[:2], refs[2:]
        bufs, refs = take_bufs(refs, 2)
        parts = (parts_d, parts_c, *dws[2:])[k]
        sums.append(PlaneSum(parts, reds, outs[k], bufs, *refs[:3], far=k < 2))
        refs = refs[3:]
    d, c, s, f, e = sums
    loads = list(zip(far, (acc2.at[1], acc2.at[0], n1, r1, cot, alow_f, h, n0, r0)))
    loads += [(x_far, x_e), (acc2.at[1], dec_o), (acc2.at[0], enc_o)]
    t = pl.program_id(0)
    kind, _ = last_of(t)

    def load(k):
        return pltpu.make_async_copy(*loads[k], ls.at[k])

    _, core, xn, yn, _ = neighbours(1)

    def swap(k):
        return pltpu.make_async_remote_copy(
            src_ref=small.at[k], dst_ref=got.at[k], send_sem=ss.at[k], recv_sem=rs.at[k],
            device_id=(core, xn, yn)[k], device_id_type=MESH,
        )

    def small_first():
        small[0] = jnp.zeros_like(small[0])
        small[0, 0:1] = gs2[2:3]
        for k, g in enumerate((gs0, gs1, gs2, gs3, gs4)):
            small[0, 1 + k : 2 + k] = g[0:1]
            small[0, 6 + k : 7 + k] = g[1:2]
        swap(0).start()

    def small_next(k):
        def run():
            swap(k).wait_recv()
            small[k + 1] = small[k] + got[k]
            if k < 2:
                swap(k + 1).start()

        return run

    def small_last():
        mask_o[...] = small[3, 0:1]
        gain_o[...] = small[3, 1:6]
        shift_o[...] = small[3, 6:11]
        for k in range(3):
            swap(k).wait_send()

    def end():
        for x in sums:
            x.sent(REDUCE)()
            x.sent(SPREAD)()

    ev = {
        (0, -1): [plane_barrier, d.p1(), c.p1()],
        (0, 1): [d.p2()],
        (0, 2): [c.p2()],
        (0, 4): [s.p1()],
        (1, 0): [d.p3()],
        (1, 2): [c.p3()],
        (1, 4): [f.p1(), s.p2()],
        (2, 1): [d.p4(), d.g1()],
        (2, 3): [f.p2()],
        (3, 0): [c.p4(), c.g1()],
        (3, 2): [d.g2()],
        (4, 0): [s.p3()],
        (4, 2): [f.p3()],
        (5, 0): [c.g2()],
        (5, 1): [d.g3()],
        (5, 2): [s.p4(), s.g1()],
        (5, 4): [e.p1()],
        (6, 0): [f.p4(), f.g1()],
        (6, 1): [c.g3()],
        (6, 2): [e.p2()],
        (7, 0): [s.g2()],
        (7, 1): [d.g4()],
        (7, 2): [f.g2()],
        (8, 0): [e.p3()],
        (8, 1): [c.g4()],
        (8, 2): [s.g3()],
        (8, 4): [small_first],
        (9, 0): [e.p4(), e.g1()],
        (9, 1): [f.g3()],
        (9, 2): [small_next(0)],
        (10, 0): [e.g2()],
        (10, 1): [small_next(1)],
        (10, 2): [s.g4()],
        (11, 0): [e.g3()],
        (11, 1): [small_next(2)],
        (11, 2): [f.g4()],
    }
    attn_steps, ffn_steps = (0, 5, 6, 7, 8, 9, 10, 11), (1, 2, 3, 4)

    @pl.when((t == 0) | (t > 4))
    def _():
        @pl.when(t == 0)
        def _():
            for k in range(10):
                load(k).start()
            load(0).wait()

        run_events(t, attn_steps, ev, -1)

        @pl.when(t == 0)
        def _():
            a = acc2.at[1]
            norm_back_all(lambda rows: a[rows], n2, r2, gains[2:3], gs2, a, g2.at[1])

        @pl.when(t == 5)
        def _():
            for k in (7, 8, 9):
                load(k).wait()
            a = acc2.at[0]
            norm_back_all(lambda rows: a[rows], n0, r0, gains[0:1], gs0, a, g2.at[0])

        attend_slot(False, None, w, pt, v, kt, q, ot, g2.at[kind], acc2.at[kind], None, scratch,
                    lambda b: run_events(t, attn_steps, ev, b))

        @pl.when(t == 0)
        def _():
            attend_weights(*dws[2], ot, g2.at[1], alow_s, alow_s, scratch)

        @pl.when(t == 5)
        def _():
            attend_weights(*dws[4], ot, g2.at[0], x_e, x_e, scratch)

        @pl.when(t == 8)
        def _():
            total = jnp.zeros((1, 512), f32)
            for b in range(4):
                rows = rows_at(b)
                hit = jnp.concatenate([mcol[rows]] * 4, axis=1) == 1
                dx = acc2[1, rows]
                total += jnp.sum(jnp.where(hit, dx, 0.0), axis=0, keepdims=True)
                acc2[1, rows] = jnp.where(hit, 0.0, dx)
            gs2[2:3] = total
            load(10).start()

        run_events(t, attn_steps, ev, 4)

        @pl.when(t == 11)
        def _():
            load(11).start()
            e.g4()()
            small_last()
            end()
            load(10).wait()
            load(11).wait()

    @pl.when((t > 0) & (t < 5))
    def _():
        @pl.when(t == 1)
        def _():
            for k in range(1, 7):
                load(k).wait()
            a = acc2.at[0]
            norm_back_all(lambda rows: a[rows] + cot[rows].astype(f32), n1, r1, gains[1:2], gs1, a,
                          g2.at[0])

        ffn_back_slot(wf, slope, g2.at[0], db_s, acc2.at[0],
                      lambda b: run_events(t, ffn_steps, ev, b))

        @pl.when(t == 1)
        def _():
            ffn_weights(*dws[3], alow_f, db_s, h, g2.at[0])

        run_events(t, ffn_steps, ev, 4)


def call_last(n2, r2, gains, alow_s, mcol, gs3, gs4, saved, wf, slope, far, parts_d, parts_c):
    w, pt, q, v, kt, ot = saved
    groups = (FFN_CHUNKS, ATTN_CHUNKS, ATTN_CHUNKS, FFN_CHUNKS, ATTN_CHUNKS)

    def by_es(*tail):
        return pl.BlockSpec((1,) + tail, lambda t: (last_of(t)[1],) + (0,) * len(tail))

    def chunk(t):
        return jnp.clip(t - 1, 0, 3)

    net = []
    for g in groups:
        net += [VM(s, f32) for s in g] + sum_bufs(g) + sum_sems(2)
    results = [chunked(*s) for g in groups for s in g]
    return pl.pallas_call(
        last_kernel,
        grid=(12,),
        in_specs=[
            held((1024, 512)), held((1024, 1)), held((5, 512)), held((1024, 512)),
            held((1024, 128)), held((8, 512)), held((8, 512)), by_es(512, 512),
            by_es(4, 512, 512), by_es(1024, 128), by_es(128, 1024), by_es(1024, 128),
            by_es(128, 1024), pl.BlockSpec((1, 2, 512, 512), lambda t: (chunk(t), 0, 0, 0)),
            pl.BlockSpec((1024, 512), lambda t: (0, chunk(t))),
        ] + [ANY] * 14,
        out_specs=[kept((1, 512)), kept((5, 512)), kept((5, 512))] + [ANY] * 12,
        out_shape=[SDS((1, 512), f32), SDS((5, 512), f32), SDS((5, 512), f32),
                   SDS((1024, 512), f32), SDS((1024, 512), f32)] + [SDS(s, f32) for s in results],
        scratch_shapes=[
            VM((2, 1024, 512), f32), VM((1024, 512), f32), VM((1024, 1), f32), VM((1024, 512), bf16),
            VM((1024, 512), bf16), VM((1024, 512), bf16), VM((1024, 512), f32), VM((1024, 1), f32),
            VM((1024, 512), bf16), VM((8, 512), f32), VM((8, 512), f32), VM((8, 512), f32),
            VM((2, 1024, 512), bf16), VM((1024, 512), bf16), VM((4, 16, 512), f32),
            VM((3, 16, 512), f32),
        ] + ATTN_SCRATCH + [VM(chunked(*s), f32) for g in groups[2:] for s in g]
        + [pltpu.SemaphoreType.DMA((12,)), pltpu.SemaphoreType.DMA((3,)),
           pltpu.SemaphoreType.DMA((3,))] + net,
        compiler_params=pltpu.CompilerParams(
            collective_id=3, has_side_effects=True, vmem_limit_bytes=VMEM_MB * MB
        ),
    )(n2, r2, gains, alow_s, mcol, gs3, gs4, w, pt, v, kt, q, ot, wf, slope, *far, *parts_d,
      *parts_c)


def deliver_kernel(count, *refs):
    srcs, dsts, bufs = refs[:count], refs[count : 2 * count], refs[2 * count : 3 * count]
    ins, outs = refs[3 * count :]

    def load(k):
        return pltpu.make_async_copy(srcs[k], bufs[k], ins.at[k])

    def store(k):
        if len(dsts[k].shape) < 6:
            return [pltpu.make_async_copy(bufs[k], dsts[k], outs.at[k, 0])]
        return [
            pltpu.make_async_copy(bufs[k].at[:, :, :, pl.ds(m * 64, 64)], dsts[k].at[m], outs.at[k, m])
            for m in range(3)
        ]

    for k in range(count):
        load(k).start()
    for k in range(count):
        load(k).wait()
        for c in store(k):
            c.start()
    for k in range(count):
        for c in store(k):
            c.wait()


def deliver(arrays):
    shapes = [(3, 2, 2, 2, 64, 128) if a.shape[-1] == 128 else a.shape for a in arrays]
    count = len(arrays)
    return pl.pallas_call(
        functools.partial(deliver_kernel, count),
        in_specs=[ANY] * count,
        out_specs=[ANY] * count,
        out_shape=[SDS(s, a.dtype) for s, a in zip(shapes, arrays)],
        scratch_shapes=[VM(a.shape, a.dtype) for a in arrays]
        + [pltpu.SemaphoreType.DMA((count,)), pltpu.SemaphoreType.DMA((count, 3))],
        compiler_params=pltpu.CompilerParams(vmem_limit_bytes=VMEM_MB * MB),
    )(*arrays)


def per_device(planes, tensor, enc_in, dec_in, src_idx, tgt_idx, masked, mask_embed, enc_qkv,
               enc_out_w, enc_w1, enc_w2, self_qkv, self_out_w, cross_qkv, cross_out_w, dec_w1,
               dec_w2, gains, shifts, enc_cot, dec_cot):
    (target_low, target, koh, mq, mcol, own_es, own_c, own_f, own_d, blob_e, blob_s, blob_c, blob_f,
     blob_d, win) = call_prep(
        dec_in[0], masked, mask_embed[None], src_idx, tgt_idx, enc_qkv, enc_out_w,
        self_qkv, self_out_w, cross_qkv, cross_out_w, enc_w1, enc_w2, dec_w1, dec_w2)
    (w_es, pt_es, q_es, v_es, kt_es, ot_es, w_f, slope_e, h_e, r0, r2, r1, n0, n2, n1, first_low,
     second_low, enc_low, land_c) = call_first(
        tensor, enc_in[0], target_low, target, koh, mq, own_es, own_f, gains, shifts,
        (blob_e, blob_s, blob_f, blob_c))
    (w_c, pt_c, q_c, v_c, kt_c, ot_c, w_d, slope_d, h_d, r3, r4, n3, n4, third_low,
     dec_low) = call_second(
        tensor, n2, second_low, enc_low, koh, mq, own_c, own_d, gains, shifts, land_c, blob_d)
    save_es = (w_es, pt_es, q_es, v_es, kt_es, ot_es)
    save_c = (w_c, pt_c, q_c, v_c, kt_c, ot_c)

    d_third, gs4, *parts_d = call_dec_ffn_bwd(
        dec_cot[0], n4, r4, gains, third_low, w_d, h_d, slope_d)
    d_second, d_key, *parts_c, gs3, enc_out, dec_out = call_cross_bwd(
        win, d_third, n3, r3, gains, save_c, second_low, enc_low, dec_low)
    far = (d_second, d_key, n1, r1, enc_cot[0], first_low, h_e, n0, r0, enc_in[0])
    (mask_grad, gain_grad, shift_grad, dec_grad, d_enc, dw1_d, dw2_d, dqkv_c, dwo_c, dqkv_s, dwo_s,
     dw1_e, dw2_e, dqkv_e, dwo_e) = call_last(
        n2, r2, gains, target_low, mcol, gs3, gs4, save_es, w_f, slope_e, far, parts_d, parts_c)

    sums = (mask_grad, gain_grad, shift_grad, dqkv_e, dwo_e, dw1_e, dw2_e, dqkv_s, dwo_s, dqkv_c,
            dwo_c, dw1_d, dw2_d)
    if planes > 1:
        same = [[p * 8 + k for p in range(planes)] for k in range(8)]
        sums = lax.psum(sums, "dp", axis_index_groups=same)
    d_enc, dec_grad, mask_grad, gain_grad, shift_grad, *mats = deliver([d_enc, dec_grad, *sums])
    mats = [m.reshape(3, 512, 128) if m.ndim == 6 else m.reshape(-1, 512) for m in mats]
    return (enc_out[None], dec_out[None], d_enc[None], dec_grad[None], mask_grad[0], *mats,
            gain_grad, shift_grad)


def solution(mesh):
    tokens, index = P("dp", None, None), P("dp", None)
    qkv, cols, rows = P(None, None, "tensor"), P(None, "tensor"), P("tensor", None)
    weights = (qkv, rows, cols, rows, qkv, rows, qkv, rows, cols, rows)
    return jax.shard_map(
        functools.partial(per_device, mesh.shape["dp"] // 8, mesh.shape["tensor"]),
        mesh=mesh,
        in_specs=(tokens, tokens, index, index, index, P()) + weights + (P(), P(), tokens, tokens),
        out_specs=(tokens,) * 4 + (P(),) + weights + (P(), P()),
        check_vma=False,
    )
```

```python
import functools

import jax
import jax.numpy as jnp
from jax import lax
from jax.experimental import pallas as pl
from jax.experimental.pallas import tpu as pltpu
from jax.sharding import PartitionSpec as P

f32, bf16 = jnp.float32, jnp.bfloat16
HEAD_DIM = 64
EPS = 1e-05
FLOOR = -1000000000.0
BLK = 256
MB = 1 << 20
VMEM_MB = 60
MESH = pl.DeviceIdType.MESH
VM = pltpu.VMEM


def nt(a, b):
    return lax.dot_general(a, b, (((1,), (1,)), ((), ())), preferred_element_type=f32)


def nn(a, b):
    return lax.dot_general(a, b, (((1,), (0,)), ((), ())), preferred_element_type=f32)


def tn(a, b):
    return lax.dot_general(a, b, (((0,), (0,)), ((), ())), preferred_element_type=f32)


def layer_norm(v):
    c = v - jnp.mean(v, axis=-1, keepdims=True)
    r = lax.rsqrt(jnp.mean(c * c, axis=-1, keepdims=True) + EPS)
    return c * r, r


def layer_norm_back(dy, n, r, gain):
    dn = dy * gain
    m1 = jnp.mean(dn, axis=-1, keepdims=True)
    m2 = jnp.mean(dn * n, axis=-1, keepdims=True)
    return r * (dn - m1 - n * m2)


def block_diag(a, b):
    z = jnp.zeros_like(a)
    return jnp.concatenate(
        [jnp.concatenate([a, z], axis=1), jnp.concatenate([z, b], axis=1)], axis=0
    )


def two_heads(x):
    lane = lax.broadcasted_iota(jnp.int32, x.shape, 1)
    z = jnp.zeros_like(x)
    return jnp.concatenate([jnp.where(lane < HEAD_DIM, x, z), jnp.where(lane < HEAD_DIM, z, x)], 0)


def rows_at(b):
    return slice(b * BLK, (b + 1) * BLK)


def self_start(b):
    return min(max(b * BLK - 128, 0), 512)


def project_slot(w, kinds, get, rows_out):
    for b in range(4):
        xb = get(b)
        nat = nt(xb, w[kinds[0] * 128 : kinds[-1] * 128 + 128])
        tr = nt(w[kinds[0] * 128 : kinds[-1] * 128 + 128], xb)
        for k, kind in enumerate(kinds):
            cut = slice(k * 128, k * 128 + 128)
            for dst, val in rows_out(kind, b, nat[:, cut], tr[cut]):
                dst[...] = val.astype(bf16)


def softmax_block(k_s, koh, mq, qt):
    lhs = jnp.concatenate([k_s, koh], axis=1)
    rhs = jnp.concatenate([block_diag(qt[:64], qt[64:]), jnp.concatenate([mq, mq], axis=1)], axis=0)
    s = nn(lhs, rhs)
    e = jnp.exp(s - jnp.max(s, axis=0, keepdims=True))
    return (e * (1.0 / jnp.sum(e, axis=0, keepdims=True))).astype(bf16)


def mix_block(vt_s, keys, pt):
    return jnp.concatenate([nn(vt_s[:64, keys], pt[:, :BLK]), nn(vt_s[64:, keys], pt[:, BLK:])], 0)


def ffn_slot(w, al, acc, slope_o, h_o, first, tick):
    for b in range(4):
        rows = rows_at(b)
        before = nt(al[rows], w[0])
        cdf = 0.5 + 0.5 * lax.erf(before * (0.5**0.5))
        pdf = jnp.exp(before * before * -0.5) * 0.3989422804014327
        slope_o[rows] = (cdf + before * pdf).astype(bf16)
        hidden = (before * cdf).astype(bf16)

        @pl.when(first)
        def _():
            h_o[rows] = hidden

        acc[rows] += nn(hidden, w[1])
        tick(b)


def finish_norm(acc, gain, shift, n_ref, r_o, y_ref):
    for b in range(4):
        rows = rows_at(b)
        n, r = layer_norm(acc[rows])
        n_ref[rows] = n
        r_o[rows] = r
        y_ref[rows] = (n * gain + shift).astype(bf16)


def plane_index():
    dp = lax.axis_index("dp")
    return dp, lax.rem(dp, 8)


def neighbours(tensor):
    dp, j = plane_index()
    z = lax.axis_index("tensor")
    c, x, y = lax.rem(j, 2), lax.rem(lax.div(j, 2), 2), lax.div(j, 4)
    core, xn, yn = (dp + 1 - 2 * c, z), (dp + 2 - 4 * x, z), (dp + 4 - 8 * y, z)
    down = {k: (dp, lax.rem(z + tensor - k, tensor)) for k in range(1, tensor)}
    return (c, x, y), core, xn, yn, down


def barrier_with(peers):
    sem = pltpu.get_barrier_semaphore()
    for peer in peers:
        pl.semaphore_signal(sem, inc=1, device_id=peer, device_id_type=MESH)
    pl.semaphore_wait(sem, len(peers))


class Gather:
    def __init__(self, items, ss, rs, tensor):
        assert tensor == 4
        self.items, self.ss, self.rs = items, ss, rs
        _, self.core, self.xn, self.yn, self.down = neighbours(tensor)
        self.dp, self.z = lax.axis_index("dp"), lax.axis_index("tensor")

    def barrier(self):
        barrier_with([self.core, self.xn, self.yn] + list(self.down.values()))

    def copy(self, t, s, src, dst, dev, r=None):
        return lambda: pltpu.make_async_remote_copy(
            src_ref=src, dst_ref=dst, send_sem=self.ss.at[t, s],
            recv_sem=self.rs.at[t, s if r is None else r], device_id=dev, device_id_type=MESH,
        )

    def along(self, t):
        rnd, src, land = self.items[t]
        z, dp = self.z, self.dp
        inner = (z == 1) | (z == 2)
        if rnd == 1:
            left, right = jnp.maximum(z - 1, 0), jnp.minimum(z + 1, 3)
            return [
                (inner, self.copy(t, 0, src, land.at[0], (dp, left), 0)),
                (inner, self.copy(t, 9, src, land.at[0], (dp, right), 0)),
            ], None
        if rnd == 2:
            return [(None, self.copy(t, 0, src, land.at[0], (dp, lax.rem(2 * z + 1, 5)), 0))], None
        outer = (z == 0) | (z == 3)
        to, on = jnp.where(z == 0, 2, 1), jnp.where(z == 1, 0, 3)
        return [(outer, self.copy(t, 0, src, land.at[0], (dp, to), 0))], (
            inner, self.copy(t, 9, land.at[0], land.at[0], (dp, on), 0))

    def make(self, t):
        land = self.items[t][2]
        half = land.shape[1] // 2
        a, b = pl.ds(0, half), pl.ds(half, half)
        return [
            self.copy(t, 0, land.at[0], land.at[0], self.down[1]),
            self.copy(t, 1, land.at[0], land.at[1], self.xn),
            self.copy(t, 2, land.at[0], land.at[2], self.yn),
            self.copy(t, 3, land.at[0], land.at[4], self.core),
            self.copy(t, 4, land.at[1, a], land.at[3, a], self.yn),
            self.copy(t, 5, land.at[1], land.at[5], self.core),
            self.copy(t, 6, land.at[2, b], land.at[3, b], self.xn),
            self.copy(t, 7, land.at[2], land.at[6], self.core),
            self.copy(t, 8, land.at[3], land.at[7], self.core),
        ]

    def send(self, t):
        for cond, c in self.along(t)[0]:
            if cond is None:
                c().start()
            else:
                pl.when(cond)(lambda c=c: c().start())

    def onward(self, t):
        inner, c = self.along(t)[1]

        @pl.when(inner)
        def _():
            self.make(t)[0]().wait_recv()
            c().start()

    def spread(self, t):
        c = self.make(t)
        if self.items[t][0] < 3:
            c[0]().wait_recv()
        else:
            pl.when((self.z == 0) | (self.z == 3))(lambda: c[0]().wait_recv())
        for k in (1, 2, 3):
            c[k]().start()

    def relay(self, t):
        c = self.make(t)
        c[1]().wait_recv()
        c[4]().start()
        c[5]().start()
        c[2]().wait_recv()
        c[6]().start()
        c[7]().start()

    def pair(self, t):
        c = self.make(t)
        c[4]().wait_recv()
        c[6]().wait_recv()
        c[8]().start()

    def done(self, t):
        c = self.make(t)
        for k in (3, 5, 7, 8):
            c[k]().wait_recv()

    def finish(self):
        for t in range(len(self.items)):
            first, on = self.along(t)
            for cond, c in first + ([on] if on else []):
                if cond is None:
                    c().wait_send()
                else:
                    pl.when(cond)(lambda c=c: c().wait_send())
            for c in self.make(t)[1:]:
                c().wait_send()

    def plan(self, text):
        acts = {"Z": self.send, "Y": self.onward, "S": self.spread, "R": self.relay, "P": self.pair, "D": self.done}
        ev = {}
        for step, point, *words in text:
            row = ev.setdefault((step, point), [])
            for word in words:
                row.append(functools.partial(acts[word[0]], int(word[1:])))
        return ev


FIRST_PLAN = (
    (0, -1, "Z2", "Z0", "Z1", "Z5", "Z3", "Z4", "Z8", "Z6", "Z7", "Z11",
     "Z9", "Z10"),
    (1, 0, "S0"),
    (1, 2, "S1", "Y2"),
    (2, -1, "R0", "S2", "S3", "R1", "P0", "S4", "Y5", "D0"),
    (2, 1, "R2"),
    (2, 2, "S5"),
    (2, 3, "R3"),
    (3, -1, "P1", "S6", "R4", "D1"),
    (3, 1, "Y8", "P2"),
    (3, 3, "R5", "S7"),
    (4, -1, "D2"),
    (4, 0, "P3"),
    (5, -1, "D3"),
    (5, 0, "R6"),
    (5, 1, "Y11", "S8", "P4", "S9"),
    (5, 2, "P5"),
    (5, 3, "S10"),
    (6, -1, "D4"),
    (6, 2, "R7"),
    (6, 3, "S11"),
    (7, -1, "D5"),
    (7, 0, "P6"),
    (8, 1, "R8"),
    (9, -1, "D6"),
    (9, 0, "R9"),
    (9, 3, "R10"),
    (10, -1, "P7", "D7"),
    (10, 1, "R11"),
    (11, -1, "P8", "P9", "P10", "D8"),
    (11, 2, "P11"),
    (11, 3, "D9", "D10", "D11"),
)
SECOND_PLAN = (
    (0, -1, "Z2", "Z0", "Z1"),
    (1, 0, "S0"),
    (1, 3, "Y2"),
    (2, 1, "R0"),
    (2, 2, "S1"),
    (3, 0, "P0"),
    (3, 1, "S2"),
    (3, 3, "R1"),
    (5, -1, "D0"),
    (5, 0, "R2"),
    (5, 3, "P1"),
    (6, -1, "D1"),
    (6, 2, "P2"),
    (7, -1, "D2"),
)


def run_events(t, steps, events, point):
    for step in steps:
        acts = events.get((step, point))
        if acts:

            @pl.when(t == step)
            def _(acts=acts):
                for act in acts:
                    act()


def es_of(t):
    kind = jnp.where((t == 1) | (t >= 5), 1, 0)
    p = jnp.where(t < 2, 0, jnp.where(t < 5, t - 1, t - 4))
    return kind, jnp.minimum(p, 3)


def es_block(t):
    kind, p = es_of(t)
    return kind * 4 + p


def first_kernel(tensor, *refs):
    (x_far, t_far, target, koh, mq, own_es, own_f, gains, shifts) = refs[:9]
    blob_e, blob_s, blob_f, blob_c = refs[9:13]
    (wes_o, pt_o, q_o, v_o, kt_o, ot_o, wf_o, slope_o, h_o, r0_o, r2_o, r1_o, n0_o, n2_o,
     n1_o, y0_o, y2_o, encl_o, zc_o) = refs[13:32]
    (lows, land_a, land_f, accs, na, ylow, encl, k_s, qt_s, vt_s, ss, rs, cs) = refs[32:]
    t = pl.program_id(0)
    items = [(k, blob_e, land_a.at[k - 1]) for k in (1, 2, 3)]
    items += [(k, blob_s, land_a.at[2 + k]) for k in (1, 2, 3)]
    items += [(k, blob_f, land_f.at[k - 1]) for k in (1, 2, 3)]
    items += [(k, blob_c, zc_o.at[k - 1]) for k in (1, 2, 3)]
    net = Gather(items, ss, rs, tensor)
    outs = [
        (na.at[0], n0_o), (ylow.at[0], y0_o), (na.at[1], n2_o), (ylow.at[1], y2_o),
        (accs.at[0], n1_o), (encl, encl_o), (x_far, lows.at[0]), (t_far, lows.at[1]),
        (target, accs.at[1]),
    ]

    def out(k):
        return pltpu.make_async_copy(*outs[k], cs.at[k])

    ev = net.plan(FIRST_PLAN)
    kind, p = es_of(t)
    es_steps, f_steps = range(8), range(8, 12)

    @pl.when(t < 8)
    def _():
        @pl.when(t == 0)
        def _():
            for k in (6, 7, 8):
                out(k).start()
            net.barrier()

        run_events(t, es_steps, ev, -1)
        pl.when(t == 0)(lambda: out(6).wait())

        @pl.when(t == 1)
        def _():
            out(7).wait()
            out(8).wait()


        @pl.when(p == 0)
        def _():
            wes_o[0] = own_es[kind]

        @pl.when((p == 0) & (kind == 0))
        def _():
            accs[0] = lows[0].astype(f32)

        @pl.when(p > 0)
        def _():
            for m in range(4):
                piece = land_a[kind * 3 + p - 1, :, m * 16 : (m + 1) * 16, :]
                wes_o[0, m * 128 : (m + 1) * 128] = piece.reshape(128, 512).astype(bf16)

        w = wes_o.at[0]

        def outs_of(m, b, nat, tr):
            rows = rows_at(b)
            if m == 0:
                return [(q_o.at[0, rows], nat * 0.125), (qt_s.at[:, rows], tr * 0.125)]
            if m == 1:
                return [(k_s.at[rows], nat), (kt_o.at[0, :, rows], tr)]
            return [(v_o.at[0, rows], nat), (vt_s.at[:, rows], tr)]

        project_slot(w, (0, 1, 2), lambda b: lows[kind, rows_at(b)], outs_of)
        for b in range(4):
            rows = rows_at(b)
            keys = slice(self_start(b), self_start(b) + 512)
            pt = softmax_block(k_s[keys], koh[kind, keys], mq[kind, :, rows], qt_s[:, rows])
            pt_o[0, b] = pt
            ot = mix_block(vt_s, keys, pt).astype(bf16)
            ot_o[0, :, rows] = ot
            accs[kind, rows] += tn(ot, w[384:])
            run_events(t, es_steps, ev, b)

        @pl.when(t == 4)
        def _():
            finish_norm(accs.at[0], gains[0:1], shifts[0:1], na.at[0], r0_o, ylow.at[0])
            out(0).start()
            out(1).start()

        @pl.when(t == 7)
        def _():
            finish_norm(accs.at[1], gains[2:3], shifts[2:3], na.at[1], r2_o, ylow.at[1])
            out(2).start()
            out(3).start()

    @pl.when(t >= 8)
    def _():
        run_events(t, f_steps, ev, -1)

        @pl.when(t == 8)
        def _():
            wf_o[0] = own_f[...]
            accs[0] = na[0] * gains[0:1] + shifts[0:1]

        @pl.when(t > 8)
        def _():
            for m in range(2):
                piece = land_f[t - 9, :, m * 64 : (m + 1) * 64, :]
                wf_o[0, m] = piece.reshape(512, 512).astype(bf16)

        ffn_slot(wf_o.at[0], ylow.at[0], accs.at[0], slope_o, h_o, t == 8,
                 lambda b: run_events(t, f_steps, ev, b))

        @pl.when(t == 11)
        def _():
            finish_norm(accs.at[0], gains[1:2], shifts[1:2], accs.at[0], r1_o, encl)
            out(4).start()
            out(5).start()
            for k in range(6):
                out(k).wait()
            net.finish()


def held(shape):
    return pl.BlockSpec(shape, lambda t: (0,) * len(shape), pipeline_mode=pl.Buffered(1))


def picked(k, *tail):
    return pl.BlockSpec((1,) + tail, lambda t: (k, 0, 0), pipeline_mode=pl.Buffered(1))


def kept(shape):
    return pl.BlockSpec(shape, lambda t: (0,) * len(shape))


ANY = pl.BlockSpec(memory_space=pl.ANY)
SMEM_SPEC = pl.BlockSpec(memory_space=pltpu.SMEM)
SDS = jax.ShapeDtypeStruct


def by_es(*tail):
    return pl.BlockSpec((1,) + tail, lambda t: (es_block(t),) + (0,) * len(tail))


def call_first(tensor, x_e, tlow, target, koh, mq, own_es, own_f, gains, shifts, blobs):
    def chunk(t):
        return jnp.maximum(t - 8, 0)

    n_items = 12
    return pl.pallas_call(
        functools.partial(first_kernel, tensor),
        grid=(12,),
        in_specs=[
            ANY, ANY, ANY, held((2, 1024, 128)), held((2, 128, 1024)),
            held((2, 512, 512)), held((2, 512, 512)), held((5, 512)), held((5, 512)),
        ] + [ANY] * 4,
        out_specs=[
            by_es(512, 512), by_es(4, 512, 512), by_es(1024, 128), by_es(1024, 128),
            by_es(128, 1024), by_es(128, 1024),
            pl.BlockSpec((1, 2, 512, 512), lambda t: (chunk(t), 0, 0, 0)),
            pl.BlockSpec((1024, 512), lambda t: (0, chunk(t))),
            kept((1024, 512)), kept((1024, 1)), kept((1024, 1)), kept((1024, 1)),
        ] + [ANY] * 7,
        out_shape=[
            SDS((8, 512, 512), bf16), SDS((8, 4, 512, 512), bf16), SDS((8, 1024, 128), bf16),
            SDS((8, 1024, 128), bf16), SDS((8, 128, 1024), bf16), SDS((8, 128, 1024), bf16),
            SDS((4, 2, 512, 512), bf16), SDS((1024, 2048), bf16), SDS((1024, 512), bf16),
            SDS((1024, 1), f32), SDS((1024, 1), f32), SDS((1024, 1), f32),
            SDS((1024, 512), f32), SDS((1024, 512), f32), SDS((1024, 512), f32),
            SDS((1024, 512), bf16), SDS((1024, 512), bf16), SDS((1024, 512), bf16), SDS((3, 8, 64, 512), f32),
        ],
        scratch_shapes=[
            VM((2, 1024, 512), bf16), VM((6, 8, 64, 512), f32), VM((3, 8, 128, 512), f32),
            VM((2, 1024, 512), f32),
            VM((2, 1024, 512), f32), VM((2, 1024, 512), bf16), VM((1024, 512), bf16),
            VM((1024, 128), bf16), VM((128, 1024), bf16), VM((128, 1024), bf16),
            pltpu.SemaphoreType.DMA((n_items, 10)), pltpu.SemaphoreType.DMA((n_items, 10)),
            pltpu.SemaphoreType.DMA((9,)),
        ],
        compiler_params=pltpu.CompilerParams(
            collective_id=0, has_side_effects=True, vmem_limit_bytes=VMEM_MB * MB
        ),
    )(x_e, tlow, target, koh, mq, own_es, own_f, gains, shifts, *blobs)


def second_kernel(tensor, *refs):
    (n2, qlow, klow, koh, mq, own_c, own_d, gains, shifts, far_c) = refs[:10]
    (blob_d,) = refs[10:11]
    (wc_o, pt_o, q_o, v_o, kt_o, ot_o, wd_o, slope_o, h_o, r3_o, r4_o, n3_o, n4_o, y3_o,
     dec_o) = refs[11:26]
    (land_c, land_d, acc, n3, ylow, decl, k_s, qt_s, vt_s, ss, rs, cs) = refs[26:]
    t = pl.program_id(0)
    items = [(k, blob_d, land_d.at[k - 1]) for k in (1, 2, 3)]
    net = Gather(items, ss, rs, tensor)
    moves = [(n3, n3_o), (ylow, y3_o), (acc, n4_o), (decl, dec_o), (far_c, land_c)]

    def move(k):
        return pltpu.make_async_copy(*moves[k], cs.at[k])

    ev = net.plan(SECOND_PLAN)
    c_steps, d_steps = range(4), range(4, 8)

    @pl.when(t < 4)
    def _():
        pl.when(t == 0)(lambda: move(4).start())
        pl.when(t == 0)(net.barrier)
        run_events(t, c_steps, ev, -1)
        pl.when(t == 1)(lambda: move(4).wait())

        @pl.when(t == 0)
        def _():
            wc_o[0] = own_c[...]
            acc[...] = n2[...] * gains[2:3] + shifts[2:3]

        @pl.when(t > 0)
        def _():
            for m in range(4):
                piece = land_c[t - 1, :, m * 16 : (m + 1) * 16, :]
                wc_o[0, m * 128 : (m + 1) * 128] = piece.reshape(128, 512).astype(bf16)

        w = wc_o.at[0]

        def outs_of(m, b, nat, tr):
            rows = rows_at(b)
            if m == 0:
                return [(q_o.at[0, rows], nat * 0.125), (qt_s.at[:, rows], tr * 0.125)]
            if m == 1:
                return [(k_s.at[rows], nat), (kt_o.at[0, :, rows], tr)]
            return [(v_o.at[0, rows], nat), (vt_s.at[:, rows], tr)]

        project_slot(w, (0,), lambda b: qlow[rows_at(b)], outs_of)
        project_slot(w, (1, 2), lambda b: klow[rows_at(b)], outs_of)
        for b in range(4):
            rows = rows_at(b)
            keys = slice(0, 1024)
            pt = softmax_block(k_s[...], koh[0], mq[0, :, rows], qt_s[:, rows])
            pt_o[0, b] = pt
            ot = mix_block(vt_s, keys, pt).astype(bf16)
            ot_o[0, :, rows] = ot
            acc[rows] += tn(ot, w[384:])
            run_events(t, c_steps, ev, b)

        @pl.when(t == 3)
        def _():
            finish_norm(acc, gains[3:4], shifts[3:4], n3, r3_o, ylow)
            move(0).start()
            move(1).start()

    @pl.when(t >= 4)
    def _():
        run_events(t, d_steps, ev, -1)

        @pl.when(t == 4)
        def _():
            wd_o[0] = own_d[...]
            acc[...] = n3[...] * gains[3:4] + shifts[3:4]

        @pl.when(t > 4)
        def _():
            for m in range(2):
                piece = land_d[t - 5, :, m * 64 : (m + 1) * 64, :]
                wd_o[0, m] = piece.reshape(512, 512).astype(bf16)

        ffn_slot(wd_o.at[0], ylow, acc, slope_o, h_o, t == 4,
                 lambda b: run_events(t, d_steps, ev, b))

        @pl.when(t == 7)
        def _():
            finish_norm(acc, gains[4:5], shifts[4:5], acc, r4_o, decl)
            move(2).start()
            move(3).start()
            for k in range(4):
                move(k).wait()
            net.finish()


def call_second(tensor, n2, qlow, klow, koh, mq, own_c, own_d, gains, shifts, land_c, blob_d):
    def slot(t):
        return jnp.minimum(t, 3)

    def chunk(t):
        return jnp.maximum(t - 4, 0)

    def by_slot(*tail):
        return pl.BlockSpec((1,) + tail, lambda t: (slot(t),) + (0,) * len(tail))

    return pl.pallas_call(
        functools.partial(second_kernel, tensor),
        grid=(8,),
        in_specs=[
            held((1024, 512)), held((1024, 512)), held((1024, 512)), picked(0, 1024, 128),
            picked(1, 128, 1024), held((512, 512)), held((2, 512, 512)), held((5, 512)),
            held((5, 512)), ANY, ANY,
        ],
        out_specs=[
            by_slot(512, 512), by_slot(4, 1024, 512), by_slot(1024, 128), by_slot(1024, 128),
            by_slot(128, 1024), by_slot(128, 1024),
            pl.BlockSpec((1, 2, 512, 512), lambda t: (chunk(t), 0, 0, 0)),
            pl.BlockSpec((1024, 512), lambda t: (0, chunk(t))),
            kept((1024, 512)), kept((1024, 1)), kept((1024, 1)),
        ] + [ANY] * 4,
        out_shape=[
            SDS((4, 512, 512), bf16), SDS((4, 4, 1024, 512), bf16), SDS((4, 1024, 128), bf16),
            SDS((4, 1024, 128), bf16), SDS((4, 128, 1024), bf16), SDS((4, 128, 1024), bf16),
            SDS((4, 2, 512, 512), bf16), SDS((1024, 2048), bf16), SDS((1024, 512), bf16),
            SDS((1024, 1), f32), SDS((1024, 1), f32),
            SDS((1024, 512), f32), SDS((1024, 512), f32), SDS((1024, 512), bf16),
            SDS((1024, 512), bf16),
        ],
        scratch_shapes=[
            VM((3, 8, 64, 512), f32), VM((3, 8, 128, 512), f32), VM((1024, 512), f32),
            VM((1024, 512), f32), VM((1024, 512), bf16), VM((1024, 512), bf16),
            VM((1024, 128), bf16), VM((128, 1024), bf16), VM((128, 1024), bf16),
            pltpu.SemaphoreType.DMA((3, 10)), pltpu.SemaphoreType.DMA((3, 10)),
            pltpu.SemaphoreType.DMA((5,)),
        ],
        compiler_params=pltpu.CompilerParams(
            collective_id=2, has_side_effects=True, vmem_limit_bytes=VMEM_MB * MB
        ),
    )(n2, qlow, klow, koh, mq, own_c, own_d, gains, shifts, land_c, blob_d)


def column(row):
    return jnp.broadcast_to(row, (128, row.shape[1])).T


def prep_kernel(x_d, masked, embed, src, tgt, qkv_e, wo_e, qkv_s, wo_s, qkv_c, wo_c,
                w1_e, w2_e, w1_d, w2_d, tlow, target, koh, mq, mcol, own_es, own_c, own_f, own_d,
                blob_e, blob_s, blob_c, blob_f, blob_d, win):
    _, j = plane_index()
    head = pl.multiple_of(lax.rem(j, 2) * 64 + lax.div(j, 2) * 16, 16)
    unit = pl.multiple_of(j * 64, 64)
    for qkv, wo, own, blob in (
        (qkv_e, wo_e, own_es.at[0], blob_e),
        (qkv_s, wo_s, own_es.at[1], blob_s),
        (qkv_c, wo_c, own_c, blob_c),
    ):
        for m in range(3):
            own[m * 128 : (m + 1) * 128] = qkv[m].T
        own[384:] = wo[...]
        for m in range(4):
            piece = own[pl.ds(m * 128 + head, 16)]
            blob[m * 16 : (m + 1) * 16] = piece.astype(f32)
    for w1, w2, own, blob in ((w1_e, w2_e, own_f, blob_f), (w1_d, w2_d, own_d, blob_d)):
        own[0] = w1[...].T
        own[1] = w2[...]
        for m in range(2):
            blob[m * 64 : (m + 1) * 64] = own[m, pl.ds(unit, 64)].astype(f32)
    for k, ids in enumerate((src[...], tgt[...])):
        lane = lax.broadcasted_iota(jnp.int32, (1024, 128), 1)
        koh[k] = jnp.where(column(ids) == lane, 1.0, 0.0).astype(bf16)
        pair = lax.broadcasted_iota(jnp.int32, (128, 1024), 0)
        mq[k] = jnp.where(ids == pair, 0.0, FLOOR).astype(bf16)
    m = column(masked[...])
    mcol[...] = m
    m4 = jnp.concatenate([m] * 4, axis=1)
    tv = jnp.where(m4 == 1, embed[...], x_d[...].astype(f32))
    target[...] = tv
    tlow[...] = tv.astype(bf16)
    s = src[...]
    for b in range(4):
        cut = tgt[:, b * BLK : (b + 1) * BLK]
        lo, hi = jnp.min(cut), jnp.max(cut)
        begin = jnp.sum((s < lo).astype(jnp.int32))
        end = jnp.sum((s <= hi).astype(jnp.int32))
        start = jnp.minimum(lax.div(begin, 128) * 128, 512)
        win[b] = start
        win[4 + b] = (end - start > 512).astype(jnp.int32)


def call_prep(*args):
    full = pl.BlockSpec(memory_space=pltpu.VMEM)
    return pl.pallas_call(
        prep_kernel,
        in_specs=[full] * len(args),
        out_specs=[full] * 14 + [SMEM_SPEC],
        out_shape=[
            SDS((1024, 512), bf16), SDS((1024, 512), f32), SDS((2, 1024, 128), bf16),
            SDS((2, 128, 1024), bf16), SDS((1024, 128), jnp.int32),
            SDS((2, 512, 512), bf16), SDS((512, 512), bf16), SDS((2, 512, 512), bf16),
            SDS((2, 512, 512), bf16), SDS((64, 512), f32), SDS((64, 512), f32),
            SDS((64, 512), f32), SDS((128, 512), f32), SDS((128, 512), f32),
            SDS((8,), jnp.int32),
        ],
        compiler_params=pltpu.CompilerParams(vmem_limit_bytes=VMEM_MB * MB),
    )(*args)


class PlaneSum:
    def __init__(self, parts, reds, outs, bufs, ss, rs, ls, far=False):
        self.far = far
        self.parts, self.reds, self.outs, self.bufs = parts, reds, outs, bufs
        self.ss, self.rs, self.ls = ss, rs, ls
        self.place, self.core, self.xn, self.yn, _ = neighbours(1)

    def copy(self, k, s):
        c, x, y = self.place
        h = self.reds[k].shape[0] // 2
        a, b = pl.ds(0, h), pl.ds(h, h)
        red = self.reds[k]
        if s < 5:
            got_c, held, got_a, got_b, got_a2, got_b2 = self.bufs[k]
            src, dst, dev = [
                lambda: (self.parts[k].at[:, :, 1 - c], got_c, self.core),
                lambda: (held.at[:, 1 - x, a], got_a, self.xn),
                lambda: (held.at[1 - y, :, b], got_b, self.yn),
                lambda: (held.at[1 - y, x, a], got_a2, self.yn),
                lambda: (held.at[y, 1 - x, b], got_b2, self.xn),
            ][s]()
        else:
            o = self.outs[k]
            src, dst, dev = [
                lambda: (red.at[a], o.at[y, x, c, a], self.yn),
                lambda: (red.at[b], o.at[y, x, c, b], self.xn),
                lambda: (o.at[:, x, c, a], o.at[:, x, c, a], self.xn),
                lambda: (o.at[y, :, c, b], o.at[y, :, c, b], self.yn),
                lambda: (o.at[:, :, c], o.at[:, :, c], self.core),
            ][s - 5]()
        return pltpu.make_async_remote_copy(
            src_ref=src, dst_ref=dst, send_sem=self.ss.at[k, s], recv_sem=self.rs.at[k, s],
            device_id=dev, device_id_type=MESH,
        )

    def local(self, k):
        c, x, y = self.place
        return pltpu.make_async_copy(self.reds[k], self.outs[k].at[y, x, c], self.ls.at[k])

    def halves(self, k):
        h = self.reds[k].shape[0] // 2
        return slice(0, h), slice(h, 2 * h)

    def each(self, act):
        def run():
            for k in range(len(self.reds)):
                act(k)

        return run

    def fetch(self, k):
        src = self.parts[k].at[:, :, self.place[0]]
        return pltpu.make_async_copy(src, self.bufs[k][1], self.ls.at[k])

    def p1(self):
        def act(k):
            self.copy(k, 0).start()
            if self.far:
                self.fetch(k).start()

        return self.each(act)

    def p2(self):
        def act(k):
            got_c, held = self.bufs[k][:2]
            self.copy(k, 0).wait_recv()
            if self.far:
                self.fetch(k).wait()
                held[...] += got_c[...]
            else:
                held[...] = self.parts[k][:, :, self.place[0]] + got_c[...]
            self.copy(k, 1).start()
            self.copy(k, 2).start()

        return self.each(act)

    def p3(self):
        def act(k):
            c, x, y = self.place
            a, b = self.halves(k)
            _, held, got_a, got_b, _, _ = self.bufs[k]
            self.copy(k, 1).wait_recv()
            held[:, x, a] += got_a[...]
            self.copy(k, 2).wait_recv()
            held[y, :, b] += got_b[...]
            self.copy(k, 3).start()
            self.copy(k, 4).start()

        return self.each(act)

    def p4(self):
        def act(k):
            c, x, y = self.place
            a, b = self.halves(k)
            _, held, _, _, got_a2, got_b2 = self.bufs[k]
            self.copy(k, 3).wait_recv()
            self.reds[k][a] = held[y, x, a] + got_a2[...]
            self.copy(k, 4).wait_recv()
            self.reds[k][b] = held[y, x, b] + got_b2[...]

        return self.each(act)

    def g1(self):
        def act(k):
            self.local(k).start()
            self.copy(k, 5).start()
            self.copy(k, 6).start()

        return self.each(act)

    def g2(self):
        def act(k):
            self.local(k).wait()
            self.copy(k, 5).wait_recv()
            self.copy(k, 6).wait_recv()
            self.copy(k, 7).start()
            self.copy(k, 8).start()

        return self.each(act)

    def g3(self):
        def act(k):
            self.copy(k, 7).wait_recv()
            self.copy(k, 8).wait_recv()
            self.copy(k, 9).start()

        return self.each(act)

    def g4(self):
        return self.each(lambda k: self.copy(k, 9).wait_recv())

    def sent(self, slots):
        def act(k):
            for s in slots:
                self.copy(k, s).wait_send()

        return self.each(act)


REDUCE, SPREAD = range(5), range(5, 10)


def sum_bufs(shapes):
    out = []
    for r, w in shapes:
        out += [VM((2, 2, r, w), f32), VM((2, 2, r, w), f32), VM((2, r // 2, w), f32),
                VM((2, r // 2, w), f32), VM((r // 2, w), f32), VM((r // 2, w), f32)]
    return out


def take_bufs(refs, count):
    return [refs[6 * k : 6 * k + 6] for k in range(count)], refs[6 * count :]


def sum_sems(count):
    return [pltpu.SemaphoreType.DMA((count, 10)), pltpu.SemaphoreType.DMA((count, 10)),
            pltpu.SemaphoreType.DMA((count,))]


def plane_barrier():
    _, core, xn, yn, _ = neighbours(1)
    barrier_with([core, xn, yn])


FFN_CHUNKS = [(64, 512), (64, 512)]
ATTN_CHUNKS = [(192, 128), (16, 512)]


def chunked(r, w):
    return (2, 2, 2, r, w)


def norm_back_all(dy, n, r, gain, gs_o, d_s, g_s):
    gs_o[...] = jnp.zeros_like(gs_o)
    for b in range(4):
        rows = rows_at(b)
        dyv, nv = dy(rows), n[rows]
        gs_o[0:1] += jnp.sum(dyv * nv, axis=0, keepdims=True)
        gs_o[1:2] += jnp.sum(dyv, axis=0, keepdims=True)
        d = layer_norm_back(dyv, nv, r[rows], gain)
        d_s[rows] = d
        g_s[rows] = d.astype(bf16)


def attend_slot(cross, win, w, pt, v, kt, q, ot, g_s, acc, dkey, scratch, tick):
    do_s, dot_s, dk_s, dv_s, dqt_s = scratch
    for b in range(4):
        rows = rows_at(b)
        do_s[rows] = nt(g_s[rows], w[0, 384:]).astype(bf16)
        dot_s[:, rows] = nt(w[0, 384:], g_s[rows]).astype(bf16)
    dk_s[...] = jnp.zeros_like(dk_s)
    dv_s[...] = jnp.zeros_like(dv_s)

    def block(b, start, width):
        rows = rows_at(b)
        keys = pl.ds(start, width)
        prow = keys if cross else slice(None)
        prod = dot_s[:, rows].astype(f32) * ot[0, :, rows].astype(f32)
        delta = jnp.concatenate(
            [jnp.sum(prod[:64], axis=0, keepdims=True), jnp.sum(prod[64:], axis=0, keepdims=True)],
            axis=1,
        )
        dpt = nn(v[0, keys], block_diag(dot_s[:64, rows], dot_s[64:, rows]))
        ptv = pt[0, b, prow]
        dst = (ptv.astype(f32) * (dpt - delta)).astype(bf16)
        dv_s[keys] += nn(ptv, two_heads(do_s[rows]))
        dk_s[keys] += nn(dst, two_heads(q[0, rows]))
        dqt_s[:64, rows] = (nn(kt[0, :64, keys], dst[:, :BLK]) * 0.125).astype(bf16)
        dqt_s[64:, rows] = (nn(kt[0, 64:, keys], dst[:, BLK:]) * 0.125).astype(bf16)

    for b in range(4):
        if cross:
            start = pl.multiple_of(win[b], 128)
            pl.when(win[4 + b] == 0)(lambda b=b, start=start: block(b, start, 512))
            pl.when(win[4 + b] != 0)(lambda b=b: block(b, 0, 1024))
        else:
            block(b, self_start(b), 512)
        tick(b)
    for b in range(4):
        rows = rows_at(b)
        dkb, dvb = dk_s[rows].astype(bf16), dv_s[rows].astype(bf16)
        kv = jnp.concatenate([dkb, dvb], axis=1)
        acc[rows] += tn(dqt_s[:, rows], w[0, :128])
        if cross:
            dkey[rows] += nn(kv, w[0, 128:384])
        else:
            acc[rows] += nn(kv, w[0, 128:384])


def attend_weights(dqkv_o, dwo_o, ot, g_s, alow, blow, scratch):
    _, _, dk_s, dv_s, dqt_s = scratch

    def put(m, val):
        dqkv_o[:, :, :, m * 64 : (m + 1) * 64] = val.T.reshape(2, 2, 2, 64, 128)

    put(0, nn(dqt_s[...], alow[...]))
    put(1, tn(dk_s[...].astype(bf16), blow[...]))
    put(2, tn(dv_s[...].astype(bf16), blow[...]))
    dwo_o[...] = nn(ot[0], g_s[...]).reshape(2, 2, 2, 16, 512)


ATTN_SCRATCH = [
    VM((1024, 128), bf16), VM((128, 1024), bf16), VM((1024, 128), f32), VM((1024, 128), f32),
    VM((128, 1024), bf16),
]


def cross_bwd_kernel(*refs):
    (win, dy, n, r, gains, w, pt, v, kt, q, ot, alow, blow, dec_low) = refs[:14]
    acc, dkey, dqkv_o, dwo_o, gs_o, enc_o, dec_o, g_s, dec_s, cs = refs[14:24]
    scratch = refs[24:]
    p = pl.program_id(0)
    moves = [(dec_low, dec_s), (dec_s, dec_o), (blow, enc_o)]

    def move(k):
        return pltpu.make_async_copy(*moves[k], cs.at[k])

    @pl.when(p == 0)
    def _():
        move(0).start()
        move(2).start()

    @pl.when(p == 2)
    def _():
        move(0).wait()
        move(1).start()

    @pl.when(p == 3)
    def _():
        move(1).wait()
        move(2).wait()

    @pl.when(p == 0)
    def _():
        norm_back_all(lambda rows: dy[rows], n, r, gains[3:4], gs_o, acc, g_s)
        dkey[...] = jnp.zeros_like(dkey)

    attend_slot(True, win, w, pt, v, kt, q, ot, g_s, acc, dkey, scratch, lambda b: None)

    @pl.when(p == 0)
    def _():
        attend_weights(dqkv_o, dwo_o, ot, g_s, alow, blow, scratch)


def call_cross_bwd(win, dy, n, r, gains, saved, alow, blow, dec_low):
    w, pt, q, v, kt, ot = saved
    a, b = [chunked(*s) for s in ATTN_CHUNKS]

    def by_slot(*tail):
        return pl.BlockSpec((1,) + tail, lambda t: (t,) + (0,) * len(tail))

    return pl.pallas_call(
        cross_bwd_kernel,
        grid=(4,),
        in_specs=[
            SMEM_SPEC, held((1024, 512)), held((1024, 512)), held((1024, 1)), held((5, 512)),
            by_slot(512, 512), by_slot(4, 1024, 512), by_slot(1024, 128), by_slot(128, 1024),
            by_slot(1024, 128), by_slot(128, 1024), held((1024, 512)), held((1024, 512)), ANY,
        ],
        out_specs=[kept((1024, 512)), kept((1024, 512)), kept(a), kept(b), kept((8, 512)), ANY, ANY],
        out_shape=[SDS((1024, 512), f32), SDS((1024, 512), f32), SDS(a, f32), SDS(b, f32),
                   SDS((8, 512), f32), SDS((1024, 512), bf16), SDS((1024, 512), bf16)],
        scratch_shapes=[VM((1024, 512), bf16), VM((1024, 512), bf16), pltpu.SemaphoreType.DMA((3,))]
        + ATTN_SCRATCH,
        compiler_params=pltpu.CompilerParams(vmem_limit_bytes=VMEM_MB * MB),
    )(win, dy, n, r, gains, w, pt, v, kt, q, ot, alow, blow, dec_low)


def ffn_back_slot(w, slope, g_s, db_s, acc, tick):
    for b in range(4):
        rows = rows_at(b)
        db = (nt(g_s[rows], w[0, 1]) * slope[rows].astype(f32)).astype(bf16)
        db_s[rows] = db
        acc[rows] += nn(db, w[0, 0])
        tick(b)


def ffn_weights(dw1_o, dw2_o, alow, db_s, h, g_s):
    dw1_o[...] = tn(alow[...], db_s[...]).reshape(2, 2, 2, 64, 512)
    dw2_o[...] = tn(h[...], g_s[...]).reshape(2, 2, 2, 64, 512)


def dec_ffn_bwd_kernel(dy, n, r, gains, alow, w, h, slope, acc, gs_o, dw1_o, dw2_o, g_s, db_s):
    c = pl.program_id(0)

    @pl.when(c == 0)
    def _():
        norm_back_all(lambda rows: dy[rows].astype(f32), n, r, gains[4:5], gs_o, acc, g_s)

    ffn_back_slot(w, slope, g_s, db_s, acc, lambda b: None)

    @pl.when(c == 0)
    def _():
        ffn_weights(dw1_o, dw2_o, alow, db_s, h, g_s)


def call_dec_ffn_bwd(dy, n, r, gains, alow, w, h, slope):
    shapes = [chunked(*s) for s in FFN_CHUNKS]
    return pl.pallas_call(
        dec_ffn_bwd_kernel,
        grid=(4,),
        in_specs=[
            held((1024, 512)), held((1024, 512)), held((1024, 1)), held((5, 512)),
            held((1024, 512)), pl.BlockSpec((1, 2, 512, 512), lambda t: (t, 0, 0, 0)),
            held((1024, 512)), pl.BlockSpec((1024, 512), lambda t: (0, t)),
        ],
        out_specs=[kept((1024, 512)), kept((8, 512))] + [kept(s) for s in shapes],
        out_shape=[SDS((1024, 512), f32), SDS((8, 512), f32)] + [SDS(s, f32) for s in shapes],
        scratch_shapes=[VM((1024, 512), bf16), VM((1024, 512), bf16)],
        compiler_params=pltpu.CompilerParams(vmem_limit_bytes=VMEM_MB * MB),
    )(dy, n, r, gains, alow, w, h, slope)


def last_of(t):
    kind = jnp.where((t == 0) | ((t >= 6) & (t <= 8)), 1, 0)
    block = jnp.where(t < 5, 4, jnp.where(t == 5, 0, jnp.where(t < 9, t - 1, t - 8)))
    return kind, block


def last_kernel(*refs):
    n2, r2, gains, alow_s, mcol, gs3, gs4 = refs[:7]
    w, pt, v, kt, q, ot, wf, slope = refs[7:15]
    far, refs = refs[15:24], refs[24:]
    x_far, parts_d, parts_c, refs = refs[0], refs[1:3], refs[3:5], refs[5:]
    mask_o, gain_o, shift_o, dec_o, enc_o, refs = *refs[:5], refs[5:]
    outs = [refs[2 * k : 2 * k + 2] for k in range(5)]
    refs = refs[10:]
    acc2, n1, r1, cot, alow_f, h, n0, r0, x_e, refs = *refs[:9], refs[9:]
    gs0, gs1, gs2, g2, db_s, small, got, refs = *refs[:7], refs[7:]
    scratch, refs = refs[:5], refs[5:]
    dws, refs = [None, None, refs[:2], refs[2:4], refs[4:6]], refs[6:]
    ls, ss, rs, refs = refs[0], refs[1], refs[2], refs[3:]
    sums = []
    for k, chunks in enumerate((FFN_CHUNKS, ATTN_CHUNKS, ATTN_CHUNKS, FFN_CHUNKS, ATTN_CHUNKS)):
        reds, refs = refs[:2], refs[2:]
        bufs, refs = take_bufs(refs, 2)
        parts = (parts_d, parts_c, *dws[2:])[k]
        sums.append(PlaneSum(parts, reds, outs[k], bufs, *refs[:3], far=k < 2))
        refs = refs[3:]
    d, c, s, f, e = sums
    loads = list(zip(far, (acc2.at[1], acc2.at[0], n1, r1, cot, alow_f, h, n0, r0)))
    loads += [(x_far, x_e), (acc2.at[1], dec_o), (acc2.at[0], enc_o)]
    t = pl.program_id(0)
    kind, _ = last_of(t)

    def load(k):
        return pltpu.make_async_copy(*loads[k], ls.at[k])

    _, core, xn, yn, _ = neighbours(1)

    def swap(k):
        return pltpu.make_async_remote_copy(
            src_ref=small.at[k], dst_ref=got.at[k], send_sem=ss.at[k], recv_sem=rs.at[k],
            device_id=(core, xn, yn)[k], device_id_type=MESH,
        )

    def small_first():
        small[0] = jnp.zeros_like(small[0])
        small[0, 0:1] = gs2[2:3]
        for k, g in enumerate((gs0, gs1, gs2, gs3, gs4)):
            small[0, 1 + k : 2 + k] = g[0:1]
            small[0, 6 + k : 7 + k] = g[1:2]
        swap(0).start()

    def small_next(k):
        def run():
            swap(k).wait_recv()
            small[k + 1] = small[k] + got[k]
            if k < 2:
                swap(k + 1).start()

        return run

    def small_last():
        mask_o[...] = small[3, 0:1]
        gain_o[...] = small[3, 1:6]
        shift_o[...] = small[3, 6:11]
        for k in range(3):
            swap(k).wait_send()

    def end():
        for x in sums:
            x.sent(REDUCE)()
            x.sent(SPREAD)()

    ev = {
        (0, -1): [plane_barrier, d.p1(), c.p1()],
        (0, 1): [d.p2()],
        (0, 2): [c.p2()],
        (0, 4): [s.p1()],
        (1, 0): [d.p3()],
        (1, 2): [c.p3()],
        (1, 4): [f.p1(), s.p2()],
        (2, 1): [d.p4(), d.g1()],
        (2, 3): [f.p2()],
        (3, 0): [c.p4(), c.g1()],
        (3, 2): [d.g2()],
        (4, 0): [s.p3()],
        (4, 2): [f.p3()],
        (5, 0): [c.g2()],
        (5, 1): [d.g3()],
        (5, 2): [s.p4(), s.g1()],
        (5, 4): [e.p1()],
        (6, 0): [f.p4(), f.g1()],
        (6, 1): [c.g3()],
        (6, 2): [e.p2()],
        (7, 0): [s.g2()],
        (7, 1): [d.g4()],
        (7, 2): [f.g2()],
        (8, 0): [e.p3()],
        (8, 1): [c.g4()],
        (8, 2): [s.g3()],
        (8, 4): [small_first],
        (9, 0): [e.p4(), e.g1()],
        (9, 1): [f.g3()],
        (9, 2): [small_next(0)],
        (10, 0): [e.g2()],
        (10, 1): [small_next(1)],
        (10, 2): [s.g4()],
        (11, 0): [e.g3()],
        (11, 1): [small_next(2)],
        (11, 2): [f.g4()],
    }
    attn_steps, ffn_steps = (0, 5, 6, 7, 8, 9, 10, 11), (1, 2, 3, 4)

    @pl.when((t == 0) | (t > 4))
    def _():
        @pl.when(t == 0)
        def _():
            for k in range(10):
                load(k).start()
            load(0).wait()

        run_events(t, attn_steps, ev, -1)

        @pl.when(t == 0)
        def _():
            a = acc2.at[1]
            norm_back_all(lambda rows: a[rows], n2, r2, gains[2:3], gs2, a, g2.at[1])

        @pl.when(t == 5)
        def _():
            for k in (7, 8, 9):
                load(k).wait()
            a = acc2.at[0]
            norm_back_all(lambda rows: a[rows], n0, r0, gains[0:1], gs0, a, g2.at[0])

        attend_slot(False, None, w, pt, v, kt, q, ot, g2.at[kind], acc2.at[kind], None, scratch,
                    lambda b: run_events(t, attn_steps, ev, b))

        @pl.when(t == 0)
        def _():
            attend_weights(*dws[2], ot, g2.at[1], alow_s, alow_s, scratch)

        @pl.when(t == 5)
        def _():
            attend_weights(*dws[4], ot, g2.at[0], x_e, x_e, scratch)

        @pl.when(t == 8)
        def _():
            total = jnp.zeros((1, 512), f32)
            for b in range(4):
                rows = rows_at(b)
                hit = jnp.concatenate([mcol[rows]] * 4, axis=1) == 1
                dx = acc2[1, rows]
                total += jnp.sum(jnp.where(hit, dx, 0.0), axis=0, keepdims=True)
                acc2[1, rows] = jnp.where(hit, 0.0, dx)
            gs2[2:3] = total
            load(10).start()

        run_events(t, attn_steps, ev, 4)

        @pl.when(t == 11)
        def _():
            load(11).start()
            e.g4()()
            small_last()
            end()
            load(10).wait()
            load(11).wait()

    @pl.when((t > 0) & (t < 5))
    def _():
        @pl.when(t == 1)
        def _():
            for k in range(1, 7):
                load(k).wait()
            a = acc2.at[0]
            norm_back_all(lambda rows: a[rows] + cot[rows].astype(f32), n1, r1, gains[1:2], gs1, a,
                          g2.at[0])

        ffn_back_slot(wf, slope, g2.at[0], db_s, acc2.at[0],
                      lambda b: run_events(t, ffn_steps, ev, b))

        @pl.when(t == 1)
        def _():
            ffn_weights(*dws[3], alow_f, db_s, h, g2.at[0])

        run_events(t, ffn_steps, ev, 4)


def call_last(n2, r2, gains, alow_s, mcol, gs3, gs4, saved, wf, slope, far, parts_d, parts_c):
    w, pt, q, v, kt, ot = saved
    groups = (FFN_CHUNKS, ATTN_CHUNKS, ATTN_CHUNKS, FFN_CHUNKS, ATTN_CHUNKS)

    def by_es(*tail):
        return pl.BlockSpec((1,) + tail, lambda t: (last_of(t)[1],) + (0,) * len(tail))

    def chunk(t):
        return jnp.clip(t - 1, 0, 3)

    net = []
    for g in groups:
        net += [VM(s, f32) for s in g] + sum_bufs(g) + sum_sems(2)
    results = [chunked(*s) for g in groups for s in g]
    return pl.pallas_call(
        last_kernel,
        grid=(12,),
        in_specs=[
            held((1024, 512)), held((1024, 1)), held((5, 512)), held((1024, 512)),
            held((1024, 128)), held((8, 512)), held((8, 512)), by_es(512, 512),
            by_es(4, 512, 512), by_es(1024, 128), by_es(128, 1024), by_es(1024, 128),
            by_es(128, 1024), pl.BlockSpec((1, 2, 512, 512), lambda t: (chunk(t), 0, 0, 0)),
            pl.BlockSpec((1024, 512), lambda t: (0, chunk(t))),
        ] + [ANY] * 14,
        out_specs=[kept((1, 512)), kept((5, 512)), kept((5, 512))] + [ANY] * 12,
        out_shape=[SDS((1, 512), f32), SDS((5, 512), f32), SDS((5, 512), f32),
                   SDS((1024, 512), f32), SDS((1024, 512), f32)] + [SDS(s, f32) for s in results],
        scratch_shapes=[
            VM((2, 1024, 512), f32), VM((1024, 512), f32), VM((1024, 1), f32), VM((1024, 512), bf16),
            VM((1024, 512), bf16), VM((1024, 512), bf16), VM((1024, 512), f32), VM((1024, 1), f32),
            VM((1024, 512), bf16), VM((8, 512), f32), VM((8, 512), f32), VM((8, 512), f32),
            VM((2, 1024, 512), bf16), VM((1024, 512), bf16), VM((4, 16, 512), f32),
            VM((3, 16, 512), f32),
        ] + ATTN_SCRATCH + [VM(chunked(*s), f32) for g in groups[2:] for s in g]
        + [pltpu.SemaphoreType.DMA((12,)), pltpu.SemaphoreType.DMA((3,)),
           pltpu.SemaphoreType.DMA((3,))] + net,
        compiler_params=pltpu.CompilerParams(
            collective_id=3, has_side_effects=True, vmem_limit_bytes=VMEM_MB * MB
        ),
    )(n2, r2, gains, alow_s, mcol, gs3, gs4, w, pt, v, kt, q, ot, wf, slope, *far, *parts_d,
      *parts_c)


def deliver_kernel(count, *refs):
    srcs, dsts, bufs = refs[:count], refs[count : 2 * count], refs[2 * count : 3 * count]
    ins, outs = refs[3 * count :]

    def load(k):
        return pltpu.make_async_copy(srcs[k], bufs[k], ins.at[k])

    def store(k):
        if len(dsts[k].shape) < 6:
            return [pltpu.make_async_copy(bufs[k], dsts[k], outs.at[k, 0])]
        return [
            pltpu.make_async_copy(bufs[k].at[:, :, :, pl.ds(m * 64, 64)], dsts[k].at[m], outs.at[k, m])
            for m in range(3)
        ]

    for k in range(count):
        load(k).start()
    for k in range(count):
        load(k).wait()
        for c in store(k):
            c.start()
    for k in range(count):
        for c in store(k):
            c.wait()


def deliver(arrays):
    shapes = [(3, 2, 2, 2, 64, 128) if a.shape[-1] == 128 else a.shape for a in arrays]
    count = len(arrays)
    return pl.pallas_call(
        functools.partial(deliver_kernel, count),
        in_specs=[ANY] * count,
        out_specs=[ANY] * count,
        out_shape=[SDS(s, a.dtype) for s, a in zip(shapes, arrays)],
        scratch_shapes=[VM(a.shape, a.dtype) for a in arrays]
        + [pltpu.SemaphoreType.DMA((count,)), pltpu.SemaphoreType.DMA((count, 3))],
        compiler_params=pltpu.CompilerParams(vmem_limit_bytes=VMEM_MB * MB),
    )(*arrays)


def per_device(planes, tensor, enc_in, dec_in, src_idx, tgt_idx, masked, mask_embed, enc_qkv,
               enc_out_w, enc_w1, enc_w2, self_qkv, self_out_w, cross_qkv, cross_out_w, dec_w1,
               dec_w2, gains, shifts, enc_cot, dec_cot):
    (target_low, target, koh, mq, mcol, own_es, own_c, own_f, own_d, blob_e, blob_s, blob_c, blob_f,
     blob_d, win) = call_prep(
        dec_in[0], masked, mask_embed[None], src_idx, tgt_idx, enc_qkv, enc_out_w,
        self_qkv, self_out_w, cross_qkv, cross_out_w, enc_w1, enc_w2, dec_w1, dec_w2)
    (w_es, pt_es, q_es, v_es, kt_es, ot_es, w_f, slope_e, h_e, r0, r2, r1, n0, n2, n1, first_low,
     second_low, enc_low, land_c) = call_first(
        tensor, enc_in[0], target_low, target, koh, mq, own_es, own_f, gains, shifts,
        (blob_e, blob_s, blob_f, blob_c))
    (w_c, pt_c, q_c, v_c, kt_c, ot_c, w_d, slope_d, h_d, r3, r4, n3, n4, third_low,
     dec_low) = call_second(
        tensor, n2, second_low, enc_low, koh, mq, own_c, own_d, gains, shifts, land_c, blob_d)
    save_es = (w_es, pt_es, q_es, v_es, kt_es, ot_es)
    save_c = (w_c, pt_c, q_c, v_c, kt_c, ot_c)

    d_third, gs4, *parts_d = call_dec_ffn_bwd(
        dec_cot[0], n4, r4, gains, third_low, w_d, h_d, slope_d)
    d_second, d_key, *parts_c, gs3, enc_out, dec_out = call_cross_bwd(
        win, d_third, n3, r3, gains, save_c, second_low, enc_low, dec_low)
    far = (d_second, d_key, n1, r1, enc_cot[0], first_low, h_e, n0, r0, enc_in[0])
    (mask_grad, gain_grad, shift_grad, dec_grad, d_enc, dw1_d, dw2_d, dqkv_c, dwo_c, dqkv_s, dwo_s,
     dw1_e, dw2_e, dqkv_e, dwo_e) = call_last(
        n2, r2, gains, target_low, mcol, gs3, gs4, save_es, w_f, slope_e, far, parts_d, parts_c)

    sums = (mask_grad, gain_grad, shift_grad, dqkv_e, dwo_e, dw1_e, dw2_e, dqkv_s, dwo_s, dqkv_c,
            dwo_c, dw1_d, dw2_d)
    if planes > 1:
        same = [[p * 8 + k for p in range(planes)] for k in range(8)]
        sums = lax.psum(sums, "dp", axis_index_groups=same)
    d_enc, dec_grad, mask_grad, gain_grad, shift_grad, *mats = deliver([d_enc, dec_grad, *sums])
    mats = [m.reshape(3, 512, 128) if m.ndim == 6 else m.reshape(-1, 512) for m in mats]
    return (enc_out[None], dec_out[None], d_enc[None], dec_grad[None], mask_grad[0], *mats,
            gain_grad, shift_grad)


def solution(mesh):
    tokens, index = P("dp", None, None), P("dp", None)
    qkv, cols, rows = P(None, None, "tensor"), P(None, "tensor"), P("tensor", None)
    weights = (qkv, rows, cols, rows, qkv, rows, qkv, rows, cols, rows)
    return jax.shard_map(
        functools.partial(per_device, mesh.shape["dp"] // 8, mesh.shape["tensor"]),
        mesh=mesh,
        in_specs=(tokens, tokens, index, index, index, P()) + weights + (P(), P(), tokens, tokens),
        out_specs=(tokens,) * 4 + (P(),) + weights + (P(), P()),
        check_vma=False,
    )
```
